32 devices in a mesh: tok: 8 (over z, x), ad: 4 (over y, core).
Axes of the slice: x: 2, y: 2, z: 4, core: 2. Of those that a mesh axis runs over, the one named last changes fastest.
Arguments:
- tokens: bfloat16 [8192, 768], P('tok'), may hold values from -6 to 6
- cotangent: bfloat16 [8192, 768], P('tok'), may hold values from -6 to 6
- attn_qkv: bfloat16 [3, 768, 768], P(None, None, 'ad'), may hold values from -0.21875 to 0.21875
- attn_out: bfloat16 [768, 768], P('ad'), may hold values from -4 to 4
- ffn_in: bfloat16 [768, 3072], P(None, 'ad'), may hold values from -0.21875 to 0.21875
- ffn_bias_in: float32 [3072], P('ad'), may hold values from -1.5 to 1.5
- ffn_out: bfloat16 [3072, 768], P('ad'), may hold values from -0.109375 to 0.109375
- ffn_bias_out: float32 [768], replicated, may hold values from -1.5 to 1.5
- norm_gains: float32 [3, 768], replicated, may hold values from 0.5 to 1.5
- norm_shifts: float32 [3, 768], replicated, may hold values from -1.5 to 1.5
- adapter_down: bfloat16 [768, 768], P(None, 'ad'), may hold values from -0.21875 to 0.21875
- adapter_up: bfloat16 [16, 48, 768], P('ad'), may hold values from -0.875 to 0.875
- merging_proj: bfloat16 [3, 768, 768], replicated, may hold values from -0.21875 to 0.21875
- adapter_mask: int32 [8, 16], P('tok', 'ad'), may hold values from 0 to 1, as said below
- lengths: int32 [8], P('tok'), may hold values from 256 to 1024, as said below
Outputs:
- output: bfloat16 [8192, 768], P('tok')
- grad_tokens: float32 [8192, 768], P('tok')
- grad_attn_qkv: float32 [3, 768, 768], P(None, None, 'ad')
- grad_attn_out: float32 [768, 768], P('ad')
- grad_ffn_in: float32 [768, 3072], P(None, 'ad')
- grad_ffn_bias_in: float32 [3072], P('ad')
- grad_ffn_out: float32 [3072, 768], P('ad')
- grad_ffn_bias_out: float32 [768], replicated
- grad_norm_gains: float32 [3, 768], replicated
- grad_norm_shifts: float32 [3, 768], replicated
- grad_merging: float32 [3, 768, 768], replicated
- usage: float32 [16], P('ad')
The draws below stay inside these ranges and needn't reach their ends.
Inputs may be any that keep to these rules, and one draw needn't show every extreme that they name: `adapter_mask`: every sequence has at least one available adapter. `lengths`: one sequence, drawn from the seed, has exactly 1024 tokens; positions at or past a sequence's length are padding.
All inputs are finite; a program needn't handle non-finite values.
Results may differ from the reference program's by a relative error of at most 0.03.
Values may be sent and summed in bfloat16 or wider, within the bound.
No kernel may reach another device: no remote copies, remote signals or barrier semaphores. Data moves between devices by JAX's collectives and lax.ppermute only.
A program may use at most 192 MiB of HBM per device.

```python
import jax
import jax.numpy as jnp
from jax import lax

D = 768
HEADS = 12
HEAD = 64
FF = 3072
RANK = 48
ADAPTERS = 16
LEN = 1024
SEQS = 8
TOKENS = 8192


def draw_adapter_mask(key, part):
    key = jax.random.fold_in(key, 11)
    rate_key, coin_key, pick_key = jax.random.split(key, 3)
    rates = jax.random.randint(rate_key, (ADAPTERS,), 2, 10)
    coins = jax.random.randint(coin_key, (SEQS, ADAPTERS), 0, 10)
    chosen = jax.random.randint(pick_key, (SEQS, 1), 0, ADAPTERS)
    forced = jnp.arange(ADAPTERS)[None, :] == chosen
    return jnp.where((coins < rates[None, :]) | forced, 1, 0).astype(jnp.int32)


def draw_lengths(key, part):
    key = jax.random.fold_in(key, 23)
    draw_key, full_key = jax.random.split(key)
    drawn = jax.random.randint(draw_key, (SEQS,), LEN // 4, LEN + 1)
    full_one = jax.random.randint(full_key, (), 0, SEQS)
    return jnp.where(jnp.arange(SEQS) == full_one, LEN, drawn).astype(jnp.int32)


def steps_of(key, dims, cuts, least, largest):
    def one(position, parts):
        heights = jax.random.uniform(jax.random.fold_in(jax.random.fold_in(key, 6), position), (parts,), jnp.float32, least / len(cuts), largest / len(cuts))
        return jnp.repeat(jnp.exp(heights), dims[position] // parts).reshape((-1,) + (1,) * (len(dims) - position - 1))

    level = one(*cuts[0])
    for cut in cuts[1:]:
        level = level * one(*cut)
    return level


def gaussian(stream_key, shape, width, bound, shards=(), kind=jnp.bfloat16):
    values = jax.random.normal(stream_key, shape, jnp.float32) * width
    if len(shards) > 0:
        values = steps_of(stream_key, shape, shards, -0.22, 0.18) * values
    return jnp.clip(values, min=-bound, max=bound).astype(kind)


def setup_inputs(seed: int = 0) -> dict:
    streams_of = jax.random.split(jax.random.key(seed), 16)
    return {
        "tokens": gaussian(streams_of[0], (TOKENS, D), 1.0, 6.0, ((0, 8),)),
        "cotangent": gaussian(streams_of[1], (TOKENS, D), 1.0, 6.0, ((0, 8),)),
        "attn_qkv": gaussian(streams_of[2], (3, D, D), D ** -0.5, 0.21875, ((2, 4),)),
        "attn_out": gaussian(streams_of[3], (D, D), (max(1, 3 * D // LEN)) ** -0.5, 4.0, ((0, 4),)),
        "ffn_in": gaussian(streams_of[4], (D, FF), D ** -0.5, 0.21875, ((1, 4),)),
        "ffn_bias_in": gaussian(streams_of[5], (FF,), 0.3, 1.5, ((0, 4),), jnp.float32),
        "ffn_out": gaussian(streams_of[6], (FF, D), FF ** -0.5, 0.109375, ((0, 4),)),
        "ffn_bias_out": gaussian(streams_of[7], (D,), 0.3, 1.5, (), jnp.float32),
        "norm_gains": jnp.clip(1.0 + 0.1 * jax.random.normal(streams_of[8], (3, D), jnp.float32), 0.5, 1.5),
        "norm_shifts": gaussian(streams_of[9], (3, D), 0.3, 1.5, (), jnp.float32),
        "adapter_down": gaussian(streams_of[10], (D, ADAPTERS * RANK), D ** -0.5, 0.21875, ((1, 4),)),
        "adapter_up": gaussian(streams_of[11], (ADAPTERS, RANK, D), RANK ** -0.5, 0.875, ((0, 4),)),
        "merging_proj": gaussian(streams_of[12], (3, D, D), D ** -0.5, 0.21875),
        "adapter_mask": draw_adapter_mask(jax.random.fold_in(streams_of[15], 71), 0),
        "lengths": draw_lengths(jax.random.fold_in(streams_of[15], 71), 0),
    }


@jax.custom_vjp
def low(v):
    return lax.optimization_barrier(v.astype(jnp.bfloat16)).astype(jnp.float32)

@jax.custom_vjp
def low_back(v):
    return v

def low_keep(v):
    return (low(v), None)

def low_pass(kept, grad):
    return (grad,)

def back_keep(v):
    return (v, None)

def back_low(kept, grad):
    return (low(grad),)
low.defvjp(low_keep, low_pass)
low_back.defvjp(back_keep, back_low)
HIGHEST = lax.Precision.HIGHEST
EPSILON = 1e-06
NEGATIVE = -1e+30

def matmul(left, right):
    return jnp.dot(left, right, precision=HIGHEST, preferred_element_type=jnp.float32)

def normalize(values, gain, shift):
    centred = values - lax.optimization_barrier(jnp.mean(values, -1, keepdims=True))
    inverse = lax.rsqrt(lax.optimization_barrier(jnp.mean(centred * centred, -1, keepdims=True)) + EPSILON)
    return centred * inverse * gain + shift

def gelu_exact(values):
    return jax.nn.gelu(values, approximate=False)

def self_attention(queries, key_rows, value_rows, length):
    positions = queries.shape[0]
    queries = queries.reshape(positions, HEADS, HEAD)
    key_rows = key_rows.reshape(positions, HEADS, HEAD)
    value_rows = value_rows.reshape(positions, HEADS, HEAD)
    logits = jnp.einsum('qhd,khd->hqk', queries, key_rows, precision=HIGHEST) * HEAD ** (-0.5)
    logits = low_back(logits)
    keep = jnp.arange(positions) < length
    logits = jnp.where(keep[None, None, :], logits, NEGATIVE)
    highest = lax.optimization_barrier(jnp.max(logits, -1, keepdims=True))
    expon = jnp.exp(logits - highest)
    weights = low(expon / lax.optimization_barrier(jnp.sum(expon, -1, keepdims=True)))
    context = jnp.einsum('hqk,khd->qhd', weights, value_rows, precision=HIGHEST)
    return low_back(low(context.reshape(positions, D)))

def sequence(params, inputs, length, mask):
    attn_qkv, attn_out, ffn_in, ffn_bias_in, ffn_out, ffn_bias_out, norm_gains, norm_shifts, adapter_down, adapter_up, merging_proj = params
    queries = low_back(low(matmul(inputs, attn_qkv[0])))
    key_rows = low_back(low(matmul(inputs, attn_qkv[1])))
    value_rows = low_back(low(matmul(inputs, attn_qkv[2])))
    context = self_attention(queries, key_rows, value_rows, length)
    attended = low_back(matmul(context, attn_out))
    first = normalize(inputs + attended, norm_gains[0], norm_shifts[0])
    inner_pre = low_back(matmul(low(first), ffn_in) + ffn_bias_in)
    inner = low(gelu_exact(inner_pre))
    fed = low_back(matmul(inner, ffn_out)) + ffn_bias_out
    second = normalize(first + fed, norm_gains[1], norm_shifts[1])
    second_low = low(second)
    bottle_pre = low_back(matmul(second_low, adapter_down))
    squeezed = low(gelu_exact(bottle_pre)).reshape(-1, ADAPTERS, RANK)
    adapted = second[:, None, :] + jnp.einsum('tar,ard->tad', squeezed, adapter_up, precision=HIGHEST)
    adapted = low_back(low(adapted))
    fquery = low_back(low(matmul(second_low, merging_proj[0])))
    fkeys = low_back(low(jnp.einsum('tad,de->tae', adapted, merging_proj[1], precision=HIGHEST)))
    fvalues = low_back(jnp.einsum('tad,de->tae', adapted, merging_proj[2], precision=HIGHEST))
    scores = jnp.einsum('td,tad->ta', fquery, fkeys, precision=HIGHEST) * D ** (-0.5)
    usable = (mask > 0)[None, :]
    scores = jnp.where(usable, scores, NEGATIVE)
    highest = lax.optimization_barrier(jnp.max(scores, -1, keepdims=True))
    weights = jnp.where(usable, jnp.exp(scores - highest), 0.0)
    probs = weights / lax.optimization_barrier(jnp.sum(weights, -1, keepdims=True))
    blended = jnp.einsum('ta,tad->td', probs, fvalues, precision=HIGHEST)
    final = normalize(second + blended, norm_gains[2], norm_shifts[2])
    valid = (jnp.arange(inputs.shape[0]) < length).astype(jnp.float32)
    mass = lax.optimization_barrier(jnp.sum(probs * valid[:, None], 0))
    return (final, mass)

def reference(tokens, cotangent, attn_qkv, attn_out, ffn_in, ffn_bias_in, ffn_out, ffn_bias_out, norm_gains, norm_shifts, adapter_down, adapter_up, merging_proj, adapter_mask, lengths):
    params = tuple((weight.astype(jnp.float32) for weight in (attn_qkv, attn_out, ffn_in, ffn_bias_in, ffn_out, ffn_bias_out, norm_gains, norm_shifts, adapter_down, adapter_up, merging_proj)))
    inputs = tokens.astype(jnp.float32).reshape(SEQS, LEN, D)
    checked = jax.checkpoint(sequence)

    def forward(inputs, params):

        def each(carried, pieces):
            final, mass = checked(params, pieces[0], pieces[1], pieces[2])
            return (carried + mass, final)
        mass, finals = lax.scan(each, jnp.zeros((ADAPTERS,), jnp.float32), (inputs, lengths, adapter_mask))
        return (finals, mass)
    finals, pullback, mass = jax.vjp(forward, inputs, params, has_aux=True)
    grad_inputs, grads = pullback(cotangent.astype(jnp.float32).reshape(SEQS, LEN, D))
    usage = mass / jnp.sum(lengths.astype(jnp.float32))
    return (finals.reshape(TOKENS, D).astype(jnp.bfloat16), grad_inputs.reshape(TOKENS, D), grads[0], grads[1], grads[2], grads[3], grads[4], grads[5], grads[6], grads[7], grads[10], usage)
```

```python
import jax
import jax.numpy as jnp
from jax import lax
from jax.sharding import PartitionSpec as P

HEAD = 64
EPSILON = 1e-06
NEGATIVE = -1e30
BLOCK_LIMIT = 512
F32 = jnp.float32
BF16 = jnp.bfloat16


def normalize(values, gain, shift):
    centred = values - jnp.mean(values, -1, keepdims=True)
    inverse = lax.rsqrt(jnp.mean(centred * centred, -1, keepdims=True) + EPSILON)
    unit_rows = centred * inverse
    return (unit_rows * gain + shift, unit_rows, inverse)


def normalize_back(gradient, unit_rows, inverse, gain):
    scaled = gradient * gain
    centred = (
        scaled
        - jnp.mean(scaled, -1, keepdims=True)
        - unit_rows * jnp.mean(scaled * unit_rows, -1, keepdims=True)
    )
    return (centred * inverse, jnp.sum(gradient * unit_rows, 0), jnp.sum(gradient, 0))


def gelu_both(values):
    cdf = 0.5 * (1.0 + lax.erf(values * 0.7071067811865476))
    density = jnp.exp(-0.5 * values * values) * 0.3989422804014327
    return values * cdf, cdf + values * density


def dot(left, right, dims=((1,), (0,))):
    return lax.dot_general(left, right, (dims, ((), ())), preferred_element_type=F32)


def dot_nt(left, right):
    return dot(left, right, ((1,), (1,)))


def dot_tn(left, right):
    return dot(left, right, ((0,), (0,)))


def split_dot(left, right):
    high = left.astype(BF16)
    rest = (left - high.astype(F32)).astype(BF16)
    return dot(high, right) + dot(rest, right)


def swap(array, axis, size, step):
    return lax.ppermute(array, axis, [(i, i ^ step) for i in range(size)])


def gather_xor(block):
    across = swap(block, "ad", 4, 2)
    beside = swap(block, "ad", 4, 1)
    return [block, beside, across, swap(across, "ad", 4, 1)]


def scatter_xor(parts):
    dtype = parts[0].dtype
    beside = swap(jnp.stack([parts[1], parts[3]]), "ad", 4, 1)
    own = parts[0].astype(F32) + beside[0].astype(F32)
    across = (parts[2].astype(F32) + beside[1].astype(F32)).astype(dtype)
    return own + swap(across, "ad", 4, 2).astype(F32)


def exchange_xor(parts):
    across = swap(jnp.stack([parts[2], parts[3]]), "ad", 4, 2)
    beside = swap(jnp.stack([parts[1], across[1]]), "ad", 4, 1)
    return [parts[0], beside[0], across[0], beside[1]]


def to_xor(blocks, me):
    return [lax.dynamic_index_in_dim(blocks, me ^ k, 0, keepdims=False) for k in range(4)]


def attend(packed, keep):
    positions = packed.shape[1]
    heads = packed.shape[2] // HEAD
    block_rows = min(BLOCK_LIMIT, positions)
    key_rows = packed[1].reshape(positions, heads, HEAD)
    value_rows = packed[2].reshape(positions, heads, HEAD)
    queries = packed[0].reshape(positions // block_rows, block_rows, heads, HEAD)
    scaling = HEAD ** (-0.5)

    def one_block(query_rows):
        logits = (
            jnp.einsum("qhd,khd->hqk", query_rows, key_rows, preferred_element_type=F32) * scaling
        )
        logits = jnp.where(keep[None, None, :], logits, NEGATIVE)
        highest = jnp.max(logits, -1, keepdims=True)
        expon = jnp.exp(logits - highest)
        totals = jnp.sum(expon, -1, keepdims=True)
        weights = (expon / totals).astype(BF16)
        context = jnp.einsum("hqk,khd->qhd", weights, value_rows, preferred_element_type=F32)
        return (
            context.astype(BF16).reshape(block_rows, -1),
            (highest + jnp.log(totals))[:, :, 0],
        )

    context, log_totals = lax.map(one_block, queries)
    return (context.reshape(positions, -1), log_totals)


def attend_back(packed, log_totals, grad_context, keep):
    positions = packed.shape[1]
    heads = packed.shape[2] // HEAD
    block_rows = min(BLOCK_LIMIT, positions)
    key_rows = packed[1].reshape(positions, heads, HEAD)
    value_rows = packed[2].reshape(positions, heads, HEAD)
    queries = packed[0].reshape(positions // block_rows, block_rows, heads, HEAD)
    scaling = HEAD ** (-0.5)
    gradients = grad_context.reshape(queries.shape)

    def one_block(carried, pieces):
        query_rows, log_block, grad_block = pieces
        logits = (
            jnp.einsum("qhd,khd->hqk", query_rows, key_rows, preferred_element_type=F32) * scaling
        )
        logits = jnp.where(keep[None, None, :], logits, NEGATIVE)
        probs = jnp.exp(logits - log_block[:, :, None])
        grad_probs = jnp.einsum("qhd,khd->hqk", grad_block, value_rows, preferred_element_type=F32)
        inner_sum = jnp.sum(probs * grad_probs, -1, keepdims=True)
        grad_logits = (probs * (grad_probs - inner_sum)).astype(BF16)
        grad_query = (
            jnp.einsum("hqk,khd->qhd", grad_logits, key_rows, preferred_element_type=F32) * scaling
        )
        grad_keys = (
            carried[0]
            + jnp.einsum("hqk,qhd->khd", grad_logits, query_rows, preferred_element_type=F32)
            * scaling
        )
        grad_values = carried[1] + jnp.einsum(
            "hqk,qhd->khd", probs.astype(BF16), grad_block, preferred_element_type=F32
        )
        return ((grad_keys, grad_values), grad_query)

    zero_rows = jnp.zeros(key_rows.shape, F32)
    (grad_keys, grad_values), grad_query = lax.scan(
        one_block, (zero_rows, zero_rows), (queries, log_totals, gradients)
    )
    return jnp.stack(
        [
            grad_query.reshape(positions, -1),
            grad_keys.reshape(positions, -1),
            grad_values.reshape(positions, -1),
        ]
    ).astype(BF16)


def merge(second, second_low, down, up, merging, usable, valid, expand, gains, shifts, cot):
    width = second.shape[1]
    scaling = width ** (-0.5)
    collect = expand.T
    bottle = dot(second_low, down)
    squeezed, slope = gelu_both(bottle)
    squeezed = squeezed.astype(BF16).astype(F32)
    fquery = dot(second_low, merging[0]).astype(BF16)
    asked = dot_nt(fquery, merging[1])
    asked_up = dot_nt(asked.astype(BF16), up)
    scores = scaling * (
        jnp.sum(asked * second, -1, keepdims=True) + split_dot(squeezed * asked_up, collect)
    )
    scores = jnp.where(usable, scores, NEGATIVE)
    highest = jnp.max(scores, -1, keepdims=True)
    weights = jnp.where(usable, jnp.exp(scores - highest), 0.0)
    probs = weights / jnp.sum(weights, -1, keepdims=True)
    total = jnp.sum(probs, -1, keepdims=True)
    probs_wide = split_dot(probs, expand)
    mixed = total * second + dot((probs_wide * squeezed).astype(BF16), up)
    mixed_low = mixed.astype(BF16)
    blended = dot(mixed_low, merging[2])
    final, unit, inverse = normalize(second + blended, gains[2], shifts[2])
    mass = jnp.sum(probs * valid, 0)
    dthird, gain_third, shift_third = normalize_back(cot, unit, inverse, gains[2])
    dthird_low = dthird.astype(BF16)
    pulled = dot_nt(dthird_low, merging[2])
    pulled_up = dot_nt(pulled.astype(BF16), up)
    dprobs = jnp.sum(pulled * second, -1, keepdims=True) + split_dot(squeezed * pulled_up, collect)
    dscores = probs * (dprobs - jnp.sum(probs * dprobs, -1, keepdims=True)) * scaling
    dscores_total = jnp.sum(dscores, -1, keepdims=True)
    dscores_wide = split_dot(dscores, expand)
    weighed = dscores_total * second + dot((dscores_wide * squeezed).astype(BF16), up)
    weighed_low = weighed.astype(BF16)
    dquery = dot(weighed_low, merging[1]).astype(BF16)
    dbottle = ((dscores_wide * asked_up + probs_wide * pulled_up) * slope).astype(BF16)
    dsecond = (
        dthird
        + dscores_total * asked
        + total * pulled
        + dot_nt(dbottle, down)
        + dot_nt(dquery, merging[0])
    )
    grads = jnp.stack(
        [
            dot_tn(second_low, dquery),
            dot_tn(weighed_low, fquery),
            dot_tn(mixed_low, dthird_low),
        ]
    )
    return final.astype(BF16), dsecond, grads, gain_third, shift_third, mass


def on_device(
    tokens,
    cotangent,
    attn_qkv,
    attn_out,
    ffn_in,
    ffn_bias_in,
    ffn_out,
    ffn_bias_out,
    norm_gains,
    norm_shifts,
    adapter_down,
    adapter_up,
    merging_proj,
    adapter_mask,
    lengths,
):
    me = lax.axis_index("ad")
    row_count, width = tokens.shape
    block = row_count // 4
    out_blocks = gather_xor(attn_out)
    down_blocks = gather_xor(adapter_down)
    up_blocks = gather_xor(adapter_up.reshape(-1, width))
    mask_blocks = gather_xor(adapter_mask.astype(F32))
    out_whole = jnp.concatenate(out_blocks, 0)
    down = jnp.concatenate(down_blocks, 1)
    up = jnp.concatenate(up_blocks, 0)
    mask_row = jnp.concatenate(mask_blocks, 1)
    adapters = mask_row.shape[1]
    rank = up.shape[0] // adapters
    expand = (
        jnp.arange(adapters)[:, None] == jnp.arange(adapters * rank)[None, :] // rank
    ).astype(BF16)

    tokens = jnp.concatenate(to_xor(tokens.reshape(4, block, width), me), 0)
    positions = jnp.concatenate([(me ^ k) * block + jnp.arange(block) for k in range(4)])
    keep = positions < lengths[0]
    packed = jnp.einsum("td,jde->jte", tokens, attn_qkv, preferred_element_type=F32).astype(BF16)
    context, log_totals = attend(packed, keep)
    columns = [context.reshape(4, block, -1)]
    for k, other in enumerate(gather_xor(context)[1:], 1):
        other = other.reshape(4, block, -1)
        columns.append(jnp.stack([other[j ^ k] for j in range(4)]))
    context_whole = jnp.concatenate(columns, 2).reshape(row_count, -1)
    attended = dot(context_whole, out_whole)
    first, unit_first, inverse_first = normalize(
        tokens.astype(F32) + attended, norm_gains[0], norm_shifts[0]
    )
    first_low = first.astype(BF16)
    inner_pre = dot(first_low, ffn_in) + ffn_bias_in
    inner, inner_slope = gelu_both(inner_pre)
    inner = inner.astype(BF16)
    inner_slope = inner_slope.astype(BF16)
    fed = dot(inner, ffn_out).astype(BF16).reshape(4, block, width)
    fed_rows = scatter_xor([fed[k] for k in range(4)]) + ffn_bias_out
    second, unit_second, inverse_second = normalize(
        first[:block] + fed_rows, norm_gains[1], norm_shifts[1]
    )
    second_low = second.astype(BF16)
    cot = lax.dynamic_slice_in_dim(cotangent, me * block, block).astype(F32)
    valid = keep[:block, None].astype(F32)
    output_block, dsecond, merging_grads, gain_third, shift_third, mass = merge(
        second,
        second_low,
        down,
        up,
        merging_proj,
        mask_row > 0.5,
        valid,
        expand,
        norm_gains,
        norm_shifts,
        cot,
    )
    output = lax.all_gather(output_block, "ad", axis=0, tiled=True)
    group_merging = lax.psum_scatter(
        merging_grads.astype(BF16).reshape(-1, width), "ad", scatter_dimension=0, tiled=True
    )
    group_merging = lax.psum(group_merging, "tok")
    dmid, gain_second, shift_second = normalize_back(
        dsecond, unit_second, inverse_second, norm_gains[1]
    )
    grad_bias_out = jnp.sum(dmid, 0)
    dmid_low = jnp.concatenate(gather_xor(dmid.astype(BF16)), 0)
    grad_ffn_out = dot_tn(inner, dmid_low)
    dinner = (dot_nt(dmid_low, ffn_out) * inner_slope.astype(F32)).astype(BF16)
    grad_bias_in = jnp.sum(dinner.astype(F32), 0)
    grad_ffn_in = dot_tn(first_low, dinner)
    dfirst = dot_nt(dinner, ffn_in).astype(BF16).reshape(4, block, width)
    dfirst = scatter_xor([dfirst[k] for k in range(4)]) + dmid
    dlow, gain_first, shift_first = normalize_back(
        dfirst, unit_first[:block], inverse_first[:block], norm_gains[0]
    )
    dlow_low = dlow.astype(BF16)
    own_context = context_whole[:block]
    grad_attn_out = dot_tn(own_context, dlow_low).astype(BF16).reshape(4, -1, width)
    grad_attn_out = scatter_xor([grad_attn_out[k] for k in range(4)]).astype(BF16)
    dcontext = dot_nt(dlow_low, out_whole).astype(BF16)
    lanes = dcontext.shape[1] // 4
    dcontext = jnp.concatenate(
        exchange_xor([dcontext[:, k * lanes : (k + 1) * lanes] for k in range(4)]), 0
    )
    dpacked = attend_back(packed, log_totals, dcontext, keep)
    grad_packed = jnp.einsum("td,jte->jde", tokens, dpacked, preferred_element_type=F32)
    dtokens = (
        jnp.einsum("jte,jde->td", dpacked, attn_qkv, preferred_element_type=F32)
        .astype(BF16)
        .reshape(4, block, width)
    )
    dtokens = scatter_xor([dtokens[k] for k in range(4)]) + dlow
    grad_tokens = lax.all_gather(dtokens.astype(BF16), "ad", axis=0, tiled=True).astype(F32)

    grad_merging = lax.all_gather(group_merging, "ad", axis=0, tiled=True)
    grad_merging = grad_merging.reshape(3, width, width).astype(F32)
    low = [
        lax.psum(a.astype(BF16), "tok").astype(F32)
        for a in (grad_packed, grad_attn_out, grad_ffn_in, grad_ffn_out)
    ]
    small = jnp.stack(
        [
            gain_first,
            gain_second,
            gain_third,
            shift_first,
            shift_second,
            shift_third,
            grad_bias_out,
        ]
    )
    counted = jnp.sum(lengths.astype(F32))
    held = adapters // 4
    mass = jnp.concatenate(to_xor(mass.reshape(4, held), me))
    small, mass = lax.psum((small, mass), ("tok", "ad"))
    grad_bias_in, counted = lax.psum((grad_bias_in, counted), "tok")
    usage = lax.dynamic_slice_in_dim(mass, me * held, held) / counted
    return (
        output,
        grad_tokens,
        low[0],
        low[1],
        low[2],
        grad_bias_in,
        low[3],
        small[6],
        small[0:3],
        small[3:6],
        grad_merging,
        usage,
    )


def solution(mesh):
    placed = (
        P("tok", None),
        P("tok", None),
        P(None, None, "ad"),
        P("ad", None),
        P(None, "ad"),
        P("ad"),
        P("ad", None),
        P(),
        P(),
        P(),
        P(None, "ad"),
        P("ad", None, None),
        P(),
        P("tok", "ad"),
        P("tok"),
    )
    return jax.shard_map(
        on_device,
        mesh=mesh,
        in_specs=placed,
        out_specs=(
            P("tok", None),
            P("tok", None),
            P(None, None, "ad"),
            P("ad", None),
            P(None, "ad"),
            P("ad"),
            P("ad", None),
            P(),
            P(),
            P(),
            P(),
            P("ad"),
        ),
        check_vma=False,
    )
```

```python
import jax
import jax.numpy as jnp
from jax import lax
from jax.experimental import pallas as pl
from jax.experimental.pallas import tpu as pltpu
from jax.sharding import PartitionSpec as P

HEAD = 64
EPSILON = 1e-06
NEGATIVE = -1e30
ADAPTERS = 16
MASK_ROWS = 16
F32 = jnp.float32
BF16 = jnp.bfloat16


def normalize(values, gain, shift):
    centred = values - jnp.mean(values, -1, keepdims=True)
    inverse = lax.rsqrt(jnp.mean(centred * centred, -1, keepdims=True) + EPSILON)
    unit_rows = centred * inverse
    return (unit_rows * gain + shift, unit_rows, inverse)


def normalize_back(gradient, unit_rows, inverse, gain):
    scaled = gradient * gain
    centred = (
        scaled
        - jnp.mean(scaled, -1, keepdims=True)
        - unit_rows * jnp.mean(scaled * unit_rows, -1, keepdims=True)
    )
    return (centred * inverse, jnp.sum(gradient * unit_rows, 0), jnp.sum(gradient, 0))


def gelu_both(values):
    cdf = 0.5 * (1.0 + lax.erf(values * 0.7071067811865476))
    density = jnp.exp(-0.5 * values * values) * 0.3989422804014327
    return values * cdf, cdf + values * density


def dot(left, right, dims=((1,), (0,))):
    return lax.dot_general(left, right, (dims, ((), ())), preferred_element_type=F32)


def dot_nt(left, right):
    return dot(left, right, ((1,), (1,)))


def dot_tn(left, right):
    return dot(left, right, ((0,), (0,)))


def split_dot(left, right):
    high = left.astype(BF16)
    rest = (left - high.astype(F32)).astype(BF16)
    return dot(high, right) + dot(rest, right)


def after(array, *others):
    return lax.optimization_barrier((array, *others))[0]


def swap(array, axis, size, step):
    return lax.ppermute(array, axis, [(i, i ^ step) for i in range(size)])


def beside(array):
    return swap(array, "ad", 4, 1)


def across(array):
    return swap(array, "ad", 4, 2)


def gather_xor(block):
    far = across(block)
    return [block, beside(block), far, beside(far)]


def tok_plan(size):
    return [("tok", size, bit) for bit in range(size.bit_length() - 1)]


def side_of(step):
    axis, _, bit = step
    return (lax.axis_index(axis) >> bit) & 1


def halve_start(array, step):
    axis, size, bit = step
    side = side_of(step)
    rows = array.shape[0] // 2
    sent = lax.dynamic_slice_in_dim(array, (1 - side) * rows, rows)
    kept = lax.dynamic_slice_in_dim(array, side * rows, rows)
    return kept, swap(sent, axis, size, 1 << bit)


def add_low(kept, received):
    return (kept.astype(F32) + received.astype(F32)).astype(BF16)


def halve(array, plan):
    for step in plan:
        array = add_low(*halve_start(array, step))
    return array


def double(array, plan):
    for step in reversed(plan):
        axis, size, bit = step
        side = side_of(step) == 1
        other = swap(array, axis, size, 1 << bit)
        array = jnp.concatenate(
            [jnp.where(side, other, array), jnp.where(side, array, other)], 0
        )
    return array


class Chain:
    def __init__(self, array, halving, doubling):
        self.array = array
        self.steps = [(True, step) for step in halving] + [(False, step) for step in doubling]

    def start(self):
        halves, step = self.steps[0]
        if halves:
            return halve_start(self.array, step)
        axis, size, bit = step
        return self.array, swap(self.array, axis, size, 1 << bit)

    def finish(self, own, received):
        halves, step = self.steps.pop(0)
        if halves:
            self.array = add_low(own, received)
        else:
            side = side_of(step) == 1
            self.array = jnp.concatenate(
                [jnp.where(side, received, own), jnp.where(side, own, received)], 0
            )


def advance(chains, *others):
    chains = [chain for chain in chains if chain.steps]
    flights = [chain.start() for chain in chains]
    flights, others = lax.optimization_barrier((flights, others))
    for chain, flight in zip(chains, flights):
        chain.finish(*flight)
    return others


def place_xor(blocks, me, dtype):
    rows = blocks[0].shape[0]
    whole = jnp.zeros((4 * rows,) + blocks[0].shape[1:], dtype)
    for k, block in enumerate(blocks):
        whole = lax.dynamic_update_slice_in_dim(whole, block.astype(dtype), (me ^ k) * rows, 0)
    return whole


def to_xor(blocks, me):
    return [lax.dynamic_index_in_dim(blocks, me ^ k, 0, keepdims=False) for k in range(4)]


VMEM = pltpu.VMEM


def whole_hbm(count):
    return [pl.BlockSpec(memory_space=pl.ANY)] * count


def fixed(shape, *index):
    return pl.BlockSpec(shape, lambda *_: index)


def params(limit=32):
    return pltpu.CompilerParams(vmem_limit_bytes=limit * 1024 * 1024)


def attend_rows(query, key_ref, value_ref, bias, context_ref, weight_ref, inverse_ref):
    lane = lax.broadcasted_iota(jnp.int32, inverse_ref.shape, 1)
    inverses = jnp.zeros(inverse_ref.shape, F32)
    for head in range(query.shape[1] // HEAD):
        lanes = slice(head * HEAD, (head + 1) * HEAD)
        logits = dot_nt(query[:, lanes], key_ref[:, lanes]) + bias
        expon = jnp.exp(logits - jnp.max(logits, -1, keepdims=True)).astype(BF16)
        weight_ref[head] = expon
        inverse = 1.0 / jnp.sum(expon.astype(F32), -1, keepdims=True)
        inverses = jnp.where(lane == head, inverse, inverses)
        context_ref[:, lanes] = (dot(expon, value_ref[:, lanes]) * inverse).astype(BF16)
    inverse_ref[...] = inverses


def key_bias(scalar_ref, rows):
    block = rows // 4
    column = lax.broadcasted_iota(jnp.int32, (1, rows), 1)
    position = ((column // block) ^ scalar_ref[0]) * block + column % block
    return jnp.where(position < scalar_ref[1], 0.0, NEGATIVE).astype(F32)


def attend_first_kernel(
    scalar_ref,
    tokens_hbm,
    qkv_ref,
    context_ref,
    weight_ref,
    inverse_ref,
    query_ref,
    key_ref,
    value_ref,
    placed_hbm,
    tokens_ref,
    sems,
):
    step = pl.program_id(0)
    rows = tokens_ref.shape[0]
    block = rows // 4
    loads = []
    for k in range(4):
        source = pl.multiple_of((scalar_ref[0] ^ k) * block, block)
        loads.append(
            pltpu.make_async_copy(
                tokens_hbm.at[pl.ds(source, block)],
                tokens_ref.at[pl.ds(k * block, block)],
                sems.at[k],
            )
        )
    placing = pltpu.make_async_copy(tokens_ref, placed_hbm, sems.at[4])

    @pl.when(step == 0)
    def _():
        for load in loads:
            load.start()
        for load in loads:
            load.wait()
        placing.start()
        placed = tokens_ref[...]
        query_ref[...] = (dot(placed, qkv_ref[0]).astype(BF16) * HEAD ** (-0.5)).astype(BF16)
        key_ref[...] = dot(placed, qkv_ref[1]).astype(BF16)
        value_ref[...] = dot(placed, qkv_ref[2]).astype(BF16)

    bias = key_bias(scalar_ref, rows)
    query = query_ref[pl.ds(pl.multiple_of(step * block, block), block), :]
    attend_rows(query, key_ref, value_ref, bias, context_ref, weight_ref, inverse_ref)

    @pl.when(step == pl.num_programs(0) - 1)
    def _():
        placing.wait()


def attend_first(scalars, tokens, attn_qkv):
    rows, width = tokens.shape
    columns = attn_qkv.shape[2]
    heads = columns // HEAD
    block = rows // 4
    projected = jax.ShapeDtypeStruct((rows, columns), BF16)
    return pl.pallas_call(
        attend_first_kernel,
        grid=(2,),
        in_specs=[
            pl.BlockSpec(memory_space=pltpu.SMEM),
            pl.BlockSpec(memory_space=pl.ANY),
            fixed(attn_qkv.shape, 0, 0, 0),
        ],
        out_specs=[
            pl.BlockSpec((block, columns), lambda i: (i, 0)),
            pl.BlockSpec((heads, block, rows), lambda i: (0, i, 0)),
            pl.BlockSpec((block, 128), lambda i: (i, 0)),
        ]
        + [fixed((rows, columns), 0, 0)] * 3
        + [pl.BlockSpec(memory_space=pl.ANY)],
        out_shape=[
            jax.ShapeDtypeStruct((2 * block, columns), BF16),
            jax.ShapeDtypeStruct((heads, rows, rows), BF16),
            jax.ShapeDtypeStruct((2 * block, 128), F32),
        ]
        + [projected] * 3
        + [jax.ShapeDtypeStruct((rows, width), BF16)],
        scratch_shapes=[VMEM((rows, width), BF16), pltpu.SemaphoreType.DMA((5,))],
        compiler_params=params(),
        cost_estimate=pl.CostEstimate(flops=3000000000, bytes_accessed=9000000, transcendentals=0),
        name="attend_first",
    )(scalars, tokens, attn_qkv)


def attend_second_kernel(
    scalar_ref,
    query_ref,
    key_ref,
    value_ref,
    filled_hbm,
    context_ref,
    weight_ref,
    inverse_ref,
):
    del filled_hbm
    bias = key_bias(scalar_ref, key_ref.shape[0])
    attend_rows(query_ref[...], key_ref, value_ref, bias, context_ref, weight_ref, inverse_ref)


def attend_second(scalars, query, key, value, weights):
    rows, columns = query.shape
    heads = columns // HEAD
    block = rows // 4
    return pl.pallas_call(
        attend_second_kernel,
        grid=(2,),
        in_specs=[
            pl.BlockSpec(memory_space=pltpu.SMEM),
            pl.BlockSpec((block, columns), lambda i: (i + 2, 0)),
            fixed((rows, columns), 0, 0),
            fixed((rows, columns), 0, 0),
            pl.BlockSpec(memory_space=pl.ANY),
        ],
        out_specs=[
            pl.BlockSpec((block, columns), lambda i: (i, 0)),
            pl.BlockSpec((heads, block, rows), lambda i: (0, i + 2, 0)),
            pl.BlockSpec((block, 128), lambda i: (i, 0)),
        ],
        out_shape=[
            jax.ShapeDtypeStruct((2 * block, columns), BF16),
            jax.ShapeDtypeStruct((heads, rows, rows), BF16),
            jax.ShapeDtypeStruct((2 * block, 128), F32),
        ],
        input_output_aliases={4: 1},
        compiler_params=params(),
        cost_estimate=pl.CostEstimate(flops=2000000000, bytes_accessed=6000000, transcendentals=0),
        name="attend_second",
    )(scalars, query, key, value, weights)


def attend_back_kernel(
    query_ref,
    key_ref,
    value_ref,
    context_ref,
    inverse_ref,
    dcontext_ref,
    weight_ref,
    tokens_hbm,
    qkv_hbm,
    late_ref,
    part0_ref,
    part1_ref,
    part2_ref,
    part3_ref,
    dquery,
    dkey,
    dvalue,
    tokens_ref,
    qkv_ref,
    sems,
):
    step = pl.program_id(0)
    block = query_ref.shape[0]
    columns = query_ref.shape[1]
    loads = (
        pltpu.make_async_copy(tokens_hbm, tokens_ref, sems.at[0]),
        pltpu.make_async_copy(qkv_hbm, qkv_ref, sems.at[1]),
    )

    @pl.when(step == 0)
    def _():
        for load in loads:
            load.start()
        dkey[...] = jnp.zeros_like(dkey)
        dvalue[...] = jnp.zeros_like(dvalue)

    scaling = HEAD ** (-0.5)
    rows = pl.ds(pl.multiple_of(step * block, block), block)
    for head in range(columns // HEAD):
        lanes = slice(head * HEAD, (head + 1) * HEAD)
        weights = weight_ref[head]
        scaled = dcontext_ref[:, lanes].astype(F32) * inverse_ref[:, head : head + 1]
        delta = jnp.sum(scaled * context_ref[:, lanes].astype(F32), -1, keepdims=True)
        dcontext = scaled.astype(BF16)
        dweights = dot_nt(dcontext, value_ref[:, lanes])
        dlogits = (weights.astype(F32) * (dweights - delta)).astype(BF16)
        dquery[rows, lanes] = (dot(dlogits, key_ref[:, lanes]) * scaling).astype(BF16)
        dkey[lanes, :] += dot_tn(query_ref[:, lanes], dlogits)
        dvalue[lanes, :] += dot_tn(dcontext, weights)

    @pl.when(step == pl.num_programs(0) - 1)
    def _():
        for load in loads:
            load.wait()
        dkey_low = dkey[...].astype(BF16)
        dvalue_low = dvalue[...].astype(BF16)
        tokens = tokens_ref[...]
        late_ref[0:columns, :] = dot_tn(dquery[...], tokens).astype(BF16)
        late_ref[columns : 2 * columns, :] = dot(dkey_low, tokens).astype(BF16)
        late_ref[2 * columns :, :] = dot(dvalue_low, tokens).astype(BF16)
        for k, part_ref in enumerate((part0_ref, part1_ref, part2_ref, part3_ref)):
            part = slice(k * block, (k + 1) * block)
            dtokens = (
                dot_nt(dquery[part, :], qkv_ref[0])
                + dot(dkey_low[:, part].T, qkv_ref[1].T)
                + dot(dvalue_low[:, part].T, qkv_ref[2].T)
            )
            part_ref[...] = dtokens.astype(BF16)


def attend_back(query, key, value, weights, context, inverses, dcontext, tokens, attn_qkv):
    rows, columns = query.shape
    heads = columns // HEAD
    width = tokens.shape[1]
    block = rows // 4
    part = jax.ShapeDtypeStruct((block, width), BF16)
    return pl.pallas_call(
        attend_back_kernel,
        grid=(4,),
        in_specs=[
            pl.BlockSpec((block, columns), lambda i: (i, 0)),
            fixed((rows, columns), 0, 0),
            fixed((rows, columns), 0, 0),
            pl.BlockSpec((block, columns), lambda i: (i, 0)),
            pl.BlockSpec((block, 128), lambda i: (i, 0)),
            pl.BlockSpec((block, columns), lambda i: (i, 0)),
            pl.BlockSpec((heads, block, rows), lambda i: (0, i, 0)),
        ]
        + whole_hbm(2),
        out_specs=[fixed((3 * columns, width), 0, 0)] + [fixed((block, width), 0, 0)] * 4,
        out_shape=[jax.ShapeDtypeStruct((3 * columns, width), BF16)] + [part] * 4,
        scratch_shapes=[
            VMEM((rows, columns), BF16),
            VMEM((columns, rows), F32),
            VMEM((columns, rows), F32),
            VMEM(tokens.shape, BF16),
            VMEM(attn_qkv.shape, BF16),
            pltpu.SemaphoreType.DMA((2,)),
        ],
        compiler_params=params(),
        cost_estimate=pl.CostEstimate(flops=6000000000, bytes_accessed=14000000, transcendentals=0),
        name="attend_back",
    )(query, key, value, context, inverses, dcontext, weights, tokens, attn_qkv)


def feed_kernel(
    tokens_ref,
    context0_ref,
    context1_ref,
    context2_ref,
    context3_ref,
    bias_ref,
    gain_ref,
    shift_ref,
    mix0_hbm,
    mix1_hbm,
    mix2_hbm,
    mix3_hbm,
    in_hbm,
    out_hbm,
    first_low_ref,
    inner_ref,
    slope_ref,
    near_ref,
    far_ref,
    *refs,
):
    own_refs, (mix_ref, in_ref, out_ref, sems) = refs[:-4], refs[-4:]
    step = pl.program_id(0)
    columns = context0_ref.shape[1]
    loads = []
    for k, mix in enumerate((mix0_hbm, mix1_hbm, mix2_hbm, mix3_hbm)):
        loads.append(
            pltpu.make_async_copy(mix.at[pl.ds(0, columns)], mix_ref.at[k], sems.at[k])
        )
    loads.append(pltpu.make_async_copy(in_hbm, in_ref, sems.at[4]))
    loads.append(pltpu.make_async_copy(out_hbm, out_ref, sems.at[5]))

    @pl.when(step == 0)
    def _():
        for load in loads:
            load.start()
        for load in loads[:4]:
            load.wait()

    attended = (
        dot(context0_ref[...], mix_ref[0])
        + dot(context1_ref[...], mix_ref[1])
        + dot(context2_ref[...], mix_ref[2])
        + dot(context3_ref[...], mix_ref[3])
    )
    first, _, inverse = normalize(
        tokens_ref[...].astype(F32) + attended, gain_ref[0:1, :], shift_ref[0:1, :]
    )
    if own_refs:

        @pl.when(step == 0)
        def _():
            own_refs[0][...] = first
            own_refs[1][...] = inverse

    @pl.when(step == 0)
    def _():
        for load in loads[4:]:
            load.wait()

    first_low = first.astype(BF16)
    first_low_ref[...] = first_low
    inner, slope = gelu_both(dot(first_low, in_ref[...]) + bias_ref[...])
    inner = inner.astype(BF16)
    inner_ref[...] = inner
    slope_ref[...] = slope.astype(BF16)
    fed = dot(inner, out_ref[...]).astype(BF16)

    @pl.when(step == 0)
    def _():
        near_ref[...] = fed

    @pl.when(step == 1)
    def _():
        far_ref[...] = fed


def feed(half, tokens, contexts, mixes, ffn_in, bias, ffn_out, gains, shifts):
    rows, width = tokens.shape
    block = rows // 4
    columns = contexts[0].shape[1]
    hidden = ffn_in.shape[1]
    row_block = pl.BlockSpec((block, width), lambda i: (i, 0))
    hidden_block = pl.BlockSpec((block, hidden), lambda i: (i, 0))
    in_specs = [pl.BlockSpec((block, width), lambda i: (i + 2 * half, 0))]
    for k in range(4):
        in_specs.append(pl.BlockSpec((block, columns), lambda i, k=k: (i ^ (k & 1), 0)))
    in_specs += [fixed(array.shape, 0, 0) for array in (bias, gains, shifts)] + whole_hbm(6)
    out_specs = [row_block, hidden_block, hidden_block] + [fixed((block, width), 0, 0)] * 2
    out_shape = [
        jax.ShapeDtypeStruct((2 * block, width), BF16),
        jax.ShapeDtypeStruct((2 * block, hidden), BF16),
        jax.ShapeDtypeStruct((2 * block, hidden), BF16),
        jax.ShapeDtypeStruct((block, width), BF16),
        jax.ShapeDtypeStruct((block, width), BF16),
    ]
    if half == 0:
        out_specs += [fixed((block, width), 0, 0), fixed((block, 1), 0, 0)]
        out_shape += [
            jax.ShapeDtypeStruct((block, width), F32),
            jax.ShapeDtypeStruct((block, 1), F32),
        ]
    return pl.pallas_call(
        feed_kernel,
        grid=(2,),
        in_specs=in_specs,
        out_specs=out_specs,
        out_shape=out_shape,
        scratch_shapes=[
            VMEM((4, columns, width), BF16),
            VMEM(ffn_in.shape, BF16),
            VMEM(ffn_out.shape, BF16),
            pltpu.SemaphoreType.DMA((6,)),
        ],
        compiler_params=params(),
        cost_estimate=pl.CostEstimate(flops=3000000000, bytes_accessed=9000000, transcendentals=0),
        name="feed",
    )(tokens, *contexts, bias, gains, shifts, *mixes, ffn_in, ffn_out)


def feed_back_kernel(
    near_ref,
    far_ref,
    slope_ref,
    out_hbm,
    in_hbm,
    dinner_ref,
    near_part_ref,
    far_part_ref,
    sum_ref,
    out_ref,
    in_ref,
    sems,
):
    block = near_ref.shape[0]
    loads = (
        pltpu.make_async_copy(out_hbm, out_ref, sems.at[0]),
        pltpu.make_async_copy(in_hbm, in_ref, sems.at[1]),
    )
    for load in loads:
        load.start()
    for load in loads:
        load.wait()
    total = jnp.zeros((1, slope_ref.shape[1]), F32)
    for k, (dmid_ref, part_ref) in enumerate(
        ((near_ref, near_part_ref), (far_ref, far_part_ref))
    ):
        rows = slice(k * block, (k + 1) * block)
        dinner = (dot_nt(dmid_ref[...], out_ref[...]) * slope_ref[rows, :].astype(F32)).astype(BF16)
        dinner_ref[rows, :] = dinner
        total = total + jnp.sum(dinner.astype(F32), 0, keepdims=True)
        part_ref[...] = dot_nt(dinner, in_ref[...]).astype(BF16)
    sum_ref[0:1, :] = total
    sum_ref[1:8, :] = jnp.zeros((7, slope_ref.shape[1]), F32)


def feed_back(near, far, slope, ffn_out, ffn_in):
    block, width = near.shape
    hidden = slope.shape[1]
    part = jax.ShapeDtypeStruct((block, width), BF16)
    return pl.pallas_call(
        feed_back_kernel,
        grid=(1,),
        in_specs=[
            fixed(near.shape, 0, 0),
            fixed(far.shape, 0, 0),
            fixed((2 * block, hidden), 0, 0),
        ]
        + whole_hbm(2),
        out_specs=[
            fixed((2 * block, hidden), 0, 0),
            fixed(near.shape, 0, 0),
            fixed(far.shape, 0, 0),
            fixed((8, hidden), 0, 0),
        ],
        out_shape=[
            jax.ShapeDtypeStruct((2 * block, hidden), BF16),
            part,
            part,
            jax.ShapeDtypeStruct((8, hidden), F32),
        ],
        scratch_shapes=[
            VMEM(ffn_out.shape, BF16),
            VMEM(ffn_in.shape, BF16),
            pltpu.SemaphoreType.DMA((2,)),
        ],
        compiler_params=params(),
        cost_estimate=pl.CostEstimate(flops=1400000000, bytes_accessed=5000000, transcendentals=0),
        name="feed_back",
    )(near, far, slope, ffn_out, ffn_in)


def feed_grads_kernel(
    near_inner_hbm,
    far_inner_hbm,
    near_first_hbm,
    far_first_hbm,
    dmid0_hbm,
    dmid1_hbm,
    dmid2_hbm,
    dmid3_hbm,
    near_hbm,
    far_hbm,
    out_ref,
    in_ref,
    inner,
    dmid,
    first,
    dinner,
    sems,
):
    loads = [[], []]
    groups = (
        (0, inner, (near_inner_hbm, far_inner_hbm)),
        (0, dmid, (dmid0_hbm, dmid1_hbm, dmid2_hbm, dmid3_hbm)),
        (1, first, (near_first_hbm, far_first_hbm)),
        (1, dinner, (near_hbm, far_hbm)),
    )
    count = 0
    for turn, whole, parts in groups:
        start = 0
        for part in parts:
            rows = part.shape[0]
            loads[turn].append(
                pltpu.make_async_copy(part, whole.at[pl.ds(start, rows)], sems.at[count])
            )
            loads[turn][-1].start()
            start += rows
            count += 1
    for load in loads[0]:
        load.wait()
    out_ref[...] = dot_tn(inner[...], dmid[...]).astype(BF16)
    for load in loads[1]:
        load.wait()
    in_ref[...] = dot_tn(first[...], dinner[...]).astype(BF16)


def feed_grads(inners, firsts, dmids, near, far):
    rows, hidden = inners[0].shape[0] * 2, inners[0].shape[1]
    width = firsts[0].shape[1]
    arrays = (*inners, *firsts, *dmids, near, far)
    return pl.pallas_call(
        feed_grads_kernel,
        in_specs=whole_hbm(len(arrays)),
        out_specs=[pl.BlockSpec(memory_space=VMEM)] * 2,
        out_shape=[
            jax.ShapeDtypeStruct((hidden, width), BF16),
            jax.ShapeDtypeStruct((width, hidden), BF16),
        ],
        scratch_shapes=[
            VMEM((rows, hidden), BF16),
            VMEM((rows, width), BF16),
            VMEM((rows, width), BF16),
            VMEM((rows, hidden), BF16),
            pltpu.SemaphoreType.DMA((len(arrays),)),
        ],
        compiler_params=params(60),
        cost_estimate=pl.CostEstimate(flops=2400000000, bytes_accessed=9000000, transcendentals=0),
        name="feed_grads",
    )(*arrays)


def low_kernel(
    part_ref,
    beside_ref,
    across_ref,
    dmid_ref,
    first_ref,
    inverse_ref,
    gain_ref,
    shift_ref,
    small_ref,
    near_sum_ref,
    far_sum_ref,
    context0_hbm,
    context1_hbm,
    context2_hbm,
    context3_hbm,
    mix0_hbm,
    mix1_hbm,
    mix2_hbm,
    mix3_hbm,
    dlow_ref,
    dcontext0_ref,
    dcontext1_ref,
    dcontext23_ref,
    grad02_ref,
    grad13_ref,
    sums_ref,
    context_ref,
    mix_ref,
    sems,
):
    block = part_ref.shape[0]
    columns = dcontext0_ref.shape[1]
    loads = []
    for k, mix in enumerate((mix0_hbm, mix1_hbm, mix2_hbm, mix3_hbm)):
        loads.append(
            pltpu.make_async_copy(mix.at[pl.ds(0, columns)], mix_ref.at[k], sems.at[k])
        )
    for k, context in enumerate((context0_hbm, context1_hbm, context2_hbm, context3_hbm)):
        rows = pl.ds((k & 1) * block, block)
        loads.append(pltpu.make_async_copy(context.at[rows], context_ref.at[k], sems.at[4 + k]))
    for load in loads:
        load.start()
    dfirst = (
        part_ref[...].astype(F32)
        + beside_ref[...].astype(F32)
        + across_ref[...].astype(F32)
        + dmid_ref[...]
    )
    unit = (first_ref[...] - shift_ref[0:1, :]) / gain_ref[0:1, :]
    dlow, gain, shift = normalize_back(dfirst, unit, inverse_ref[...], gain_ref[0:1, :])
    dlow_ref[...] = dlow
    dlow_low = dlow.astype(BF16)
    for load in loads[:4]:
        load.wait()
    dcontext0_ref[...] = dot_nt(dlow_low, mix_ref[0]).astype(BF16)
    dcontext1_ref[...] = dot_nt(dlow_low, mix_ref[1]).astype(BF16)
    dcontext23_ref[0] = dot_nt(dlow_low, mix_ref[2]).astype(BF16)
    dcontext23_ref[1] = dot_nt(dlow_low, mix_ref[3]).astype(BF16)
    for load in loads[4:]:
        load.wait()
    grad02_ref[0:columns, :] = dot_tn(context_ref[0], dlow_low).astype(BF16)
    grad02_ref[columns:, :] = dot_tn(context_ref[2], dlow_low).astype(BF16)
    grad13_ref[0:columns, :] = dot_tn(context_ref[1], dlow_low).astype(BF16)
    grad13_ref[columns:, :] = dot_tn(context_ref[3], dlow_low).astype(BF16)
    sums_ref[0:6, :] = small_ref[0:6, :]
    sums_ref[6:7, :] = gain[None, :]
    sums_ref[7:8, :] = shift[None, :]
    sums_ref[8:16, :] = near_sum_ref[...] + far_sum_ref[...]


def low(
    part,
    near,
    far,
    dmid,
    first,
    inverse,
    gains,
    shifts,
    contexts,
    mixes,
    small,
    near_sum,
    far_sum,
):
    block, width = dmid.shape
    columns = contexts[0].shape[1]
    rows = fixed((block, width), 0, 0)
    in_specs = [rows] * 5
    in_specs += [fixed(array.shape, 0, 0) for array in (inverse, gains, shifts)]
    in_specs += [fixed(small.shape, 0, 0)] + [fixed(near_sum.shape, 0, 0)] * 2
    in_specs += whole_hbm(8)
    out_shape = [
        jax.ShapeDtypeStruct((block, width), F32),
        jax.ShapeDtypeStruct((block, columns), BF16),
        jax.ShapeDtypeStruct((block, columns), BF16),
        jax.ShapeDtypeStruct((2, block, columns), BF16),
        jax.ShapeDtypeStruct((2 * columns, width), BF16),
        jax.ShapeDtypeStruct((2 * columns, width), BF16),
        jax.ShapeDtypeStruct((16, width), F32),
    ]
    return pl.pallas_call(
        low_kernel,
        grid=(1,),
        in_specs=in_specs,
        out_specs=[fixed(out.shape, *([0] * len(out.shape))) for out in out_shape],
        out_shape=out_shape,
        scratch_shapes=[
            VMEM((4, block, columns), BF16),
            VMEM((4, columns, width), BF16),
            pltpu.SemaphoreType.DMA((8,)),
        ],
        compiler_params=params(60),
        cost_estimate=pl.CostEstimate(flops=600000000, bytes_accessed=6000000, transcendentals=0),
        name="low",
    )(
        part,
        near,
        far,
        dmid,
        first,
        inverse,
        gains,
        shifts,
        small,
        near_sum,
        far_sum,
        *contexts,
        *mixes,
    )


def merge_kernel(
    scalar_ref,
    first_ref,
    fed_ref,
    fed_beside_ref,
    fed_across_ref,
    bias_ref,
    gain_ref,
    shift_ref,
    cotangent_hbm,
    mix0_hbm,
    mix1_hbm,
    mix2_hbm,
    mix3_hbm,
    up0_hbm,
    up1_hbm,
    up2_hbm,
    up3_hbm,
    merging_hbm,
    output_ref,
    dmid_ref,
    dmid_low_ref,
    kept_ref,
    sent_ref,
    small_ref,
    down_ref,
    up_ref,
    mask_ref,
    merging_ref,
    cotangent_ref,
    sems,
):
    rows, width = first_ref.shape
    me = scalar_ref[0]
    length = scalar_ref[1]
    part = up0_hbm.shape[0] // 2
    columns = 4 * part
    copies = []
    for k, (mix, up) in enumerate(
        ((mix0_hbm, up0_hbm), (mix1_hbm, up1_hbm), (mix2_hbm, up2_hbm), (mix3_hbm, up3_hbm))
    ):
        place = pl.ds(k * part, part)
        copies.append(
            (
                pltpu.make_async_copy(up.at[pl.ds(0, part)], down_ref.at[place], sems.at[k]),
                pltpu.make_async_copy(up.at[pl.ds(part, part)], up_ref.at[place], sems.at[4 + k]),
                pltpu.make_async_copy(
                    mix.at[pl.ds(mix.shape[0] - MASK_ROWS, MASK_ROWS)],
                    mask_ref.at[k],
                    sems.at[8 + k],
                ),
            )
        )
    merging_copy = pltpu.make_async_copy(merging_hbm, merging_ref, sems.at[12])
    cotangent_copy = pltpu.make_async_copy(
        cotangent_hbm.at[pl.ds(pl.multiple_of(me * rows, rows), rows)], cotangent_ref, sems.at[13]
    )
    for group in copies:
        group[0].start()
    merging_copy.start()
    for group in copies:
        group[1].start()
        group[2].start()
    cotangent_copy.start()
    adapters = ADAPTERS
    scaling = width ** (-0.5)
    rank = columns // adapters
    held = adapters // 4
    expand = (
        lax.broadcasted_iota(jnp.int32, (adapters, columns), 1) // rank
        == lax.broadcasted_iota(jnp.int32, (adapters, columns), 0)
    ).astype(F32)
    expand = expand.astype(BF16)

    def collect(wide):
        high = wide.astype(BF16)
        rest = (wide - high.astype(F32)).astype(BF16)
        return dot_nt(high, expand) + dot_nt(rest, expand)

    fed = (
        fed_ref[...].astype(F32)
        + fed_beside_ref[...].astype(F32)
        + fed_across_ref[...].astype(F32)
        + bias_ref[...]
    )
    second, unit_second, inverse_second = normalize(
        first_ref[...] + fed, gain_ref[1:2, :], shift_ref[1:2, :]
    )
    second_low = second.astype(BF16)
    for group in copies:
        group[0].wait()
    squeezed, slope = gelu_both(dot_nt(second_low, down_ref[...]))
    squeezed = squeezed.astype(BF16).astype(F32)
    merging_copy.wait()
    fquery = dot(second_low, merging_ref[0]).astype(BF16)
    asked = dot_nt(fquery, merging_ref[1])
    for group in copies:
        group[1].wait()
        group[2].wait()
    cotangent_copy.wait()
    asked_up = dot_nt(asked.astype(BF16), up_ref[...])
    scores = scaling * (
        jnp.sum(asked * second, -1, keepdims=True) + collect(squeezed * asked_up)
    )
    lane = lax.broadcasted_iota(jnp.int32, (1, adapters), 1)
    usable = jnp.zeros((1, adapters), F32)
    for k in range(4):
        usable = jnp.where(lane // held == k, mask_ref[k, 0:1, 0:adapters].astype(F32), usable)
    usable = usable > 0.5
    scores = jnp.where(usable, scores, NEGATIVE)
    highest = jnp.max(scores, -1, keepdims=True)
    weights = jnp.where(usable, jnp.exp(scores - highest), 0.0)
    probs = weights / jnp.sum(weights, -1, keepdims=True)
    total = jnp.sum(probs, -1, keepdims=True)
    probs_wide = split_dot(probs, expand)
    mixed = total * second + dot((probs_wide * squeezed).astype(BF16), up_ref[...])
    mixed_low = mixed.astype(BF16)
    blended = dot(mixed_low, merging_ref[2])
    final, unit_third, inverse_third = normalize(
        second + blended, gain_ref[2:3, :], shift_ref[2:3, :]
    )
    output_ref[...] = final.astype(BF16)
    dthird, gain_third, shift_third = normalize_back(
        cotangent_ref[...].astype(F32), unit_third, inverse_third, gain_ref[2:3, :]
    )
    dthird_low = dthird.astype(BF16)
    pulled = dot_nt(dthird_low, merging_ref[2])
    pulled_up = dot_nt(pulled.astype(BF16), up_ref[...])
    dprobs = jnp.sum(pulled * second, -1, keepdims=True) + collect(squeezed * pulled_up)
    dscores = probs * (dprobs - jnp.sum(probs * dprobs, -1, keepdims=True)) * scaling
    dscores_total = jnp.sum(dscores, -1, keepdims=True)
    dscores_wide = split_dot(dscores, expand)
    weighed = dscores_total * second + dot((dscores_wide * squeezed).astype(BF16), up_ref[...])
    weighed_low = weighed.astype(BF16)
    dquery = dot(weighed_low, merging_ref[1]).astype(BF16)
    dbottle = ((dscores_wide * asked_up + probs_wide * pulled_up) * slope).astype(BF16)
    dsecond = (
        dthird
        + dscores_total * asked
        + total * pulled
        + dot(dbottle, down_ref[...])
        + dot_nt(dquery, merging_ref[0])
    )
    dmid, gain_second, shift_second = normalize_back(
        dsecond, unit_second, inverse_second, gain_ref[1:2, :]
    )
    dmid_ref[...] = dmid
    dmid_low_ref[...] = dmid.astype(BF16)
    position = me * rows + lax.broadcasted_iota(jnp.int32, (rows, 1), 0)
    mass = jnp.sum(jnp.where(position < length, probs, 0.0), 0, keepdims=True)
    source = lax.broadcasted_iota(jnp.int32, (adapters, width), 0)
    target = lax.broadcasted_iota(jnp.int32, (adapters, width), 1)
    move = ((source // held) ^ me) * held + source % held == target
    mass = lax.dot_general(
        jnp.broadcast_to(mass, (8, adapters)),
        move.astype(F32),
        (((1,), (0,)), ((), ())),
        precision=lax.Precision.HIGHEST,
        preferred_element_type=F32,
    )[0:1, :]
    counted = lax.broadcasted_iota(jnp.int32, (1, width), 1) == adapters
    small_ref[0:1, :] = gain_second[None, :]
    small_ref[1:2, :] = gain_third[None, :]
    small_ref[2:3, :] = shift_second[None, :]
    small_ref[3:4, :] = shift_third[None, :]
    small_ref[4:5, :] = jnp.sum(dmid, 0, keepdims=True)
    small_ref[5:6, :] = jnp.where(counted, 0.25 * length.astype(F32), mass)
    small_ref[6:8, :] = jnp.zeros((2, width), F32)
    core = me & 1
    half = width // 2
    for j, (left, right) in enumerate(
        ((second_low, dquery), (weighed_low, fquery), (mixed_low, dthird_low))
    ):
        grad = dot_tn(left, right).astype(BF16)
        for piece in (2 * j, 2 * j + 1):
            owner, place = piece // 3, piece % 3
            value = grad[(piece - 2 * j) * half : (piece - 2 * j + 1) * half, :]

            @pl.when(core == owner)
            def _():
                kept_ref[place * half : (place + 1) * half, :] = value

            @pl.when(core != owner)
            def _():
                sent_ref[place * half : (place + 1) * half, :] = value


def merge(scalars, first, fed, near, far, bias, gains, shifts, cotangent, mixes, ups, merging):
    rows, width = first.shape
    part = ups[0].shape[0] // 2
    grads = jax.ShapeDtypeStruct((3 * width // 2, width), BF16)
    out_shape = [
        jax.ShapeDtypeStruct((rows, width), BF16),
        jax.ShapeDtypeStruct((rows, width), F32),
        jax.ShapeDtypeStruct((rows, width), BF16),
        grads,
        grads,
        jax.ShapeDtypeStruct((8, width), F32),
    ]
    return pl.pallas_call(
        merge_kernel,
        grid=(1,),
        in_specs=[pl.BlockSpec(memory_space=pltpu.SMEM)]
        + [fixed(array.shape, 0, 0) for array in (first, fed, near, far, bias, gains, shifts)]
        + whole_hbm(10),
        out_specs=[fixed(array.shape, 0, 0) for array in out_shape],
        out_shape=out_shape,
        scratch_shapes=[
            VMEM((4 * part, width), BF16),
            VMEM((4 * part, width), BF16),
            VMEM((4, MASK_ROWS, width), BF16),
            VMEM(merging.shape, BF16),
            VMEM((rows, width), BF16),
            pltpu.SemaphoreType.DMA((14,)),
        ],
        compiler_params=params(),
        cost_estimate=pl.CostEstimate(flops=6000000000, bytes_accessed=14000000, transcendentals=0),
        name="merge",
    )(scalars, first, fed, near, far, bias, gains, shifts, cotangent, *mixes, *ups, merging)


def on_device(
    tokens,
    cotangent,
    attn_qkv,
    attn_out,
    ffn_in,
    ffn_bias_in,
    ffn_out,
    ffn_bias_out,
    norm_gains,
    norm_shifts,
    adapter_down,
    adapter_up,
    merging_proj,
    adapter_mask,
    lengths,
):
    me = lax.axis_index("ad")
    tok = lax.axis_size("tok")
    over_tok = tok_plan(tok)
    row_count, width = tokens.shape
    block = row_count // 4
    scalars = jnp.stack([me.astype(jnp.int32), lengths[0]])

    mask = jnp.tile(adapter_mask.astype(BF16), (MASK_ROWS, width // adapter_mask.shape[1]))
    mixes = gather_xor(jnp.concatenate([attn_out, mask], 0))

    near, weights, near_inverse, query, key, value, tokens = attend_first(
        scalars, tokens, attn_qkv
    )
    near_across = across(near)
    far, weights, far_inverse = attend_second(scalars, query, key, value, weights)
    far_across = across(far)
    near_contexts = [near, beside(near), far_across, beside(far_across)]
    far_contexts = [far, beside(far), near_across, beside(near_across)]
    ups = jnp.concatenate([adapter_down.T, adapter_up.reshape(-1, width)], 0)
    ups = gather_xor(after(ups, far))
    shared_weights = (mixes, ffn_in, ffn_bias_in[None, :], ffn_out, norm_gains, norm_shifts)
    far_first, far_inner, far_slope, fed2, fed3 = feed(1, tokens, far_contexts, *shared_weights)
    fed_far = across(add_low(fed2, beside(fed3)))
    near_contexts[0] = after(near, fed3)
    near_first, near_inner, near_slope, fed0, fed1, first, inverse = feed(
        0, tokens, near_contexts, *shared_weights
    )
    output_block, dmid, dmid_low, kept, sent, small = merge(
        scalars,
        first,
        fed0,
        beside(fed1),
        fed_far,
        ffn_bias_out[None, :],
        norm_gains,
        norm_shifts,
        cotangent,
        mixes,
        ups,
        merging_proj,
    )

    dmids = gather_xor(dmid_low)
    received = beside(sent)
    near_dinner, part0, part1, near_sum = feed_back(
        dmids[0], dmids[1], near_slope, ffn_out, ffn_in
    )
    merging = add_low(after(kept, part0), received)
    far_dinner, part2, part3, far_sum = feed_back(dmids[2], dmids[3], far_slope, ffn_out, ffn_in)
    part_beside = beside(part1)
    part_sum = add_low(part2, beside(part3))
    part_far = across(part_sum)
    nearest, further = over_tok[:1], over_tok[1:]
    merging = Chain(merging, nearest + further + [("ad", 4, 1)], [])
    grad_out, grad_in = feed_grads(
        (after(near_inner, part_sum), far_inner),
        (near_first, far_first),
        dmids,
        near_dinner,
        far_dinner,
    )
    part_far, part_beside, grad_out, grad_in = advance(
        [merging], part_far, part_beside, grad_out, grad_in
    )
    grad_out = Chain(grad_out, over_tok, over_tok[::-1])
    grad_in = Chain(grad_in, over_tok, over_tok[::-1])

    dlow, dcontext0, dcontext1, dcontext23, grad02, grad13, sums = low(
        part0,
        part_beside,
        part_far,
        dmid,
        first,
        inverse,
        norm_gains,
        norm_shifts,
        near_contexts,
        mixes,
        small,
        near_sum,
        far_sum,
    )
    dcontext_far = across(dcontext23)
    dcontext = jnp.concatenate(
        [dcontext0, beside(dcontext1), dcontext_far[0], beside(dcontext_far[1])], 0
    )
    grad02 = add_low(grad02, beside(grad13))
    columns = near.shape[1]
    shared = sums[:8] + beside(sums[:8])
    dcontext, grad02, shared = advance([merging, grad_in], dcontext, grad02, shared)

    grad_attn_far = across(grad02[columns:])
    shared_far = across(shared)
    late, dtokens0, dtokens1, dtokens2, dtokens3 = attend_back(
        query,
        key,
        value,
        weights,
        jnp.concatenate([near, far], 0),
        jnp.concatenate([near_inverse, far_inverse], 0),
        dcontext,
        tokens,
        attn_qkv,
    )
    late, grad_attn_far, shared_far = advance(
        [merging, grad_in, grad_out], late, grad_attn_far, shared_far
    )
    late = jnp.concatenate([late, add_low(grad02[:columns], grad_attn_far)], 0)
    late = Chain(late, over_tok, over_tok[::-1])
    sums = jnp.concatenate([shared + shared_far, sums[8:]], 0)
    dtokens_sum = add_low(dtokens2, beside(dtokens3))
    dtokens = dtokens0.astype(F32) + beside(dtokens1).astype(F32) + dlow
    dtokens_far = across(dtokens_sum)
    chains = [late, grad_out, grad_in]

    def sum_step(k):
        axis, size, bit = over_tok[k]
        return swap(sums, axis, size, 1 << bit)

    received, dtokens, dtokens_far = advance(
        [merging] + chains, sum_step(0), dtokens, dtokens_far
    )
    sums = sums + received
    while merging.steps:
        advance([merging])
    merging = lax.all_gather(merging.array, ("tok", "ad"), axis=0)
    dtokens = (dtokens + dtokens_far.astype(F32)).astype(BF16)
    received, dtokens_far = advance(chains, sum_step(1), across(dtokens))
    sums = sums + received
    pair = beside(jnp.concatenate([dtokens, dtokens_far], 0))
    received, pair, output_far = advance(chains, sum_step(2), pair, across(output_block))
    sums = sums + received
    grad_tokens = place_xor([dtokens, pair[:block], dtokens_far, pair[block:]], me, F32)
    pair = beside(jnp.concatenate([output_block, output_far], 0))
    (pair,) = advance(chains, pair)
    output = place_xor([output_block, pair[:block], output_far, pair[block:]], me, BF16)
    for k in range(3, len(over_tok)):
        (received,) = advance(chains, sum_step(k))
        sums = sums + received
    while late.steps:
        advance(chains)
    late, grad_out, grad_in = late.array, grad_out.array, grad_in.array
    bits = len(over_tok)
    merging = merging.reshape((2,) * bits + (2, 2) + merging.shape[1:])
    order = [bits + 1] + list(range(bits))[::-1] + [bits, bits + 2, bits + 3]
    merging = merging.transpose(order)

    held = ADAPTERS // 4
    usage = lax.dynamic_slice_in_dim(sums[5], me * held, held) / sums[5, ADAPTERS]
    return (
        output,
        grad_tokens,
        late[: 3 * columns].reshape(3, columns, width).swapaxes(1, 2).astype(F32),
        late[3 * columns :].astype(F32),
        grad_in.astype(F32),
        sums[8],
        grad_out.astype(F32),
        sums[4],
        jnp.stack([sums[6], sums[0], sums[1]]),
        jnp.stack([sums[7], sums[2], sums[3]]),
        merging.reshape(3, width, width).astype(F32),
        usage,
    )


def solution(mesh):
    placed = (
        P("tok", None),
        P("tok", None),
        P(None, None, "ad"),
        P("ad", None),
        P(None, "ad"),
        P("ad"),
        P("ad", None),
        P(),
        P(),
        P(),
        P(None, "ad"),
        P("ad", None, None),
        P(),
        P("tok", "ad"),
        P("tok"),
    )
    return jax.shard_map(
        on_device,
        mesh=mesh,
        in_specs=placed,
        out_specs=(
            P("tok", None),
            P("tok", None),
            P(None, None, "ad"),
            P("ad", None),
            P(None, "ad"),
            P("ad"),
            P("ad", None),
            P(),
            P(),
            P(),
            P(),
            P("ad"),
        ),
        check_vma=False,
    )
```

```python
import jax
import jax.numpy as jnp
from jax import lax
from jax.experimental import pallas as pl
from jax.experimental.pallas import tpu as pltpu
from jax.sharding import PartitionSpec as P

HEAD = 64
EPSILON = 1e-06
NEGATIVE = -1e30
ADAPTERS = 16
MASK_ROWS = 16
F32 = jnp.float32
BF16 = jnp.bfloat16


def normalize(values, gain, shift):
    centred = values - jnp.mean(values, -1, keepdims=True)
    inverse = lax.rsqrt(jnp.mean(centred * centred, -1, keepdims=True) + EPSILON)
    unit_rows = centred * inverse
    return (unit_rows * gain + shift, unit_rows, inverse)


def normalize_back(gradient, unit_rows, inverse, gain):
    scaled = gradient * gain
    centred = (
        scaled
        - jnp.mean(scaled, -1, keepdims=True)
        - unit_rows * jnp.mean(scaled * unit_rows, -1, keepdims=True)
    )
    return (centred * inverse, jnp.sum(gradient * unit_rows, 0), jnp.sum(gradient, 0))


def gelu_both(values):
    cdf = 0.5 * (1.0 + lax.erf(values * 0.7071067811865476))
    density = jnp.exp(-0.5 * values * values) * 0.3989422804014327
    return values * cdf, cdf + values * density


def dot(left, right, dims=((1,), (0,))):
    return lax.dot_general(left, right, (dims, ((), ())), preferred_element_type=F32)


def dot_nt(left, right):
    return dot(left, right, ((1,), (1,)))


def dot_tn(left, right):
    return dot(left, right, ((0,), (0,)))


def split_dot(left, right):
    high = left.astype(BF16)
    rest = (left - high.astype(F32)).astype(BF16)
    return dot(high, right) + dot(rest, right)


def after(array, *others):
    return lax.optimization_barrier((array, *others))[0]


def swap(array, axis, size, step):
    return lax.ppermute(array, axis, [(i, i ^ step) for i in range(size)])


def beside(array):
    return swap(array, "ad", 4, 1)


def across(array):
    return swap(array, "ad", 4, 2)


def gather_xor(block):
    far = across(block)
    return [block, beside(block), far, beside(far)]


def tok_plan(size):
    return [("tok", size, bit) for bit in range(size.bit_length() - 1)]


def side_of(step):
    axis, _, bit = step
    return (lax.axis_index(axis) >> bit) & 1


def halve_start(array, step):
    axis, size, bit = step
    side = side_of(step)
    rows = array.shape[0] // 2
    sent = lax.dynamic_slice_in_dim(array, (1 - side) * rows, rows)
    kept = lax.dynamic_slice_in_dim(array, side * rows, rows)
    return kept, swap(sent, axis, size, 1 << bit)


def add_low(kept, received):
    return (kept.astype(F32) + received.astype(F32)).astype(BF16)


def halve(array, plan):
    for step in plan:
        array = add_low(*halve_start(array, step))
    return array


def double(array, plan):
    for step in reversed(plan):
        axis, size, bit = step
        side = side_of(step) == 1
        other = swap(array, axis, size, 1 << bit)
        array = jnp.concatenate(
            [jnp.where(side, other, array), jnp.where(side, array, other)], 0
        )
    return array


class Chain:
    def __init__(self, array, halving, doubling=()):
        self.array = array
        self.steps = [(True, *step) for step in halving] + [(False, *step) for step in doubling]
        self.parts = None

    def prepare(self):
        halves, step, place = self.steps[0]
        self.parts = (self.array, self.array)
        if halves:
            side = side_of(step)
            self.parts = tuple(
                lax.dynamic_index_in_dim(self.array, part, place, keepdims=False)
                for part in (side, 1 - side)
            )
        return self.parts

    def start(self):
        _, (axis, size, bit), _ = self.steps[0]
        kept, sent = self.parts or self.prepare()
        self.parts = None
        return kept, swap(sent, axis, size, 1 << bit)

    def finish(self, own, received):
        halves, step, place = self.steps.pop(0)
        if halves:
            self.array = add_low(own, received)
        else:
            side = side_of(step) == 1
            self.array = jnp.stack(
                [jnp.where(side, received, own), jnp.where(side, own, received)], place
            )


def tok_chain(array, over_tok):
    bits = len(over_tok)
    steps = [(step, 0) for step in over_tok]
    return Chain(array.reshape((2,) * bits + (-1, array.shape[1])), steps, steps[::-1])


def advance(chains, *others):
    chains = [chain for chain in chains if chain.steps]
    flights = [chain.start() for chain in chains]
    flights, others = lax.optimization_barrier((flights, others))
    for chain, flight in zip(chains, flights):
        chain.finish(*flight)
    return others


def place_xor(blocks, me, dtype):
    rows = blocks[0].shape[0]
    whole = jnp.zeros((4 * rows,) + blocks[0].shape[1:], dtype)
    for k, block in enumerate(blocks):
        whole = lax.dynamic_update_slice_in_dim(whole, block.astype(dtype), (me ^ k) * rows, 0)
    return whole


def to_xor(blocks, me):
    return [lax.dynamic_index_in_dim(blocks, me ^ k, 0, keepdims=False) for k in range(4)]


VMEM = pltpu.VMEM


def whole_hbm(count):
    return [pl.BlockSpec(memory_space=pl.ANY)] * count


def fixed(shape, *index):
    return pl.BlockSpec(shape, lambda *_: index)


def params(limit=32):
    return pltpu.CompilerParams(vmem_limit_bytes=limit * 1024 * 1024)


def attend_rows(query, key_ref, value_ref, bias, context_ref, weight_ref, inverse_ref):
    lane = lax.broadcasted_iota(jnp.int32, inverse_ref.shape, 1)
    inverses = jnp.zeros(inverse_ref.shape, F32)
    for head in range(query.shape[1] // HEAD):
        lanes = slice(head * HEAD, (head + 1) * HEAD)
        logits = dot_nt(query[:, lanes], key_ref[:, lanes]) + bias
        expon = jnp.exp(logits - jnp.max(logits, -1, keepdims=True)).astype(BF16)
        weight_ref[head] = expon
        inverse = 1.0 / jnp.sum(expon.astype(F32), -1, keepdims=True)
        inverses = jnp.where(lane == head, inverse, inverses)
        context_ref[:, lanes] = (dot(expon, value_ref[:, lanes]) * inverse).astype(BF16)
    inverse_ref[...] = inverses


def key_bias(scalar_ref, rows):
    block = rows // 4
    column = lax.broadcasted_iota(jnp.int32, (1, rows), 1)
    position = ((column // block) ^ scalar_ref[0]) * block + column % block
    return jnp.where(position < scalar_ref[1], 0.0, NEGATIVE).astype(F32)


def attend_kernel(
    scalar_ref,
    tokens_hbm,
    qkv_ref,
    context_ref,
    weight_ref,
    inverse_ref,
    query_ref,
    key_ref,
    value_ref,
    placed_hbm,
    tokens_ref,
    sems,
):
    step = pl.program_id(0)
    rows = tokens_ref.shape[0]
    block = rows // 4
    loads = []
    for k in range(4):
        source = pl.multiple_of((scalar_ref[0] ^ k) * block, block)
        loads.append(
            pltpu.make_async_copy(
                tokens_hbm.at[pl.ds(source, block)],
                tokens_ref.at[pl.ds(k * block, block)],
                sems.at[k],
            )
        )
    placing = pltpu.make_async_copy(tokens_ref, placed_hbm, sems.at[4])

    @pl.when(step == 0)
    def _():
        for load in loads:
            load.start()
        for load in loads:
            load.wait()
        placing.start()
        placed = tokens_ref[...]
        query_ref[...] = (dot_nt(placed, qkv_ref[0]).astype(BF16) * HEAD ** (-0.5)).astype(BF16)
        key_ref[...] = dot_nt(placed, qkv_ref[1]).astype(BF16)
        value_ref[...] = dot_nt(placed, qkv_ref[2]).astype(BF16)

    bias = key_bias(scalar_ref, rows)
    query = query_ref[pl.ds(pl.multiple_of(step * block, block), block), :]
    attend_rows(query, key_ref, value_ref, bias, context_ref, weight_ref, inverse_ref)

    @pl.when(step == pl.num_programs(0) - 1)
    def _():
        placing.wait()


def attend(scalars, tokens, attn_qkv):
    rows, width = tokens.shape
    columns = attn_qkv.shape[1]
    heads = columns // HEAD
    block = rows // 4
    projected = jax.ShapeDtypeStruct((rows, columns), BF16)
    return pl.pallas_call(
        attend_kernel,
        grid=(4,),
        in_specs=[
            pl.BlockSpec(memory_space=pltpu.SMEM),
            pl.BlockSpec(memory_space=pl.ANY),
            fixed(attn_qkv.shape, 0, 0, 0),
        ],
        out_specs=[
            pl.BlockSpec((block, columns), lambda i: (i, 0)),
            pl.BlockSpec((heads, block, rows), lambda i: (0, i, 0)),
            pl.BlockSpec((block, 128), lambda i: (i, 0)),
        ]
        + [fixed((rows, columns), 0, 0)] * 3
        + [pl.BlockSpec(memory_space=pl.ANY)],
        out_shape=[
            jax.ShapeDtypeStruct((rows, columns), BF16),
            jax.ShapeDtypeStruct((heads, rows, rows), BF16),
            jax.ShapeDtypeStruct((rows, 128), F32),
        ]
        + [projected] * 3
        + [jax.ShapeDtypeStruct((rows, width), BF16)],
        scratch_shapes=[VMEM((rows, width), BF16), pltpu.SemaphoreType.DMA((5,))],
        compiler_params=params(),
        cost_estimate=pl.CostEstimate(flops=5000000000, bytes_accessed=14000000, transcendentals=0),
        name="attend",
    )(scalars, tokens, attn_qkv)


def attend_back_kernel(
    query_ref,
    key_ref,
    value_ref,
    context_ref,
    inverse_ref,
    dcontext_ref,
    weight_ref,
    tokens_hbm,
    qkv_hbm,
    late_ref,
    part0_ref,
    part2_ref,
    part13_ref,
    dquery,
    dkey,
    dvalue,
    tokens_ref,
    qkv_ref,
    sems,
):
    step = pl.program_id(0)
    block = query_ref.shape[0]
    columns = query_ref.shape[1]
    loads = (
        pltpu.make_async_copy(tokens_hbm, tokens_ref, sems.at[0]),
        pltpu.make_async_copy(qkv_hbm, qkv_ref, sems.at[1]),
    )

    @pl.when(step == 0)
    def _():
        for load in loads:
            load.start()
        dkey[...] = jnp.zeros_like(dkey)
        dvalue[...] = jnp.zeros_like(dvalue)

    scaling = HEAD ** (-0.5)
    rows = pl.ds(pl.multiple_of(step * block, block), block)
    for head in range(columns // HEAD):
        lanes = slice(head * HEAD, (head + 1) * HEAD)
        weights = weight_ref[head]
        scaled = dcontext_ref[:, lanes].astype(F32) * inverse_ref[:, head : head + 1]
        delta = jnp.sum(scaled * context_ref[:, lanes].astype(F32), -1, keepdims=True)
        dcontext = scaled.astype(BF16)
        dweights = dot_nt(dcontext, value_ref[:, lanes])
        dlogits = (weights.astype(F32) * (dweights - delta)).astype(BF16)
        dquery[rows, lanes] = (dot(dlogits, key_ref[:, lanes]) * scaling).astype(BF16)
        dkey[lanes, :] += dot_tn(query_ref[:, lanes], dlogits)
        dvalue[lanes, :] += dot_tn(dcontext, weights)

    @pl.when(step == pl.num_programs(0) - 1)
    def _():
        for load in loads:
            load.wait()
        dkey_low = dkey[...].astype(BF16)
        dvalue_low = dvalue[...].astype(BF16)
        tokens = tokens_ref[...]
        late_ref[0:columns, :] = dot_tn(dquery[...], tokens).astype(BF16)
        late_ref[columns : 2 * columns, :] = dot(dkey_low, tokens).astype(BF16)
        late_ref[2 * columns :, :] = dot(dvalue_low, tokens).astype(BF16)
        part_refs = (part0_ref, part13_ref.at[0], part2_ref, part13_ref.at[1])
        for k, part_ref in enumerate(part_refs):
            part = slice(k * block, (k + 1) * block)
            dtokens = (
                dot(dquery[part, :], qkv_ref[0])
                + dot_tn(dkey_low[:, part], qkv_ref[1])
                + dot_tn(dvalue_low[:, part], qkv_ref[2])
            )
            part_ref[...] = dtokens.astype(BF16)


def attend_back(query, key, value, weights, context, inverses, dcontext, tokens, attn_qkv):
    rows, columns = query.shape
    heads = columns // HEAD
    width = tokens.shape[1]
    block = rows // 4
    part = jax.ShapeDtypeStruct((block, width), BF16)
    return pl.pallas_call(
        attend_back_kernel,
        grid=(4,),
        in_specs=[
            pl.BlockSpec((block, columns), lambda i: (i, 0)),
            fixed((rows, columns), 0, 0),
            fixed((rows, columns), 0, 0),
            pl.BlockSpec((block, columns), lambda i: (i, 0)),
            pl.BlockSpec((block, 128), lambda i: (i, 0)),
            pl.BlockSpec((block, columns), lambda i: (i, 0)),
            pl.BlockSpec((heads, block, rows), lambda i: (0, i, 0)),
        ]
        + whole_hbm(2),
        out_specs=[fixed((3 * columns, width), 0, 0)]
        + [fixed((block, width), 0, 0)] * 2
        + [fixed((2, block, width), 0, 0, 0)],
        out_shape=[
            jax.ShapeDtypeStruct((3 * columns, width), BF16),
            part,
            part,
            jax.ShapeDtypeStruct((2, block, width), BF16),
        ],
        scratch_shapes=[
            VMEM((rows, columns), BF16),
            VMEM((columns, rows), F32),
            VMEM((columns, rows), F32),
            VMEM(tokens.shape, BF16),
            VMEM(attn_qkv.shape, BF16),
            pltpu.SemaphoreType.DMA((2,)),
        ],
        compiler_params=params(),
        cost_estimate=pl.CostEstimate(flops=6000000000, bytes_accessed=14000000, transcendentals=0),
        name="attend_back",
    )(query, key, value, context, inverses, dcontext, weights, tokens, attn_qkv)


def feed_kernel(
    tokens_ref,
    context0_ref,
    context1_ref,
    context2_ref,
    context3_ref,
    bias_ref,
    gain_ref,
    shift_ref,
    mix0_hbm,
    mix1_hbm,
    mix2_hbm,
    mix3_hbm,
    in_hbm,
    out_hbm,
    first_low_ref,
    inner_ref,
    slope_ref,
    near_ref,
    far_ref,
    *refs,
):
    own_refs, (mix_ref, in_ref, out_ref, sems) = refs[:-4], refs[-4:]
    step = pl.program_id(0)
    columns = context0_ref.shape[1]
    loads = []
    for k, mix in enumerate((mix0_hbm, mix1_hbm, mix2_hbm, mix3_hbm)):
        loads.append(
            pltpu.make_async_copy(mix.at[pl.ds(0, columns)], mix_ref.at[k], sems.at[k])
        )
    loads.append(pltpu.make_async_copy(in_hbm, in_ref, sems.at[4]))
    loads.append(pltpu.make_async_copy(out_hbm, out_ref, sems.at[5]))

    @pl.when(step == 0)
    def _():
        for load in loads:
            load.start()
        for load in loads[:4]:
            load.wait()

    attended = (
        dot(context0_ref[...], mix_ref[0])
        + dot(context1_ref[...], mix_ref[1])
        + dot(context2_ref[...], mix_ref[2])
        + dot(context3_ref[...], mix_ref[3])
    )
    first, _, inverse = normalize(
        tokens_ref[...].astype(F32) + attended, gain_ref[0:1, :], shift_ref[0:1, :]
    )
    if own_refs:

        @pl.when(step == 0)
        def _():
            own_refs[0][...] = first
            own_refs[1][...] = inverse

    @pl.when(step == 0)
    def _():
        for load in loads[4:]:
            load.wait()

    first_low = first.astype(BF16)
    first_low_ref[...] = first_low
    inner, slope = gelu_both(dot(first_low, in_ref[...]) + bias_ref[...])
    inner = inner.astype(BF16)
    inner_ref[...] = inner
    slope_ref[...] = slope.astype(BF16)
    fed = dot(inner, out_ref[...]).astype(BF16)

    @pl.when(step == 0)
    def _():
        near_ref[...] = fed

    @pl.when(step == 1)
    def _():
        far_ref[...] = fed


def feed(half, tokens, contexts, mixes, ffn_in, bias, ffn_out, gains, shifts):
    rows, width = tokens.shape
    block = rows // 4
    columns = contexts[0].shape[1]
    hidden = ffn_in.shape[1]
    row_block = pl.BlockSpec((block, width), lambda i: (i, 0))
    hidden_block = pl.BlockSpec((block, hidden), lambda i: (i, 0))
    in_specs = [pl.BlockSpec((block, width), lambda i: (i + 2 * half, 0))]
    for k in range(4):
        in_specs.append(pl.BlockSpec((block, columns), lambda i, k=k: ((i + 2 * half) ^ k, 0)))
    in_specs += [fixed(array.shape, 0, 0) for array in (bias, gains, shifts)] + whole_hbm(6)
    out_specs = [row_block, hidden_block, hidden_block] + [fixed((block, width), 0, 0)] * 2
    out_shape = [
        jax.ShapeDtypeStruct((2 * block, width), BF16),
        jax.ShapeDtypeStruct((2 * block, hidden), BF16),
        jax.ShapeDtypeStruct((2 * block, hidden), BF16),
        jax.ShapeDtypeStruct((block, width), BF16),
        jax.ShapeDtypeStruct((block, width), BF16),
    ]
    if half == 0:
        out_specs += [fixed((block, width), 0, 0), fixed((block, 1), 0, 0)]
        out_shape += [
            jax.ShapeDtypeStruct((block, width), F32),
            jax.ShapeDtypeStruct((block, 1), F32),
        ]
    return pl.pallas_call(
        feed_kernel,
        grid=(2,),
        in_specs=in_specs,
        out_specs=out_specs,
        out_shape=out_shape,
        scratch_shapes=[
            VMEM((4, columns, width), BF16),
            VMEM(ffn_in.shape, BF16),
            VMEM(ffn_out.shape, BF16),
            pltpu.SemaphoreType.DMA((6,)),
        ],
        compiler_params=params(),
        cost_estimate=pl.CostEstimate(flops=3000000000, bytes_accessed=9000000, transcendentals=0),
        name="feed",
    )(tokens, *contexts, bias, gains, shifts, *mixes, ffn_in, ffn_out)


def feed_back_kernel(
    near_ref,
    far_ref,
    slope_ref,
    out_hbm,
    in_hbm,
    dinner_ref,
    near_part_ref,
    far_part_ref,
    sum_ref,
    out_ref,
    in_ref,
    sems,
):
    block = near_ref.shape[0]
    loads = (
        pltpu.make_async_copy(out_hbm, out_ref, sems.at[0]),
        pltpu.make_async_copy(in_hbm, in_ref, sems.at[1]),
    )
    for load in loads:
        load.start()
    for load in loads:
        load.wait()
    total = jnp.zeros((1, slope_ref.shape[1]), F32)
    for k, (dmid_ref, part_ref) in enumerate(
        ((near_ref, near_part_ref), (far_ref, far_part_ref))
    ):
        rows = slice(k * block, (k + 1) * block)
        dinner = (dot_nt(dmid_ref[...], out_ref[...]) * slope_ref[rows, :].astype(F32)).astype(BF16)
        dinner_ref[rows, :] = dinner
        total = total + jnp.sum(dinner.astype(F32), 0, keepdims=True)
        part_ref[...] = dot_nt(dinner, in_ref[...]).astype(BF16)
    sum_ref[0:1, :] = total
    sum_ref[1:8, :] = jnp.zeros((7, slope_ref.shape[1]), F32)


def feed_back(near, far, slope, ffn_out, ffn_in):
    block, width = near.shape
    hidden = slope.shape[1]
    part = jax.ShapeDtypeStruct((block, width), BF16)
    return pl.pallas_call(
        feed_back_kernel,
        grid=(1,),
        in_specs=[
            fixed(near.shape, 0, 0),
            fixed(far.shape, 0, 0),
            fixed((2 * block, hidden), 0, 0),
        ]
        + whole_hbm(2),
        out_specs=[
            fixed((2 * block, hidden), 0, 0),
            fixed(near.shape, 0, 0),
            fixed(far.shape, 0, 0),
            fixed((8, hidden), 0, 0),
        ],
        out_shape=[
            jax.ShapeDtypeStruct((2 * block, hidden), BF16),
            part,
            part,
            jax.ShapeDtypeStruct((8, hidden), F32),
        ],
        scratch_shapes=[
            VMEM(ffn_out.shape, BF16),
            VMEM(ffn_in.shape, BF16),
            pltpu.SemaphoreType.DMA((2,)),
        ],
        compiler_params=params(),
        cost_estimate=pl.CostEstimate(flops=1400000000, bytes_accessed=5000000, transcendentals=0),
        name="feed_back",
    )(near, far, slope, ffn_out, ffn_in)


def feed_grads_kernel(
    near_inner_hbm,
    far_inner_hbm,
    near_first_hbm,
    far_first_hbm,
    dmid0_hbm,
    dmid1_hbm,
    dmid2_hbm,
    dmid3_hbm,
    near_hbm,
    far_hbm,
    out_ref,
    in_ref,
    inner,
    dmid,
    first,
    dinner,
    sems,
):
    loads = [[], []]
    groups = (
        (0, inner, (near_inner_hbm, far_inner_hbm)),
        (0, dmid, (dmid0_hbm, dmid1_hbm, dmid2_hbm, dmid3_hbm)),
        (1, first, (near_first_hbm, far_first_hbm)),
        (1, dinner, (near_hbm, far_hbm)),
    )
    count = 0
    for turn, whole, parts in groups:
        start = 0
        for part in parts:
            rows = part.shape[0]
            loads[turn].append(
                pltpu.make_async_copy(part, whole.at[pl.ds(start, rows)], sems.at[count])
            )
            loads[turn][-1].start()
            start += rows
            count += 1
    for load in loads[0]:
        load.wait()
    out_ref[...] = dot_tn(inner[...], dmid[...]).astype(BF16)
    for load in loads[1]:
        load.wait()
    in_ref[...] = dot_tn(first[...], dinner[...]).astype(BF16)


def feed_grads(inners, firsts, dmids, near, far):
    rows, hidden = inners[0].shape[0] * 2, inners[0].shape[1]
    width = firsts[0].shape[1]
    arrays = (*inners, *firsts, *dmids, near, far)
    return pl.pallas_call(
        feed_grads_kernel,
        in_specs=whole_hbm(len(arrays)),
        out_specs=[pl.BlockSpec(memory_space=VMEM)] * 2,
        out_shape=[
            jax.ShapeDtypeStruct((hidden, width), BF16),
            jax.ShapeDtypeStruct((width, hidden), BF16),
        ],
        scratch_shapes=[
            VMEM((rows, hidden), BF16),
            VMEM((rows, width), BF16),
            VMEM((rows, width), BF16),
            VMEM((rows, hidden), BF16),
            pltpu.SemaphoreType.DMA((len(arrays),)),
        ],
        compiler_params=params(60),
        cost_estimate=pl.CostEstimate(flops=2400000000, bytes_accessed=9000000, transcendentals=0),
        name="feed_grads",
    )(*arrays)


def low_kernel(
    part_ref,
    beside_ref,
    across_ref,
    dmid_ref,
    first_ref,
    inverse_ref,
    gain_ref,
    shift_ref,
    small_ref,
    near_sum_ref,
    far_sum_ref,
    context0_hbm,
    context1_hbm,
    context2_hbm,
    context3_hbm,
    mix0_hbm,
    mix1_hbm,
    mix2_hbm,
    mix3_hbm,
    dlow_ref,
    dcontext0_ref,
    dcontext1_ref,
    dcontext23_ref,
    grad02_ref,
    grad13_ref,
    sums_ref,
    context_ref,
    mix_ref,
    sems,
):
    block = part_ref.shape[0]
    columns = dcontext0_ref.shape[1]
    loads = []
    for k, mix in enumerate((mix0_hbm, mix1_hbm, mix2_hbm, mix3_hbm)):
        loads.append(
            pltpu.make_async_copy(mix.at[pl.ds(0, columns)], mix_ref.at[k], sems.at[k])
        )
    for k, context in enumerate((context0_hbm, context1_hbm, context2_hbm, context3_hbm)):
        rows = pl.ds(k * block, block)
        loads.append(pltpu.make_async_copy(context.at[rows], context_ref.at[k], sems.at[4 + k]))
    for load in loads:
        load.start()
    dfirst = (
        part_ref[...].astype(F32)
        + beside_ref[...].astype(F32)
        + across_ref[...].astype(F32)
        + dmid_ref[...]
    )
    unit = (first_ref[...] - shift_ref[0:1, :]) / gain_ref[0:1, :]
    dlow, gain, shift = normalize_back(dfirst, unit, inverse_ref[...], gain_ref[0:1, :])
    dlow_ref[...] = dlow
    dlow_low = dlow.astype(BF16)
    for load in loads[:4]:
        load.wait()
    dcontext0_ref[...] = dot_nt(dlow_low, mix_ref[0]).astype(BF16)
    dcontext1_ref[...] = dot_nt(dlow_low, mix_ref[1]).astype(BF16)
    dcontext23_ref[0] = dot_nt(dlow_low, mix_ref[2]).astype(BF16)
    dcontext23_ref[1] = dot_nt(dlow_low, mix_ref[3]).astype(BF16)
    for load in loads[4:]:
        load.wait()
    grad02_ref[0:columns, :] = dot_tn(context_ref[0], dlow_low).astype(BF16)
    grad02_ref[columns:, :] = dot_tn(context_ref[2], dlow_low).astype(BF16)
    grad13_ref[0:columns, :] = dot_tn(context_ref[1], dlow_low).astype(BF16)
    grad13_ref[columns:, :] = dot_tn(context_ref[3], dlow_low).astype(BF16)
    sums_ref[0:6, :] = small_ref[0:6, :]
    sums_ref[6:7, :] = gain[None, :]
    sums_ref[7:8, :] = shift[None, :]
    sums_ref[8:16, :] = near_sum_ref[...] + far_sum_ref[...]


def low(
    part,
    near,
    far,
    dmid,
    first,
    inverse,
    gains,
    shifts,
    contexts,
    mixes,
    small,
    near_sum,
    far_sum,
):
    block, width = dmid.shape
    columns = contexts[0].shape[1]
    rows = fixed((block, width), 0, 0)
    in_specs = [rows] * 5
    in_specs += [fixed(array.shape, 0, 0) for array in (inverse, gains, shifts)]
    in_specs += [fixed(small.shape, 0, 0)] + [fixed(near_sum.shape, 0, 0)] * 2
    in_specs += whole_hbm(8)
    out_shape = [
        jax.ShapeDtypeStruct((block, width), F32),
        jax.ShapeDtypeStruct((block, columns), BF16),
        jax.ShapeDtypeStruct((block, columns), BF16),
        jax.ShapeDtypeStruct((2, block, columns), BF16),
        jax.ShapeDtypeStruct((2 * columns, width), BF16),
        jax.ShapeDtypeStruct((2 * columns, width), BF16),
        jax.ShapeDtypeStruct((16, width), F32),
    ]
    return pl.pallas_call(
        low_kernel,
        grid=(1,),
        in_specs=in_specs,
        out_specs=[fixed(out.shape, *([0] * len(out.shape))) for out in out_shape],
        out_shape=out_shape,
        scratch_shapes=[
            VMEM((4, block, columns), BF16),
            VMEM((4, columns, width), BF16),
            pltpu.SemaphoreType.DMA((8,)),
        ],
        compiler_params=params(60),
        cost_estimate=pl.CostEstimate(flops=600000000, bytes_accessed=6000000, transcendentals=0),
        name="low",
    )(
        part,
        near,
        far,
        dmid,
        first,
        inverse,
        gains,
        shifts,
        small,
        near_sum,
        far_sum,
        *contexts,
        *mixes,
    )


def merge_kernel(
    scalar_ref,
    first_ref,
    fed_ref,
    fed_beside_ref,
    fed_across_ref,
    bias_ref,
    gain_ref,
    shift_ref,
    cotangent_hbm,
    mix0_hbm,
    mix1_hbm,
    mix2_hbm,
    mix3_hbm,
    merging_hbm,
    output_ref,
    dmid_ref,
    dmid_low_ref,
    kept_ref,
    sent_ref,
    small_ref,
    down_ref,
    up_ref,
    mask_ref,
    merging_ref,
    cotangent_ref,
    sems,
):
    rows, width = first_ref.shape
    me = scalar_ref[0]
    length = scalar_ref[1]
    part = (mix0_hbm.shape[0] - MASK_ROWS) // 3
    columns = 4 * part
    copies = []
    for k, mix in enumerate((mix0_hbm, mix1_hbm, mix2_hbm, mix3_hbm)):
        place = pl.ds(k * part, part)
        copies.append(
            (
                pltpu.make_async_copy(mix.at[pl.ds(part, part)], down_ref.at[place], sems.at[k]),
                pltpu.make_async_copy(
                    mix.at[pl.ds(2 * part, part)], up_ref.at[place], sems.at[4 + k]
                ),
                pltpu.make_async_copy(
                    mix.at[pl.ds(3 * part, MASK_ROWS)], mask_ref.at[k], sems.at[8 + k]
                ),
            )
        )
    merging_copy = pltpu.make_async_copy(merging_hbm, merging_ref, sems.at[12])
    cotangent_copy = pltpu.make_async_copy(
        cotangent_hbm.at[pl.ds(pl.multiple_of(me * rows, rows), rows)], cotangent_ref, sems.at[13]
    )
    for group in copies:
        group[0].start()
    merging_copy.start()
    for group in copies:
        group[1].start()
        group[2].start()
    cotangent_copy.start()
    adapters = ADAPTERS
    scaling = width ** (-0.5)
    rank = columns // adapters
    held = adapters // 4
    expand = (
        lax.broadcasted_iota(jnp.int32, (adapters, columns), 1) // rank
        == lax.broadcasted_iota(jnp.int32, (adapters, columns), 0)
    ).astype(F32)
    expand = expand.astype(BF16)

    def collect(wide):
        high = wide.astype(BF16)
        rest = (wide - high.astype(F32)).astype(BF16)
        return dot_nt(high, expand) + dot_nt(rest, expand)

    fed = (
        fed_ref[...].astype(F32)
        + fed_beside_ref[...].astype(F32)
        + fed_across_ref[...].astype(F32)
        + bias_ref[...]
    )
    second, unit_second, inverse_second = normalize(
        first_ref[...] + fed, gain_ref[1:2, :], shift_ref[1:2, :]
    )
    second_low = second.astype(BF16)
    for group in copies:
        group[0].wait()
    squeezed, slope = gelu_both(dot_nt(second_low, down_ref[...]))
    squeezed = squeezed.astype(BF16).astype(F32)
    merging_copy.wait()
    fquery = dot(second_low, merging_ref[0]).astype(BF16)
    asked = dot_nt(fquery, merging_ref[1])
    for group in copies:
        group[1].wait()
        group[2].wait()
    cotangent_copy.wait()
    asked_up = dot_nt(asked.astype(BF16), up_ref[...])
    scores = scaling * (
        jnp.sum(asked * second, -1, keepdims=True) + collect(squeezed * asked_up)
    )
    lane = lax.broadcasted_iota(jnp.int32, (1, adapters), 1)
    usable = jnp.zeros((1, adapters), F32)
    for k in range(4):
        usable = jnp.where(lane // held == k, mask_ref[k, 0:1, 0:adapters].astype(F32), usable)
    usable = usable > 0.5
    scores = jnp.where(usable, scores, NEGATIVE)
    highest = jnp.max(scores, -1, keepdims=True)
    weights = jnp.where(usable, jnp.exp(scores - highest), 0.0)
    probs = weights / jnp.sum(weights, -1, keepdims=True)
    total = jnp.sum(probs, -1, keepdims=True)
    probs_wide = split_dot(probs, expand)
    mixed = total * second + dot((probs_wide * squeezed).astype(BF16), up_ref[...])
    mixed_low = mixed.astype(BF16)
    blended = dot(mixed_low, merging_ref[2])
    final, unit_third, inverse_third = normalize(
        second + blended, gain_ref[2:3, :], shift_ref[2:3, :]
    )
    output_ref[...] = final.astype(BF16)
    dthird, gain_third, shift_third = normalize_back(
        cotangent_ref[...].astype(F32), unit_third, inverse_third, gain_ref[2:3, :]
    )
    dthird_low = dthird.astype(BF16)
    pulled = dot_nt(dthird_low, merging_ref[2])
    pulled_up = dot_nt(pulled.astype(BF16), up_ref[...])
    dprobs = jnp.sum(pulled * second, -1, keepdims=True) + collect(squeezed * pulled_up)
    dscores = probs * (dprobs - jnp.sum(probs * dprobs, -1, keepdims=True)) * scaling
    dscores_total = jnp.sum(dscores, -1, keepdims=True)
    dscores_wide = split_dot(dscores, expand)
    weighed = dscores_total * second + dot((dscores_wide * squeezed).astype(BF16), up_ref[...])
    weighed_low = weighed.astype(BF16)
    dquery = dot(weighed_low, merging_ref[1]).astype(BF16)
    dbottle = ((dscores_wide * asked_up + probs_wide * pulled_up) * slope).astype(BF16)
    dsecond = (
        dthird
        + dscores_total * asked
        + total * pulled
        + dot(dbottle, down_ref[...])
        + dot_nt(dquery, merging_ref[0])
    )
    dmid, gain_second, shift_second = normalize_back(
        dsecond, unit_second, inverse_second, gain_ref[1:2, :]
    )
    dmid_ref[...] = dmid
    dmid_low_ref[...] = dmid.astype(BF16)
    position = me * rows + lax.broadcasted_iota(jnp.int32, (rows, 1), 0)
    mass = jnp.sum(jnp.where(position < length, probs, 0.0), 0, keepdims=True)
    source = lax.broadcasted_iota(jnp.int32, (adapters, width), 0)
    target = lax.broadcasted_iota(jnp.int32, (adapters, width), 1)
    move = ((source // held) ^ me) * held + source % held == target
    mass = lax.dot_general(
        jnp.broadcast_to(mass, (8, adapters)),
        move.astype(F32),
        (((1,), (0,)), ((), ())),
        precision=lax.Precision.HIGHEST,
        preferred_element_type=F32,
    )[0:1, :]
    counted = lax.broadcasted_iota(jnp.int32, (1, width), 1) == adapters
    small_ref[0:1, :] = gain_second[None, :]
    small_ref[1:2, :] = gain_third[None, :]
    small_ref[2:3, :] = shift_second[None, :]
    small_ref[3:4, :] = shift_third[None, :]
    small_ref[4:5, :] = jnp.sum(dmid, 0, keepdims=True)
    small_ref[5:6, :] = jnp.where(counted, 0.25 * length.astype(F32), mass)
    small_ref[6:8, :] = jnp.zeros((2, width), F32)
    core = me & 1
    quarter = width // 4
    for j, (left, right) in enumerate(
        ((second_low, dquery), (weighed_low, fquery), (mixed_low, dthird_low))
    ):
        grad = dot_tn(left, right).astype(BF16)
        for k in range(4):
            piece = 4 * j + k
            owner, place = piece // 3 % 2, piece // 6 * 3 + piece % 3
            value = grad[k * quarter : (k + 1) * quarter, :]

            @pl.when(core == owner)
            def _():
                kept_ref[place * quarter : (place + 1) * quarter, :] = value

            @pl.when(core != owner)
            def _():
                sent_ref[place * quarter : (place + 1) * quarter, :] = value


def merge(scalars, first, fed, near, far, bias, gains, shifts, cotangent, mixes, merging):
    rows, width = first.shape
    part = (mixes[0].shape[0] - MASK_ROWS) // 3
    grads = jax.ShapeDtypeStruct((3 * width // 2, width), BF16)
    out_shape = [
        jax.ShapeDtypeStruct((rows, width), BF16),
        jax.ShapeDtypeStruct((rows, width), F32),
        jax.ShapeDtypeStruct((rows, width), BF16),
        grads,
        grads,
        jax.ShapeDtypeStruct((8, width), F32),
    ]
    return pl.pallas_call(
        merge_kernel,
        grid=(1,),
        in_specs=[pl.BlockSpec(memory_space=pltpu.SMEM)]
        + [fixed(array.shape, 0, 0) for array in (first, fed, near, far, bias, gains, shifts)]
        + whole_hbm(6),
        out_specs=[fixed(array.shape, 0, 0) for array in out_shape],
        out_shape=out_shape,
        scratch_shapes=[
            VMEM((4 * part, width), BF16),
            VMEM((4 * part, width), BF16),
            VMEM((4, MASK_ROWS, width), BF16),
            VMEM(merging.shape, BF16),
            VMEM((rows, width), BF16),
            pltpu.SemaphoreType.DMA((14,)),
        ],
        compiler_params=params(),
        cost_estimate=pl.CostEstimate(flops=6000000000, bytes_accessed=14000000, transcendentals=0),
        name="merge",
    )(scalars, first, fed, near, far, bias, gains, shifts, cotangent, *mixes, merging)


def on_device(
    tokens,
    cotangent,
    attn_qkv,
    attn_out,
    ffn_in,
    ffn_bias_in,
    ffn_out,
    ffn_bias_out,
    norm_gains,
    norm_shifts,
    adapter_down,
    adapter_up,
    merging_proj,
    adapter_mask,
    lengths,
):
    me = lax.axis_index("ad")
    tok = lax.axis_size("tok")
    over_tok = tok_plan(tok)
    row_count, width = tokens.shape
    block = row_count // 4
    scalars = jnp.stack([me.astype(jnp.int32), lengths[0]])
    attn_qkv = attn_qkv.swapaxes(1, 2)

    mask = jnp.tile(adapter_mask.astype(BF16), (MASK_ROWS, width // adapter_mask.shape[1]))
    mix = jnp.concatenate([attn_out, adapter_down.T, adapter_up.reshape(-1, width), mask], 0)
    mix_far = across(mix)

    context, weights, inverses, query, key, value, tokens = attend(scalars, tokens, attn_qkv)
    contexts = gather_xor(context)
    mix_far = after(mix_far, context)
    mixes = [mix, beside(mix), mix_far, beside(mix_far)]
    shared_weights = (mixes, ffn_in, ffn_bias_in[None, :], ffn_out, norm_gains, norm_shifts)
    far_first, far_inner, far_slope, fed2, fed3 = feed(1, tokens, contexts, *shared_weights)
    fed_sum = add_low(fed2, beside(fed3))
    contexts[0] = after(context, fed_sum)
    near_first, near_inner, near_slope, fed0, fed1, first, inverse = feed(
        0, tokens, contexts, *shared_weights
    )
    fed_far, fed0, fed1 = lax.optimization_barrier((across(fed_sum), fed0, fed1))
    output_block, dmid, dmid_low, kept, sent, small = merge(
        scalars,
        first,
        fed0,
        beside(fed1),
        fed_far,
        ffn_bias_out[None, :],
        norm_gains,
        norm_shifts,
        cotangent,
        mixes,
        merging_proj,
    )

    dmids = [dmid_low, beside(dmid_low), across(dmid_low)]
    received = beside(sent)
    near_dinner, part0, part1, near_sum = feed_back(
        dmids[0], dmids[1], near_slope, ffn_out, ffn_in
    )
    merging = add_low(after(kept, part0), received)
    bits = len(over_tok)
    merging = merging.reshape((2,) * (bits + 1) + (-1, width))
    places = [(over_tok[k], bits - k) for k in range(bits)]
    down_y = [(("ad", 4, 1), 0)]
    swapped = [(over_tok[1], bits - 1), (over_tok[0], bits - 1)]
    merging = [
        Chain(merging[..., : width // 2], places[:2]),
        Chain(merging[..., width // 2 :], swapped),
    ]
    dmids[2] = after(dmids[2], part0, *[chain.prepare() for chain in merging])
    dmids.append(beside(dmids[2]))
    far_dinner, part2, part3, far_sum = feed_back(dmids[2], dmids[3], far_slope, ffn_out, ffn_in)
    part_beside = beside(part1)
    part_sum = add_low(part2, beside(part3))
    part_far = across(part_sum)
    grad_out, grad_in = feed_grads(
        (after(near_inner, part_sum), far_inner),
        (near_first, far_first),
        dmids,
        near_dinner,
        far_dinner,
    )
    part_far, part_beside, grad_out, grad_in = advance(
        merging, part_far, part_beside, grad_out, grad_in
    )
    grad_out = tok_chain(grad_out, over_tok)
    grad_in = tok_chain(grad_in, over_tok)
    part_far = after(part_far, grad_in.prepare())

    dlow, dcontext0, dcontext1, dcontext23, grad02, grad13, sums = low(
        part0,
        part_beside,
        part_far,
        dmid,
        first,
        inverse,
        norm_gains,
        norm_shifts,
        contexts,
        mixes,
        small,
        near_sum,
        far_sum,
    )
    dcontext_far = across(dcontext23)
    dcontext = jnp.concatenate(
        [dcontext0, beside(dcontext1), dcontext_far[0], beside(dcontext_far[1])], 0
    )
    grad02 = add_low(grad02, beside(grad13))
    columns = context.shape[1]
    dcontext, grad02, grad_out.array = advance(
        merging + [grad_in], dcontext, grad02, grad_out.array
    )
    merging = Chain(
        jnp.concatenate([chain.array for chain in merging], -1), places[2:] + down_y
    )

    grad_attn_far = across(grad02[columns:])
    late, dtokens0, dtokens2, dtokens13 = attend_back(
        query,
        key,
        value,
        weights,
        context,
        inverses,
        dcontext,
        tokens,
        attn_qkv,
    )
    shared = sums[:8]
    late, grad_attn_far, received = advance(
        [merging, grad_in, grad_out], late, grad_attn_far, beside(shared)
    )
    shared = shared + received
    late = jnp.concatenate([late, add_low(grad02[:columns], grad_attn_far)], 0)
    late = tok_chain(late, over_tok)
    chains = [late, grad_out, grad_in]
    (received,) = advance([merging] + chains, beside(dtokens13))
    dtokens = dtokens0.astype(F32) + received[0].astype(F32) + dlow
    dtokens_far = across(add_low(dtokens2, received[1]))
    while merging.steps:
        advance([merging])
    merging = lax.all_gather(merging.array, ("ad", "tok"), axis=0)
    received, dtokens_far = advance(chains, across(shared), dtokens_far)
    sums = jnp.concatenate([shared + received, sums[8:]], 0)
    dtokens = (dtokens + dtokens_far.astype(F32)).astype(BF16)

    def sum_step(k):
        axis, size, bit = over_tok[k]
        return swap(sums, axis, size, 1 << bit)

    received, dtokens_far = advance(chains, sum_step(0), across(dtokens))
    sums = sums + received
    pair = beside(jnp.concatenate([dtokens, dtokens_far], 0))
    received, pair = advance(chains, sum_step(1), pair)
    sums = sums + received
    grad_tokens = place_xor([dtokens, pair[:block], dtokens_far, pair[block:]], me, F32)
    received, output_far = advance(chains, sum_step(2), across(output_block))
    sums = sums + received
    for k in range(3, bits):
        (received,) = advance(chains, sum_step(k))
        sums = sums + received
    while len(late.steps) > 1:
        advance(chains)
    merging = merging.reshape(3, width, width).astype(F32)
    pair = beside(jnp.concatenate([output_block, output_far], 0))
    pair, merging = advance(chains, pair, merging)
    output = place_xor([output_block, pair[:block], output_far, pair[block:]], me, BF16)
    late, grad_out, grad_in = [
        chain.array.reshape(-1, width) for chain in (late, grad_out, grad_in)
    ]

    held = ADAPTERS // 4
    usage = lax.dynamic_slice_in_dim(sums[5], me * held, held) / sums[5, ADAPTERS]
    return (
        output,
        grad_tokens,
        late[: 3 * columns].reshape(3, columns, width).swapaxes(1, 2).astype(F32),
        late[3 * columns :].astype(F32),
        grad_in.astype(F32),
        sums[8],
        grad_out.astype(F32),
        sums[4],
        jnp.stack([sums[6], sums[0], sums[1]]),
        jnp.stack([sums[7], sums[2], sums[3]]),
        merging,
        usage,
    )


def solution(mesh):
    placed = (
        P("tok", None),
        P("tok", None),
        P(None, None, "ad"),
        P("ad", None),
        P(None, "ad"),
        P("ad"),
        P("ad", None),
        P(),
        P(),
        P(),
        P(None, "ad"),
        P("ad", None, None),
        P(),
        P("tok", "ad"),
        P("tok"),
    )
    return jax.shard_map(
        on_device,
        mesh=mesh,
        in_specs=placed,
        out_specs=(
            P("tok", None),
            P("tok", None),
            P(None, None, "ad"),
            P("ad", None),
            P(None, "ad"),
            P("ad"),
            P("ad", None),
            P(),
            P(),
            P(),
            P(),
            P("ad"),
        ),
        check_vma=False,
    )
```

```python
import jax
import jax.numpy as jnp
from jax import lax
from jax.experimental import pallas as pl
from jax.experimental.pallas import tpu as pltpu
from jax.sharding import PartitionSpec as P

HEAD = 64
EPSILON = 1e-06
NEGATIVE = -1e30
ADAPTERS = 16
MASK_ROWS = 16
F32 = jnp.float32
BF16 = jnp.bfloat16


def normalize(values, gain, shift):
    centred = values - jnp.mean(values, -1, keepdims=True)
    inverse = lax.rsqrt(jnp.mean(centred * centred, -1, keepdims=True) + EPSILON)
    unit_rows = centred * inverse
    return (unit_rows * gain + shift, unit_rows, inverse)


def normalize_back(gradient, unit_rows, inverse, gain):
    scaled = gradient * gain
    centred = (
        scaled
        - jnp.mean(scaled, -1, keepdims=True)
        - unit_rows * jnp.mean(scaled * unit_rows, -1, keepdims=True)
    )
    return (centred * inverse, jnp.sum(gradient * unit_rows, 0), jnp.sum(gradient, 0))


def gelu_both(values):
    cdf = 0.5 * (1.0 + lax.erf(values * 0.7071067811865476))
    density = jnp.exp(-0.5 * values * values) * 0.3989422804014327
    return values * cdf, cdf + values * density


def dot(left, right, dims=((1,), (0,))):
    return lax.dot_general(left, right, (dims, ((), ())), preferred_element_type=F32)


def dot_nt(left, right):
    return dot(left, right, ((1,), (1,)))


def dot_tn(left, right):
    return dot(left, right, ((0,), (0,)))


def split_dot(left, right):
    high = left.astype(BF16)
    rest = (left - high.astype(F32)).astype(BF16)
    return dot(high, right) + dot(rest, right)


def after(array, *others):
    return lax.optimization_barrier((array, *others))[0]


def swap(array, axis, size, step):
    return lax.ppermute(array, axis, [(i, i ^ step) for i in range(size)])


def beside(array):
    return swap(array, "ad", 4, 1)


def across(array):
    return swap(array, "ad", 4, 2)


def gather_xor(block):
    far = across(block)
    return [block, beside(block), far, beside(far)]


def tok_plan(size):
    return [("tok", size, bit) for bit in range(size.bit_length() - 1)]


def side_of(step):
    axis, _, bit = step
    return (lax.axis_index(axis) >> bit) & 1


def halve_start(array, step):
    axis, size, bit = step
    side = side_of(step)
    rows = array.shape[0] // 2
    sent = lax.dynamic_slice_in_dim(array, (1 - side) * rows, rows)
    kept = lax.dynamic_slice_in_dim(array, side * rows, rows)
    return kept, swap(sent, axis, size, 1 << bit)


def add_low(kept, received):
    return (kept.astype(F32) + received.astype(F32)).astype(BF16)


def halve(array, plan):
    for step in plan:
        array = add_low(*halve_start(array, step))
    return array


def double(array, plan):
    for step in reversed(plan):
        axis, size, bit = step
        side = side_of(step) == 1
        other = swap(array, axis, size, 1 << bit)
        array = jnp.concatenate(
            [jnp.where(side, other, array), jnp.where(side, array, other)], 0
        )
    return array


class Chain:
    def __init__(self, array, halving, doubling=()):
        self.array = array
        self.steps = [(True, *step) for step in halving] + [(False, *step) for step in doubling]
        self.parts = None

    def prepare(self):
        halves, step, place = self.steps[0]
        self.parts = (self.array, self.array)
        if halves:
            side = side_of(step)
            self.parts = tuple(
                lax.dynamic_index_in_dim(self.array, part, place, keepdims=False)
                for part in (side, 1 - side)
            )
        return self.parts

    def start(self):
        _, (axis, size, bit), _ = self.steps[0]
        kept, sent = self.parts or self.prepare()
        self.parts = None
        return kept, swap(sent, axis, size, 1 << bit)

    def finish(self, own, received):
        halves, step, place = self.steps.pop(0)
        if halves:
            self.array = add_low(own, received)
        else:
            side = side_of(step) == 1
            self.array = jnp.stack(
                [jnp.where(side, received, own), jnp.where(side, own, received)], place
            )


def tok_chain(array, over_tok):
    bits = len(over_tok)
    steps = [(step, 0) for step in over_tok]
    return Chain(array.reshape((2,) * bits + (-1, array.shape[1])), steps, steps[::-1])


def advance(chains, *others):
    chains = [chain for chain in chains if chain.steps]
    flights = [chain.start() for chain in chains]
    flights, others = lax.optimization_barrier((flights, others))
    for chain, flight in zip(chains, flights):
        chain.finish(*flight)
    return others


def place_xor(blocks, me, dtype):
    rows = blocks[0].shape[0]
    whole = jnp.zeros((4 * rows,) + blocks[0].shape[1:], dtype)
    for k, block in enumerate(blocks):
        whole = lax.dynamic_update_slice_in_dim(whole, block.astype(dtype), (me ^ k) * rows, 0)
    return whole


def to_xor(blocks, me):
    return [lax.dynamic_index_in_dim(blocks, me ^ k, 0, keepdims=False) for k in range(4)]


VMEM = pltpu.VMEM


def whole_hbm(count):
    return [pl.BlockSpec(memory_space=pl.ANY)] * count


def fixed(shape, *index):
    return pl.BlockSpec(shape, lambda *_: index)


def params(limit=32):
    return pltpu.CompilerParams(vmem_limit_bytes=limit * 1024 * 1024)


def attend_rows(query, key_ref, value_ref, bias, context_ref, weight_ref, inverse_ref):
    lane = lax.broadcasted_iota(jnp.int32, inverse_ref.shape, 1)
    inverses = jnp.zeros(inverse_ref.shape, F32)
    for head in range(query.shape[1] // HEAD):
        lanes = slice(head * HEAD, (head + 1) * HEAD)
        logits = dot_nt(query[:, lanes], key_ref[:, lanes]) + bias
        expon = jnp.exp(logits - jnp.max(logits, -1, keepdims=True)).astype(BF16)
        weight_ref[head] = expon
        inverse = 1.0 / jnp.sum(expon.astype(F32), -1, keepdims=True)
        inverses = jnp.where(lane == head, inverse, inverses)
        context_ref[:, lanes] = (dot(expon, value_ref[:, lanes]) * inverse).astype(BF16)
    inverse_ref[...] = inverses


def key_bias(scalar_ref, rows):
    block = rows // 4
    column = lax.broadcasted_iota(jnp.int32, (1, rows), 1)
    position = ((column // block) ^ scalar_ref[0]) * block + column % block
    return jnp.where(position < scalar_ref[1], 0.0, NEGATIVE).astype(F32)


def attend_kernel(
    scalar_ref,
    tokens_hbm,
    qkv_ref,
    context_ref,
    weight_ref,
    inverse_ref,
    query_ref,
    key_ref,
    value_ref,
    placed_hbm,
    tokens_ref,
    sems,
):
    step = pl.program_id(0)
    rows = tokens_ref.shape[0]
    block = rows // 4
    loads = []
    for k in range(4):
        source = pl.multiple_of((scalar_ref[0] ^ k) * block, block)
        loads.append(
            pltpu.make_async_copy(
                tokens_hbm.at[pl.ds(source, block)],
                tokens_ref.at[pl.ds(k * block, block)],
                sems.at[k],
            )
        )
    placing = pltpu.make_async_copy(tokens_ref, placed_hbm, sems.at[4])

    @pl.when(step == 0)
    def _():
        for load in loads:
            load.start()
        for load in loads:
            load.wait()
        placing.start()
        placed = tokens_ref[...]
        query_ref[...] = (dot_nt(placed, qkv_ref[0]).astype(BF16) * HEAD ** (-0.5)).astype(BF16)
        key_ref[...] = dot_nt(placed, qkv_ref[1]).astype(BF16)
        value_ref[...] = dot_nt(placed, qkv_ref[2]).astype(BF16)

    bias = key_bias(scalar_ref, rows)
    query = query_ref[pl.ds(pl.multiple_of(step * block, block), block), :]
    attend_rows(query, key_ref, value_ref, bias, context_ref, weight_ref, inverse_ref)

    @pl.when(step == pl.num_programs(0) - 1)
    def _():
        placing.wait()


def attend(scalars, tokens, attn_qkv):
    rows, width = tokens.shape
    columns = attn_qkv.shape[1]
    heads = columns // HEAD
    block = rows // 4
    projected = jax.ShapeDtypeStruct((rows, columns), BF16)
    return pl.pallas_call(
        attend_kernel,
        grid=(4,),
        in_specs=[
            pl.BlockSpec(memory_space=pltpu.SMEM),
            pl.BlockSpec(memory_space=pl.ANY),
            fixed(attn_qkv.shape, 0, 0, 0),
        ],
        out_specs=[
            pl.BlockSpec((block, columns), lambda i: (i, 0)),
            pl.BlockSpec((heads, block, rows), lambda i: (0, i, 0)),
            pl.BlockSpec((block, 128), lambda i: (i, 0)),
        ]
        + [fixed((rows, columns), 0, 0)] * 3
        + [pl.BlockSpec(memory_space=pl.ANY)],
        out_shape=[
            jax.ShapeDtypeStruct((rows, columns), BF16),
            jax.ShapeDtypeStruct((heads, rows, rows), BF16),
            jax.ShapeDtypeStruct((rows, 128), F32),
        ]
        + [projected] * 3
        + [jax.ShapeDtypeStruct((rows, width), BF16)],
        scratch_shapes=[VMEM((rows, width), BF16), pltpu.SemaphoreType.DMA((5,))],
        compiler_params=params(),
        cost_estimate=pl.CostEstimate(flops=5000000000, bytes_accessed=14000000, transcendentals=0),
        name="attend",
    )(scalars, tokens, attn_qkv)


def attend_back_kernel(
    query_ref,
    key_ref,
    value_ref,
    context_ref,
    inverse_ref,
    dcontext_ref,
    weight_ref,
    tokens_hbm,
    qkv_hbm,
    late_ref,
    part0_ref,
    part2_ref,
    part13_ref,
    dquery,
    dkey,
    dvalue,
    tokens_ref,
    qkv_ref,
    sems,
):
    step = pl.program_id(0)
    block = query_ref.shape[0]
    columns = query_ref.shape[1]
    loads = (
        pltpu.make_async_copy(tokens_hbm, tokens_ref, sems.at[0]),
        pltpu.make_async_copy(qkv_hbm, qkv_ref, sems.at[1]),
    )

    @pl.when(step == 0)
    def _():
        for load in loads:
            load.start()
        dkey[...] = jnp.zeros_like(dkey)
        dvalue[...] = jnp.zeros_like(dvalue)

    scaling = HEAD ** (-0.5)
    rows = pl.ds(pl.multiple_of(step * block, block), block)
    for head in range(columns // HEAD):
        lanes = slice(head * HEAD, (head + 1) * HEAD)
        weights = weight_ref[head]
        scaled = dcontext_ref[:, lanes].astype(F32) * inverse_ref[:, head : head + 1]
        delta = jnp.sum(scaled * context_ref[:, lanes].astype(F32), -1, keepdims=True)
        dcontext = scaled.astype(BF16)
        dweights = dot_nt(dcontext, value_ref[:, lanes])
        dlogits = (weights.astype(F32) * (dweights - delta)).astype(BF16)
        dquery[rows, lanes] = (dot(dlogits, key_ref[:, lanes]) * scaling).astype(BF16)
        dkey[lanes, :] += dot_tn(query_ref[:, lanes], dlogits)
        dvalue[lanes, :] += dot_tn(dcontext, weights)

    @pl.when(step == pl.num_programs(0) - 1)
    def _():
        for load in loads:
            load.wait()
        dkey_low = dkey[...].astype(BF16)
        dvalue_low = dvalue[...].astype(BF16)
        tokens = tokens_ref[...]
        late_ref[0:columns, :] = dot_tn(dquery[...], tokens).astype(BF16)
        late_ref[columns : 2 * columns, :] = dot(dkey_low, tokens).astype(BF16)
        late_ref[2 * columns :, :] = dot(dvalue_low, tokens).astype(BF16)
        part_refs = (part0_ref, part13_ref.at[0], part2_ref, part13_ref.at[1])
        for k, part_ref in enumerate(part_refs):
            part = slice(k * block, (k + 1) * block)
            dtokens = (
                dot(dquery[part, :], qkv_ref[0])
                + dot_tn(dkey_low[:, part], qkv_ref[1])
                + dot_tn(dvalue_low[:, part], qkv_ref[2])
            )
            part_ref[...] = dtokens.astype(BF16)


def attend_back(query, key, value, weights, context, inverses, dcontext, tokens, attn_qkv):
    rows, columns = query.shape
    heads = columns // HEAD
    width = tokens.shape[1]
    block = rows // 4
    part = jax.ShapeDtypeStruct((block, width), BF16)
    return pl.pallas_call(
        attend_back_kernel,
        grid=(4,),
        in_specs=[
            pl.BlockSpec((block, columns), lambda i: (i, 0)),
            fixed((rows, columns), 0, 0),
            fixed((rows, columns), 0, 0),
            pl.BlockSpec((block, columns), lambda i: (i, 0)),
            pl.BlockSpec((block, 128), lambda i: (i, 0)),
            pl.BlockSpec((block, columns), lambda i: (i, 0)),
            pl.BlockSpec((heads, block, rows), lambda i: (0, i, 0)),
        ]
        + whole_hbm(2),
        out_specs=[fixed((3 * columns, width), 0, 0)]
        + [fixed((block, width), 0, 0)] * 2
        + [fixed((2, block, width), 0, 0, 0)],
        out_shape=[
            jax.ShapeDtypeStruct((3 * columns, width), BF16),
            part,
            part,
            jax.ShapeDtypeStruct((2, block, width), BF16),
        ],
        scratch_shapes=[
            VMEM((rows, columns), BF16),
            VMEM((columns, rows), F32),
            VMEM((columns, rows), F32),
            VMEM(tokens.shape, BF16),
            VMEM(attn_qkv.shape, BF16),
            pltpu.SemaphoreType.DMA((2,)),
        ],
        compiler_params=params(),
        cost_estimate=pl.CostEstimate(flops=6000000000, bytes_accessed=14000000, transcendentals=0),
        name="attend_back",
    )(query, key, value, context, inverses, dcontext, weights, tokens, attn_qkv)


def feed_kernel(
    tokens_ref,
    context0_ref,
    context1_ref,
    context2_ref,
    context3_ref,
    bias_ref,
    gain_ref,
    shift_ref,
    mix0_hbm,
    mix1_hbm,
    mix2_hbm,
    mix3_hbm,
    in_hbm,
    out_hbm,
    first_low_ref,
    inner_ref,
    slope_ref,
    near_ref,
    far_ref,
    *refs,
):
    own_refs, (mix_ref, in_ref, out_ref, sems) = refs[:-4], refs[-4:]
    step = pl.program_id(0)
    columns = context0_ref.shape[1]
    loads = []
    for k, mix in enumerate((mix0_hbm, mix1_hbm, mix2_hbm, mix3_hbm)):
        loads.append(
            pltpu.make_async_copy(mix.at[pl.ds(0, columns)], mix_ref.at[k], sems.at[k])
        )
    loads.append(pltpu.make_async_copy(in_hbm, in_ref, sems.at[4]))
    loads.append(pltpu.make_async_copy(out_hbm, out_ref, sems.at[5]))

    @pl.when(step == 0)
    def _():
        for load in loads:
            load.start()
        for load in loads[:4]:
            load.wait()

    attended = (
        dot(context0_ref[...], mix_ref[0])
        + dot(context1_ref[...], mix_ref[1])
        + dot(context2_ref[...], mix_ref[2])
        + dot(context3_ref[...], mix_ref[3])
    )
    first, _, inverse = normalize(
        tokens_ref[...].astype(F32) + attended, gain_ref[0:1, :], shift_ref[0:1, :]
    )
    if own_refs:

        @pl.when(step == 0)
        def _():
            own_refs[0][...] = first
            own_refs[1][...] = inverse

    @pl.when(step == 0)
    def _():
        for load in loads[4:]:
            load.wait()

    first_low = first.astype(BF16)
    first_low_ref[...] = first_low
    inner, slope = gelu_both(dot(first_low, in_ref[...]) + bias_ref[...])
    inner = inner.astype(BF16)
    inner_ref[...] = inner
    slope_ref[...] = slope.astype(BF16)
    fed = dot(inner, out_ref[...]).astype(BF16)

    @pl.when(step == 0)
    def _():
        near_ref[...] = fed

    @pl.when(step == 1)
    def _():
        far_ref[...] = fed


def feed(half, tokens, contexts, mixes, ffn_in, bias, ffn_out, gains, shifts):
    rows, width = tokens.shape
    block = rows // 4
    columns = contexts[0].shape[1]
    hidden = ffn_in.shape[1]
    row_block = pl.BlockSpec((block, width), lambda i: (i, 0))
    hidden_block = pl.BlockSpec((block, hidden), lambda i: (i, 0))
    in_specs = [pl.BlockSpec((block, width), lambda i: (i + 2 * half, 0))]
    for k in range(4):
        in_specs.append(pl.BlockSpec((block, columns), lambda i, k=k: ((i + 2 * half) ^ k, 0)))
    in_specs += [fixed(array.shape, 0, 0) for array in (bias, gains, shifts)] + whole_hbm(6)
    out_specs = [row_block, hidden_block, hidden_block] + [fixed((block, width), 0, 0)] * 2
    out_shape = [
        jax.ShapeDtypeStruct((2 * block, width), BF16),
        jax.ShapeDtypeStruct((2 * block, hidden), BF16),
        jax.ShapeDtypeStruct((2 * block, hidden), BF16),
        jax.ShapeDtypeStruct((block, width), BF16),
        jax.ShapeDtypeStruct((block, width), BF16),
    ]
    if half == 0:
        out_specs += [fixed((block, width), 0, 0), fixed((block, 1), 0, 0)]
        out_shape += [
            jax.ShapeDtypeStruct((block, width), F32),
            jax.ShapeDtypeStruct((block, 1), F32),
        ]
    return pl.pallas_call(
        feed_kernel,
        grid=(2,),
        in_specs=in_specs,
        out_specs=out_specs,
        out_shape=out_shape,
        scratch_shapes=[
            VMEM((4, columns, width), BF16),
            VMEM(ffn_in.shape, BF16),
            VMEM(ffn_out.shape, BF16),
            pltpu.SemaphoreType.DMA((6,)),
        ],
        compiler_params=params(),
        cost_estimate=pl.CostEstimate(flops=3000000000, bytes_accessed=9000000, transcendentals=0),
        name="feed",
    )(tokens, *contexts, bias, gains, shifts, *mixes, ffn_in, ffn_out)


def feed_back_kernel(
    near_ref,
    far_ref,
    slope_ref,
    out_hbm,
    in_hbm,
    dinner_ref,
    near_part_ref,
    far_part_ref,
    sum_ref,
    out_ref,
    in_ref,
    sems,
):
    block = near_ref.shape[0]
    loads = (
        pltpu.make_async_copy(out_hbm, out_ref, sems.at[0]),
        pltpu.make_async_copy(in_hbm, in_ref, sems.at[1]),
    )
    for load in loads:
        load.start()
    for load in loads:
        load.wait()
    total = jnp.zeros((1, slope_ref.shape[1]), F32)
    for k, (dmid_ref, part_ref) in enumerate(
        ((near_ref, near_part_ref), (far_ref, far_part_ref))
    ):
        rows = slice(k * block, (k + 1) * block)
        dinner = (dot_nt(dmid_ref[...], out_ref[...]) * slope_ref[rows, :].astype(F32)).astype(BF16)
        dinner_ref[rows, :] = dinner
        total = total + jnp.sum(dinner.astype(F32), 0, keepdims=True)
        part_ref[...] = dot_nt(dinner, in_ref[...]).astype(BF16)
    sum_ref[0:1, :] = total
    sum_ref[1:8, :] = jnp.zeros((7, slope_ref.shape[1]), F32)


def feed_back(near, far, slope, ffn_out, ffn_in):
    block, width = near.shape
    hidden = slope.shape[1]
    part = jax.ShapeDtypeStruct((block, width), BF16)
    return pl.pallas_call(
        feed_back_kernel,
        grid=(1,),
        in_specs=[
            fixed(near.shape, 0, 0),
            fixed(far.shape, 0, 0),
            fixed((2 * block, hidden), 0, 0),
        ]
        + whole_hbm(2),
        out_specs=[
            fixed((2 * block, hidden), 0, 0),
            fixed(near.shape, 0, 0),
            fixed(far.shape, 0, 0),
            fixed((8, hidden), 0, 0),
        ],
        out_shape=[
            jax.ShapeDtypeStruct((2 * block, hidden), BF16),
            part,
            part,
            jax.ShapeDtypeStruct((8, hidden), F32),
        ],
        scratch_shapes=[
            VMEM(ffn_out.shape, BF16),
            VMEM(ffn_in.shape, BF16),
            pltpu.SemaphoreType.DMA((2,)),
        ],
        compiler_params=params(),
        cost_estimate=pl.CostEstimate(flops=1400000000, bytes_accessed=5000000, transcendentals=0),
        name="feed_back",
    )(near, far, slope, ffn_out, ffn_in)


def feed_grads_kernel(
    near_inner_hbm,
    far_inner_hbm,
    near_first_hbm,
    far_first_hbm,
    dmid0_hbm,
    dmid1_hbm,
    dmid2_hbm,
    dmid3_hbm,
    near_hbm,
    far_hbm,
    out_ref,
    in_ref,
    inner,
    dmid,
    first,
    dinner,
    sems,
):
    loads = [[], []]
    groups = (
        (0, inner, (near_inner_hbm, far_inner_hbm)),
        (0, dmid, (dmid0_hbm, dmid1_hbm, dmid2_hbm, dmid3_hbm)),
        (1, first, (near_first_hbm, far_first_hbm)),
        (1, dinner, (near_hbm, far_hbm)),
    )
    count = 0
    for turn, whole, parts in groups:
        start = 0
        for part in parts:
            rows = part.shape[0]
            loads[turn].append(
                pltpu.make_async_copy(part, whole.at[pl.ds(start, rows)], sems.at[count])
            )
            loads[turn][-1].start()
            start += rows
            count += 1
    for load in loads[0]:
        load.wait()
    out_ref[...] = dot_tn(inner[...], dmid[...]).astype(BF16)
    for load in loads[1]:
        load.wait()
    in_ref[...] = dot_tn(first[...], dinner[...]).astype(BF16)


def feed_grads(inners, firsts, dmids, near, far):
    rows, hidden = inners[0].shape[0] * 2, inners[0].shape[1]
    width = firsts[0].shape[1]
    arrays = (*inners, *firsts, *dmids, near, far)
    return pl.pallas_call(
        feed_grads_kernel,
        in_specs=whole_hbm(len(arrays)),
        out_specs=[pl.BlockSpec(memory_space=VMEM)] * 2,
        out_shape=[
            jax.ShapeDtypeStruct((hidden, width), BF16),
            jax.ShapeDtypeStruct((width, hidden), BF16),
        ],
        scratch_shapes=[
            VMEM((rows, hidden), BF16),
            VMEM((rows, width), BF16),
            VMEM((rows, width), BF16),
            VMEM((rows, hidden), BF16),
            pltpu.SemaphoreType.DMA((len(arrays),)),
        ],
        compiler_params=params(60),
        cost_estimate=pl.CostEstimate(flops=2400000000, bytes_accessed=9000000, transcendentals=0),
        name="feed_grads",
    )(*arrays)


def low_kernel(
    part_ref,
    beside_ref,
    across_ref,
    dmid_ref,
    first_ref,
    inverse_ref,
    gain_ref,
    shift_ref,
    small_ref,
    near_sum_ref,
    far_sum_ref,
    context0_hbm,
    context1_hbm,
    context2_hbm,
    context3_hbm,
    mix0_hbm,
    mix1_hbm,
    mix2_hbm,
    mix3_hbm,
    dlow_ref,
    dcontext0_ref,
    dcontext1_ref,
    dcontext23_ref,
    grad02_ref,
    grad13_ref,
    sums_ref,
    context_ref,
    mix_ref,
    sems,
):
    block = part_ref.shape[0]
    columns = dcontext0_ref.shape[1]
    loads = []
    for k, mix in enumerate((mix0_hbm, mix1_hbm, mix2_hbm, mix3_hbm)):
        loads.append(
            pltpu.make_async_copy(mix.at[pl.ds(0, columns)], mix_ref.at[k], sems.at[k])
        )
    for k, context in enumerate((context0_hbm, context1_hbm, context2_hbm, context3_hbm)):
        rows = pl.ds(k * block, block)
        loads.append(pltpu.make_async_copy(context.at[rows], context_ref.at[k], sems.at[4 + k]))
    for load in loads:
        load.start()
    dfirst = (
        part_ref[...].astype(F32)
        + beside_ref[...].astype(F32)
        + across_ref[...].astype(F32)
        + dmid_ref[...]
    )
    unit = (first_ref[...] - shift_ref[0:1, :]) / gain_ref[0:1, :]
    dlow, gain, shift = normalize_back(dfirst, unit, inverse_ref[...], gain_ref[0:1, :])
    dlow_ref[...] = dlow
    dlow_low = dlow.astype(BF16)
    for load in loads[:4]:
        load.wait()
    dcontext0_ref[...] = dot_nt(dlow_low, mix_ref[0]).astype(BF16)
    dcontext1_ref[...] = dot_nt(dlow_low, mix_ref[1]).astype(BF16)
    dcontext23_ref[0] = dot_nt(dlow_low, mix_ref[2]).astype(BF16)
    dcontext23_ref[1] = dot_nt(dlow_low, mix_ref[3]).astype(BF16)
    for load in loads[4:]:
        load.wait()
    grad02_ref[0:columns, :] = dot_tn(context_ref[0], dlow_low).astype(BF16)
    grad02_ref[columns:, :] = dot_tn(context_ref[2], dlow_low).astype(BF16)
    grad13_ref[0:columns, :] = dot_tn(context_ref[1], dlow_low).astype(BF16)
    grad13_ref[columns:, :] = dot_tn(context_ref[3], dlow_low).astype(BF16)
    sums_ref[0:6, :] = small_ref[0:6, :]
    sums_ref[6:7, :] = gain[None, :]
    sums_ref[7:8, :] = shift[None, :]
    sums_ref[8:16, :] = near_sum_ref[...] + far_sum_ref[...]


def low(
    part,
    near,
    far,
    dmid,
    first,
    inverse,
    gains,
    shifts,
    contexts,
    mixes,
    small,
    near_sum,
    far_sum,
):
    block, width = dmid.shape
    columns = contexts[0].shape[1]
    rows = fixed((block, width), 0, 0)
    in_specs = [rows] * 5
    in_specs += [fixed(array.shape, 0, 0) for array in (inverse, gains, shifts)]
    in_specs += [fixed(small.shape, 0, 0)] + [fixed(near_sum.shape, 0, 0)] * 2
    in_specs += whole_hbm(8)
    out_shape = [
        jax.ShapeDtypeStruct((block, width), F32),
        jax.ShapeDtypeStruct((block, columns), BF16),
        jax.ShapeDtypeStruct((block, columns), BF16),
        jax.ShapeDtypeStruct((2, block, columns), BF16),
        jax.ShapeDtypeStruct((2 * columns, width), BF16),
        jax.ShapeDtypeStruct((2 * columns, width), BF16),
        jax.ShapeDtypeStruct((16, width), F32),
    ]
    return pl.pallas_call(
        low_kernel,
        grid=(1,),
        in_specs=in_specs,
        out_specs=[fixed(out.shape, *([0] * len(out.shape))) for out in out_shape],
        out_shape=out_shape,
        scratch_shapes=[
            VMEM((4, block, columns), BF16),
            VMEM((4, columns, width), BF16),
            pltpu.SemaphoreType.DMA((8,)),
        ],
        compiler_params=params(60),
        cost_estimate=pl.CostEstimate(flops=600000000, bytes_accessed=6000000, transcendentals=0),
        name="low",
    )(
        part,
        near,
        far,
        dmid,
        first,
        inverse,
        gains,
        shifts,
        small,
        near_sum,
        far_sum,
        *contexts,
        *mixes,
    )


def merge_kernel(
    scalar_ref,
    first_ref,
    fed_ref,
    fed_beside_ref,
    fed_across_ref,
    bias_ref,
    gain_ref,
    shift_ref,
    cotangent_hbm,
    mix0_hbm,
    mix1_hbm,
    mix2_hbm,
    mix3_hbm,
    merging_hbm,
    output_ref,
    dmid_ref,
    dmid_low_ref,
    kept_ref,
    sent_ref,
    small_ref,
    down_ref,
    up_ref,
    mask_ref,
    merging_ref,
    cotangent_ref,
    sems,
):
    rows, width = first_ref.shape
    me = scalar_ref[0]
    length = scalar_ref[1]
    part = (mix0_hbm.shape[0] - MASK_ROWS) // 3
    columns = 4 * part
    copies = []
    for k, mix in enumerate((mix0_hbm, mix1_hbm, mix2_hbm, mix3_hbm)):
        place = pl.ds(k * part, part)
        copies.append(
            (
                pltpu.make_async_copy(mix.at[pl.ds(part, part)], down_ref.at[place], sems.at[k]),
                pltpu.make_async_copy(
                    mix.at[pl.ds(2 * part, part)], up_ref.at[place], sems.at[4 + k]
                ),
                pltpu.make_async_copy(
                    mix.at[pl.ds(3 * part, MASK_ROWS)], mask_ref.at[k], sems.at[8 + k]
                ),
            )
        )
    merging_copy = pltpu.make_async_copy(merging_hbm, merging_ref, sems.at[12])
    cotangent_copy = pltpu.make_async_copy(
        cotangent_hbm.at[pl.ds(pl.multiple_of(me * rows, rows), rows)], cotangent_ref, sems.at[13]
    )
    for group in copies:
        group[0].start()
    merging_copy.start()
    for group in copies:
        group[1].start()
        group[2].start()
    cotangent_copy.start()
    adapters = ADAPTERS
    scaling = width ** (-0.5)
    rank = columns // adapters
    held = adapters // 4
    expand = (
        lax.broadcasted_iota(jnp.int32, (adapters, columns), 1) // rank
        == lax.broadcasted_iota(jnp.int32, (adapters, columns), 0)
    ).astype(F32)
    expand = expand.astype(BF16)

    def collect(wide):
        high = wide.astype(BF16)
        rest = (wide - high.astype(F32)).astype(BF16)
        return dot_nt(high, expand) + dot_nt(rest, expand)

    fed = (
        fed_ref[...].astype(F32)
        + fed_beside_ref[...].astype(F32)
        + fed_across_ref[...].astype(F32)
        + bias_ref[...]
    )
    second, unit_second, inverse_second = normalize(
        first_ref[...] + fed, gain_ref[1:2, :], shift_ref[1:2, :]
    )
    second_low = second.astype(BF16)
    for group in copies:
        group[0].wait()
    squeezed, slope = gelu_both(dot_nt(second_low, down_ref[...]))
    squeezed = squeezed.astype(BF16).astype(F32)
    merging_copy.wait()
    fquery = dot(second_low, merging_ref[0]).astype(BF16)
    asked = dot_nt(fquery, merging_ref[1])
    for group in copies:
        group[1].wait()
        group[2].wait()
    cotangent_copy.wait()
    asked_up = dot_nt(asked.astype(BF16), up_ref[...])
    scores = scaling * (
        jnp.sum(asked * second, -1, keepdims=True) + collect(squeezed * asked_up)
    )
    lane = lax.broadcasted_iota(jnp.int32, (1, adapters), 1)
    usable = jnp.zeros((1, adapters), F32)
    for k in range(4):
        usable = jnp.where(lane // held == k, mask_ref[k, 0:1, 0:adapters].astype(F32), usable)
    usable = usable > 0.5
    scores = jnp.where(usable, scores, NEGATIVE)
    highest = jnp.max(scores, -1, keepdims=True)
    weights = jnp.where(usable, jnp.exp(scores - highest), 0.0)
    probs = weights / jnp.sum(weights, -1, keepdims=True)
    total = jnp.sum(probs, -1, keepdims=True)
    probs_wide = split_dot(probs, expand)
    mixed = total * second + dot((probs_wide * squeezed).astype(BF16), up_ref[...])
    mixed_low = mixed.astype(BF16)
    blended = dot(mixed_low, merging_ref[2])
    final, unit_third, inverse_third = normalize(
        second + blended, gain_ref[2:3, :], shift_ref[2:3, :]
    )
    output_ref[...] = final.astype(BF16)
    dthird, gain_third, shift_third = normalize_back(
        cotangent_ref[...].astype(F32), unit_third, inverse_third, gain_ref[2:3, :]
    )
    dthird_low = dthird.astype(BF16)
    pulled = dot_nt(dthird_low, merging_ref[2])
    pulled_up = dot_nt(pulled.astype(BF16), up_ref[...])
    dprobs = jnp.sum(pulled * second, -1, keepdims=True) + collect(squeezed * pulled_up)
    dscores = probs * (dprobs - jnp.sum(probs * dprobs, -1, keepdims=True)) * scaling
    dscores_total = jnp.sum(dscores, -1, keepdims=True)
    dscores_wide = split_dot(dscores, expand)
    weighed = dscores_total * second + dot((dscores_wide * squeezed).astype(BF16), up_ref[...])
    weighed_low = weighed.astype(BF16)
    dquery = dot(weighed_low, merging_ref[1]).astype(BF16)
    dbottle = ((dscores_wide * asked_up + probs_wide * pulled_up) * slope).astype(BF16)
    dsecond = (
        dthird
        + dscores_total * asked
        + total * pulled
        + dot(dbottle, down_ref[...])
        + dot_nt(dquery, merging_ref[0])
    )
    dmid, gain_second, shift_second = normalize_back(
        dsecond, unit_second, inverse_second, gain_ref[1:2, :]
    )
    dmid_ref[...] = dmid
    dmid_low_ref[...] = dmid.astype(BF16)
    position = me * rows + lax.broadcasted_iota(jnp.int32, (rows, 1), 0)
    mass = jnp.sum(jnp.where(position < length, probs, 0.0), 0, keepdims=True)
    source = lax.broadcasted_iota(jnp.int32, (adapters, width), 0)
    target = lax.broadcasted_iota(jnp.int32, (adapters, width), 1)
    move = ((source // held) ^ me) * held + source % held == target
    mass = lax.dot_general(
        jnp.broadcast_to(mass, (8, adapters)),
        move.astype(F32),
        (((1,), (0,)), ((), ())),
        precision=lax.Precision.HIGHEST,
        preferred_element_type=F32,
    )[0:1, :]
    counted = lax.broadcasted_iota(jnp.int32, (1, width), 1) == adapters
    small_ref[0:1, :] = gain_second[None, :]
    small_ref[1:2, :] = gain_third[None, :]
    small_ref[2:3, :] = shift_second[None, :]
    small_ref[3:4, :] = shift_third[None, :]
    small_ref[4:5, :] = jnp.sum(dmid, 0, keepdims=True)
    small_ref[5:6, :] = jnp.where(counted, 0.25 * length.astype(F32), mass)
    small_ref[6:8, :] = jnp.zeros((2, width), F32)
    core = me & 1
    quarter = width // 4
    for j, (left, right) in enumerate(
        ((second_low, dquery), (weighed_low, fquery), (mixed_low, dthird_low))
    ):
        grad = dot_tn(left, right).astype(BF16)
        for k in range(4):
            piece = 4 * j + k
            owner, place = piece // 3 % 2, piece // 6 * 3 + piece % 3
            value = grad[k * quarter : (k + 1) * quarter, :]

            @pl.when(core == owner)
            def _():
                kept_ref[place * quarter : (place + 1) * quarter, :] = value

            @pl.when(core != owner)
            def _():
                sent_ref[place * quarter : (place + 1) * quarter, :] = value


def merge(scalars, first, fed, near, far, bias, gains, shifts, cotangent, mixes, merging):
    rows, width = first.shape
    part = (mixes[0].shape[0] - MASK_ROWS) // 3
    grads = jax.ShapeDtypeStruct((3 * width // 2, width), BF16)
    out_shape = [
        jax.ShapeDtypeStruct((rows, width), BF16),
        jax.ShapeDtypeStruct((rows, width), F32),
        jax.ShapeDtypeStruct((rows, width), BF16),
        grads,
        grads,
        jax.ShapeDtypeStruct((8, width), F32),
    ]
    return pl.pallas_call(
        merge_kernel,
        grid=(1,),
        in_specs=[pl.BlockSpec(memory_space=pltpu.SMEM)]
        + [fixed(array.shape, 0, 0) for array in (first, fed, near, far, bias, gains, shifts)]
        + whole_hbm(6),
        out_specs=[fixed(array.shape, 0, 0) for array in out_shape],
        out_shape=out_shape,
        scratch_shapes=[
            VMEM((4 * part, width), BF16),
            VMEM((4 * part, width), BF16),
            VMEM((4, MASK_ROWS, width), BF16),
            VMEM(merging.shape, BF16),
            VMEM((rows, width), BF16),
            pltpu.SemaphoreType.DMA((14,)),
        ],
        compiler_params=params(),
        cost_estimate=pl.CostEstimate(flops=6000000000, bytes_accessed=14000000, transcendentals=0),
        name="merge",
    )(scalars, first, fed, near, far, bias, gains, shifts, cotangent, *mixes, merging)


def on_device(
    tokens,
    cotangent,
    attn_qkv,
    attn_out,
    ffn_in,
    ffn_bias_in,
    ffn_out,
    ffn_bias_out,
    norm_gains,
    norm_shifts,
    adapter_down,
    adapter_up,
    merging_proj,
    adapter_mask,
    lengths,
):
    me = lax.axis_index("ad")
    tok = lax.axis_size("tok")
    over_tok = tok_plan(tok)
    row_count, width = tokens.shape
    block = row_count // 4
    scalars = jnp.stack([me.astype(jnp.int32), lengths[0]])
    attn_qkv = attn_qkv.swapaxes(1, 2)

    mask = jnp.tile(adapter_mask.astype(BF16), (MASK_ROWS, width // adapter_mask.shape[1]))
    mix = jnp.concatenate([attn_out, adapter_down.T, adapter_up.reshape(-1, width), mask], 0)
    mix_far = across(mix)

    context, weights, inverses, query, key, value, tokens = attend(scalars, tokens, attn_qkv)
    contexts = gather_xor(context)
    mix_far = after(mix_far, context)
    mixes = [mix, beside(mix), mix_far, beside(mix_far)]
    shared_weights = (mixes, ffn_in, ffn_bias_in[None, :], ffn_out, norm_gains, norm_shifts)
    far_first, far_inner, far_slope, fed2, fed3 = feed(1, tokens, contexts, *shared_weights)
    fed_sum = add_low(fed2, beside(fed3))
    contexts[0] = after(context, fed_sum)
    near_first, near_inner, near_slope, fed0, fed1, first, inverse = feed(
        0, tokens, contexts, *shared_weights
    )
    fed_far, fed0, fed1 = lax.optimization_barrier((across(fed_sum), fed0, fed1))
    output_block, dmid, dmid_low, kept, sent, small = merge(
        scalars,
        first,
        fed0,
        beside(fed1),
        fed_far,
        ffn_bias_out[None, :],
        norm_gains,
        norm_shifts,
        cotangent,
        mixes,
        merging_proj,
    )

    dmids = [dmid_low, beside(dmid_low), across(dmid_low)]
    received = beside(sent)
    near_dinner, part0, part1, near_sum = feed_back(
        dmids[0], dmids[1], near_slope, ffn_out, ffn_in
    )
    merging = add_low(after(kept, part0), received)
    bits = len(over_tok)
    merging = merging.reshape((2,) * (bits + 1) + (-1, width))
    places = [(over_tok[k], bits - k) for k in range(bits)]
    down_y = [(("ad", 4, 1), 0)]
    swapped = [(over_tok[1], bits - 1), (over_tok[0], bits - 1)]
    merging = [
        Chain(merging[..., : width // 2], places[:2]),
        Chain(merging[..., width // 2 :], swapped),
    ]
    dmids[2] = after(dmids[2], part0, *[chain.prepare() for chain in merging])
    dmids.append(beside(dmids[2]))
    far_dinner, part2, part3, far_sum = feed_back(dmids[2], dmids[3], far_slope, ffn_out, ffn_in)
    part_beside = beside(part1)
    part_sum = add_low(part2, beside(part3))
    part_far = across(part_sum)
    for chain in merging:
        chain.parts = (chain.parts[0], after(chain.parts[1], part_sum))
    grad_out, grad_in = feed_grads(
        (after(near_inner, part_sum), far_inner),
        (near_first, far_first),
        dmids,
        near_dinner,
        far_dinner,
    )
    grad_out = tok_chain(grad_out, over_tok)
    grad_in = tok_chain(grad_in, over_tok)
    part_far, part_beside, grad_out.array, grad_in.parts = advance(
        merging, part_far, part_beside, grad_out.array, grad_in.prepare()
    )
    part_far = after(part_far, grad_in.parts)

    dlow, dcontext0, dcontext1, dcontext23, grad02, grad13, sums = low(
        part0,
        part_beside,
        part_far,
        dmid,
        first,
        inverse,
        norm_gains,
        norm_shifts,
        contexts,
        mixes,
        small,
        near_sum,
        far_sum,
    )
    dcontext_far = across(dcontext23)
    pair = beside(jnp.stack([dcontext1, dcontext_far[1]]))
    dcontext = jnp.concatenate([dcontext0, pair[0], dcontext_far[0], pair[1]], 0)
    grad02 = add_low(grad02, beside(grad13))
    columns = context.shape[1]
    dcontext, grad02, grad_out.array = advance(
        merging + [grad_in], dcontext, grad02, grad_out.array
    )
    merging = Chain(
        jnp.concatenate([chain.array for chain in merging], -1), places[2:] + down_y
    )

    grad_attn_far = across(grad02[columns:])
    late, dtokens0, dtokens2, dtokens13 = attend_back(
        query,
        key,
        value,
        weights,
        context,
        inverses,
        dcontext,
        tokens,
        attn_qkv,
    )
    shared = sums[:8]
    late, grad_attn_far, received = advance(
        [merging, grad_in, grad_out], late, grad_attn_far, beside(shared)
    )
    shared = shared + received
    late = jnp.concatenate([late, add_low(grad02[:columns], grad_attn_far)], 0)
    late = tok_chain(late, over_tok)
    chains = [late, grad_out, grad_in]
    (received,) = advance([merging] + chains, beside(dtokens13))
    dtokens = dtokens0.astype(F32) + received[0].astype(F32) + dlow
    dtokens_far = across(add_low(dtokens2, received[1]))
    while merging.steps:
        advance([merging])
    merging = lax.all_gather(merging.array, ("ad", "tok"), axis=0)
    received, dtokens_far = advance(chains, across(shared), dtokens_far)
    sums = jnp.concatenate([shared + received, sums[8:]], 0)
    dtokens = (dtokens + dtokens_far.astype(F32)).astype(BF16)

    def sum_step(k):
        axis, size, bit = over_tok[k]
        return swap(sums, axis, size, 1 << bit)

    received, dtokens_far = advance(chains, sum_step(0), across(dtokens))
    sums = sums + received
    pair = beside(jnp.concatenate([dtokens, dtokens_far], 0))
    received, pair, output_far = advance(chains, sum_step(1), pair, across(output_block))
    sums = sums + received
    grad_tokens = place_xor([dtokens, pair[:block], dtokens_far, pair[block:]], me, F32)
    pair = beside(jnp.concatenate([output_block, output_far], 0))
    received, pair = advance(chains, sum_step(2), pair)
    sums = sums + received
    output = place_xor([output_block, pair[:block], output_far, pair[block:]], me, BF16)
    for k in range(3, bits):
        (received,) = advance(chains, sum_step(k))
        sums = sums + received
    while len(late.steps) > 1:
        advance(chains)
    merging = merging.reshape(3, width, width).astype(F32)
    output, merging = advance(chains, output, merging)
    late, grad_out, grad_in = [
        chain.array.reshape(-1, width) for chain in (late, grad_out, grad_in)
    ]

    held = ADAPTERS // 4
    usage = lax.dynamic_slice_in_dim(sums[5], me * held, held) / sums[5, ADAPTERS]
    return (
        output,
        grad_tokens,
        late[: 3 * columns].reshape(3, columns, width).swapaxes(1, 2).astype(F32),
        late[3 * columns :].astype(F32),
        grad_in.astype(F32),
        sums[8],
        grad_out.astype(F32),
        sums[4],
        jnp.stack([sums[6], sums[0], sums[1]]),
        jnp.stack([sums[7], sums[2], sums[3]]),
        merging,
        usage,
    )


def solution(mesh):
    placed = (
        P("tok", None),
        P("tok", None),
        P(None, None, "ad"),
        P("ad", None),
        P(None, "ad"),
        P("ad"),
        P("ad", None),
        P(),
        P(),
        P(),
        P(None, "ad"),
        P("ad", None, None),
        P(),
        P("tok", "ad"),
        P("tok"),
    )
    return jax.shard_map(
        on_device,
        mesh=mesh,
        in_specs=placed,
        out_specs=(
            P("tok", None),
            P("tok", None),
            P(None, None, "ad"),
            P("ad", None),
            P(None, "ad"),
            P("ad"),
            P("ad", None),
            P(),
            P(),
            P(),
            P(),
            P("ad"),
        ),
        check_vma=False,
    )
```

```python
import jax
import jax.numpy as jnp
from jax import lax
from jax.experimental import pallas as pl
from jax.experimental.pallas import tpu as pltpu
from jax.sharding import PartitionSpec as P

HEAD = 64
EPSILON = 1e-06
NEGATIVE = -1e30
ADAPTERS = 16
MASK_ROWS = 16
F32 = jnp.float32
BF16 = jnp.bfloat16


def normalize(values, gain, shift):
    centred = values - jnp.mean(values, -1, keepdims=True)
    inverse = lax.rsqrt(jnp.mean(centred * centred, -1, keepdims=True) + EPSILON)
    unit_rows = centred * inverse
    return (unit_rows * gain + shift, unit_rows, inverse)


def normalize_back(gradient, unit_rows, inverse, gain):
    scaled = gradient * gain
    centred = (
        scaled
        - jnp.mean(scaled, -1, keepdims=True)
        - unit_rows * jnp.mean(scaled * unit_rows, -1, keepdims=True)
    )
    return (centred * inverse, jnp.sum(gradient * unit_rows, 0), jnp.sum(gradient, 0))


def gelu_both(values):
    cdf = 0.5 * (1.0 + lax.erf(values * 0.7071067811865476))
    density = jnp.exp(-0.5 * values * values) * 0.3989422804014327
    return values * cdf, cdf + values * density


def dot(left, right, dims=((1,), (0,))):
    return lax.dot_general(left, right, (dims, ((), ())), preferred_element_type=F32)


def dot_nt(left, right):
    return dot(left, right, ((1,), (1,)))


def dot_tn(left, right):
    return dot(left, right, ((0,), (0,)))


def split_dot(left, right):
    high = left.astype(BF16)
    rest = (left - high.astype(F32)).astype(BF16)
    return dot(high, right) + dot(rest, right)


def after(array, *others):
    return lax.optimization_barrier((array, *others))[0]


def swap(array, axis, size, step):
    return lax.ppermute(array, axis, [(i, i ^ step) for i in range(size)])


def beside(array):
    return swap(array, "ad", 4, 1)


def across(array):
    return swap(array, "ad", 4, 2)


def gather_xor(block):
    far = across(block)
    return [block, beside(block), far, beside(far)]


def tok_plan(size):
    return [("tok", size, bit) for bit in range(size.bit_length() - 1)]


def side_of(step):
    axis, _, bit = step
    return (lax.axis_index(axis) >> bit) & 1


def halve_start(array, step):
    axis, size, bit = step
    side = side_of(step)
    rows = array.shape[0] // 2
    sent = lax.dynamic_slice_in_dim(array, (1 - side) * rows, rows)
    kept = lax.dynamic_slice_in_dim(array, side * rows, rows)
    return kept, swap(sent, axis, size, 1 << bit)


def add_low(kept, received):
    return (kept.astype(F32) + received.astype(F32)).astype(BF16)


def halve(array, plan):
    for step in plan:
        array = add_low(*halve_start(array, step))
    return array


def double(array, plan):
    for step in reversed(plan):
        axis, size, bit = step
        side = side_of(step) == 1
        other = swap(array, axis, size, 1 << bit)
        array = jnp.concatenate(
            [jnp.where(side, other, array), jnp.where(side, array, other)], 0
        )
    return array


class Chain:
    def __init__(self, array, halving, doubling=()):
        self.array = array
        self.steps = [(True, *step) for step in halving] + [(False, *step) for step in doubling]
        self.parts = None

    def prepare(self):
        halves, step, place = self.steps[0]
        self.parts = (self.array, self.array)
        if halves:
            side = side_of(step)
            self.parts = tuple(
                lax.dynamic_index_in_dim(self.array, part, place, keepdims=False)
                for part in (side, 1 - side)
            )
        return self.parts

    def start(self):
        _, (axis, size, bit), _ = self.steps[0]
        kept, sent = self.parts or self.prepare()
        self.parts = None
        return kept, swap(sent, axis, size, 1 << bit)

    def finish(self, own, received):
        halves, step, place = self.steps.pop(0)
        if halves:
            self.array = add_low(own, received)
        else:
            side = side_of(step) == 1
            self.array = jnp.stack(
                [jnp.where(side, received, own), jnp.where(side, own, received)], place
            )


def tok_chain(array, over_tok):
    bits = len(over_tok)
    steps = [(step, 0) for step in over_tok]
    return Chain(array.reshape((2,) * bits + (-1, array.shape[1])), steps, steps[::-1])


def advance(chains, *others):
    chains = [chain for chain in chains if chain.steps]
    flights = [chain.start() for chain in chains]
    flights, others = lax.optimization_barrier((flights, others))
    for chain, flight in zip(chains, flights):
        chain.finish(*flight)
    return others


def place_xor(blocks, me, dtype):
    rows = blocks[0].shape[0]
    whole = jnp.zeros((4 * rows,) + blocks[0].shape[1:], dtype)
    for k, block in enumerate(blocks):
        whole = lax.dynamic_update_slice_in_dim(whole, block.astype(dtype), (me ^ k) * rows, 0)
    return whole


def to_xor(blocks, me):
    return [lax.dynamic_index_in_dim(blocks, me ^ k, 0, keepdims=False) for k in range(4)]


VMEM = pltpu.VMEM


def whole_hbm(count):
    return [pl.BlockSpec(memory_space=pl.ANY)] * count


def fixed(shape, *index):
    return pl.BlockSpec(shape, lambda *_: index)


def params(limit=32):
    return pltpu.CompilerParams(vmem_limit_bytes=limit * 1024 * 1024)


def attend_rows(query, key_ref, value_ref, bias, context_ref, weight_ref, inverse_ref):
    lane = lax.broadcasted_iota(jnp.int32, inverse_ref.shape, 1)
    inverses = jnp.zeros(inverse_ref.shape, F32)
    for head in range(query.shape[1] // HEAD):
        lanes = slice(head * HEAD, (head + 1) * HEAD)
        logits = dot_nt(query[:, lanes], key_ref[:, lanes]) + bias
        expon = jnp.exp(logits - jnp.max(logits, -1, keepdims=True)).astype(BF16)
        weight_ref[head] = expon
        inverse = 1.0 / jnp.sum(expon.astype(F32), -1, keepdims=True)
        inverses = jnp.where(lane == head, inverse, inverses)
        context_ref[:, lanes] = (dot(expon, value_ref[:, lanes]) * inverse).astype(BF16)
    inverse_ref[...] = inverses


def key_bias(scalar_ref, rows):
    block = rows // 4
    column = lax.broadcasted_iota(jnp.int32, (1, rows), 1)
    position = ((column // block) ^ scalar_ref[0]) * block + column % block
    return jnp.where(position < scalar_ref[1], 0.0, NEGATIVE).astype(F32)


def attend_kernel(
    scalar_ref,
    tokens_hbm,
    qkv_ref,
    context_ref,
    weight_ref,
    inverse_ref,
    query_ref,
    key_ref,
    value_ref,
    placed_hbm,
    tokens_ref,
    sems,
):
    step = pl.program_id(0)
    rows = tokens_ref.shape[0]
    block = rows // 4
    loads = []
    for k in range(4):
        source = pl.multiple_of((scalar_ref[0] ^ k) * block, block)
        loads.append(
            pltpu.make_async_copy(
                tokens_hbm.at[pl.ds(source, block)],
                tokens_ref.at[pl.ds(k * block, block)],
                sems.at[k],
            )
        )
    placing = pltpu.make_async_copy(tokens_ref, placed_hbm, sems.at[4])

    @pl.when(step == 0)
    def _():
        for load in loads:
            load.start()
        for load in loads:
            load.wait()
        placing.start()
        placed = tokens_ref[...]
        query_ref[...] = (dot_nt(placed, qkv_ref[0]).astype(BF16) * HEAD ** (-0.5)).astype(BF16)
        key_ref[...] = dot_nt(placed, qkv_ref[1]).astype(BF16)
        value_ref[...] = dot_nt(placed, qkv_ref[2]).astype(BF16)

    bias = key_bias(scalar_ref, rows)
    query = query_ref[pl.ds(pl.multiple_of(step * block, block), block), :]
    attend_rows(query, key_ref, value_ref, bias, context_ref, weight_ref, inverse_ref)

    @pl.when(step == pl.num_programs(0) - 1)
    def _():
        placing.wait()


def attend(scalars, tokens, attn_qkv):
    rows, width = tokens.shape
    columns = attn_qkv.shape[1]
    heads = columns // HEAD
    block = rows // 4
    projected = jax.ShapeDtypeStruct((rows, columns), BF16)
    return pl.pallas_call(
        attend_kernel,
        grid=(4,),
        in_specs=[
            pl.BlockSpec(memory_space=pltpu.SMEM),
            pl.BlockSpec(memory_space=pl.ANY),
            fixed(attn_qkv.shape, 0, 0, 0),
        ],
        out_specs=[
            pl.BlockSpec((block, columns), lambda i: (i, 0)),
            pl.BlockSpec((heads, block, rows), lambda i: (0, i, 0)),
            pl.BlockSpec((block, 128), lambda i: (i, 0)),
        ]
        + [fixed((rows, columns), 0, 0)] * 3
        + [pl.BlockSpec(memory_space=pl.ANY)],
        out_shape=[
            jax.ShapeDtypeStruct((rows, columns), BF16),
            jax.ShapeDtypeStruct((heads, rows, rows), BF16),
            jax.ShapeDtypeStruct((rows, 128), F32),
        ]
        + [projected] * 3
        + [jax.ShapeDtypeStruct((rows, width), BF16)],
        scratch_shapes=[VMEM((rows, width), BF16), pltpu.SemaphoreType.DMA((5,))],
        compiler_params=params(),
        cost_estimate=pl.CostEstimate(flops=5000000000, bytes_accessed=14000000, transcendentals=0),
        name="attend",
    )(scalars, tokens, attn_qkv)


def attend_back_kernel(
    query_ref,
    key_ref,
    value_ref,
    context_ref,
    inverse_ref,
    dcontext_ref,
    weight_ref,
    tokens_hbm,
    qkv_hbm,
    late_ref,
    part0_ref,
    part2_ref,
    part13_ref,
    dquery,
    dkey,
    dvalue,
    tokens_ref,
    qkv_ref,
    sems,
):
    step = pl.program_id(0)
    block = query_ref.shape[0]
    columns = query_ref.shape[1]
    loads = (
        pltpu.make_async_copy(tokens_hbm, tokens_ref, sems.at[0]),
        pltpu.make_async_copy(qkv_hbm, qkv_ref, sems.at[1]),
    )

    @pl.when(step == 0)
    def _():
        for load in loads:
            load.start()
        dkey[...] = jnp.zeros_like(dkey)
        dvalue[...] = jnp.zeros_like(dvalue)

    scaling = HEAD ** (-0.5)
    rows = pl.ds(pl.multiple_of(step * block, block), block)
    for head in range(columns // HEAD):
        lanes = slice(head * HEAD, (head + 1) * HEAD)
        weights = weight_ref[head]
        scaled = dcontext_ref[:, lanes].astype(F32) * inverse_ref[:, head : head + 1]
        delta = jnp.sum(scaled * context_ref[:, lanes].astype(F32), -1, keepdims=True)
        dcontext = scaled.astype(BF16)
        dweights = dot_nt(dcontext, value_ref[:, lanes])
        dlogits = (weights.astype(F32) * (dweights - delta)).astype(BF16)
        dquery[rows, lanes] = (dot(dlogits, key_ref[:, lanes]) * scaling).astype(BF16)
        dkey[lanes, :] += dot_tn(query_ref[:, lanes], dlogits)
        dvalue[lanes, :] += dot_tn(dcontext, weights)

    @pl.when(step == pl.num_programs(0) - 1)
    def _():
        for load in loads:
            load.wait()
        dkey_low = dkey[...].astype(BF16)
        dvalue_low = dvalue[...].astype(BF16)
        tokens = tokens_ref[...]
        late_ref[0:columns, :] = dot_tn(dquery[...], tokens).astype(BF16)
        late_ref[columns : 2 * columns, :] = dot(dkey_low, tokens).astype(BF16)
        late_ref[2 * columns :, :] = dot(dvalue_low, tokens).astype(BF16)
        part_refs = (part0_ref, part13_ref.at[0], part2_ref, part13_ref.at[1])
        for k, part_ref in enumerate(part_refs):
            part = slice(k * block, (k + 1) * block)
            dtokens = (
                dot(dquery[part, :], qkv_ref[0])
                + dot_tn(dkey_low[:, part], qkv_ref[1])
                + dot_tn(dvalue_low[:, part], qkv_ref[2])
            )
            part_ref[...] = dtokens.astype(BF16)


def attend_back(query, key, value, weights, context, inverses, dcontext, tokens, attn_qkv):
    rows, columns = query.shape
    heads = columns // HEAD
    width = tokens.shape[1]
    block = rows // 4
    part = jax.ShapeDtypeStruct((block, width), BF16)
    return pl.pallas_call(
        attend_back_kernel,
        grid=(4,),
        in_specs=[
            pl.BlockSpec((block, columns), lambda i: (i, 0)),
            fixed((rows, columns), 0, 0),
            fixed((rows, columns), 0, 0),
            pl.BlockSpec((block, columns), lambda i: (i, 0)),
            pl.BlockSpec((block, 128), lambda i: (i, 0)),
            pl.BlockSpec((block, columns), lambda i: (i, 0)),
            pl.BlockSpec((heads, block, rows), lambda i: (0, i, 0)),
        ]
        + whole_hbm(2),
        out_specs=[fixed((3 * columns, width), 0, 0)]
        + [fixed((block, width), 0, 0)] * 2
        + [fixed((2, block, width), 0, 0, 0)],
        out_shape=[
            jax.ShapeDtypeStruct((3 * columns, width), BF16),
            part,
            part,
            jax.ShapeDtypeStruct((2, block, width), BF16),
        ],
        scratch_shapes=[
            VMEM((rows, columns), BF16),
            VMEM((columns, rows), F32),
            VMEM((columns, rows), F32),
            VMEM(tokens.shape, BF16),
            VMEM(attn_qkv.shape, BF16),
            pltpu.SemaphoreType.DMA((2,)),
        ],
        compiler_params=params(),
        cost_estimate=pl.CostEstimate(flops=6000000000, bytes_accessed=14000000, transcendentals=0),
        name="attend_back",
    )(query, key, value, context, inverses, dcontext, weights, tokens, attn_qkv)


def feed_kernel(
    tokens_ref,
    context0_ref,
    context1_ref,
    context2_ref,
    context3_ref,
    bias_ref,
    gain_ref,
    shift_ref,
    mix0_hbm,
    mix1_hbm,
    mix2_hbm,
    mix3_hbm,
    in_hbm,
    out_hbm,
    first_low_ref,
    inner_ref,
    slope_ref,
    near_ref,
    far_ref,
    *refs,
):
    own_refs, (mix_ref, in_ref, out_ref, sems) = refs[:-4], refs[-4:]
    step = pl.program_id(0)
    columns = context0_ref.shape[1]
    loads = []
    for k, mix in enumerate((mix0_hbm, mix1_hbm, mix2_hbm, mix3_hbm)):
        loads.append(
            pltpu.make_async_copy(mix.at[pl.ds(0, columns)], mix_ref.at[k], sems.at[k])
        )
    loads.append(pltpu.make_async_copy(in_hbm, in_ref, sems.at[4]))
    loads.append(pltpu.make_async_copy(out_hbm, out_ref, sems.at[5]))

    @pl.when(step == 0)
    def _():
        for load in loads:
            load.start()
        for load in loads[:4]:
            load.wait()

    attended = (
        dot(context0_ref[...], mix_ref[0])
        + dot(context1_ref[...], mix_ref[1])
        + dot(context2_ref[...], mix_ref[2])
        + dot(context3_ref[...], mix_ref[3])
    )
    first, _, inverse = normalize(
        tokens_ref[...].astype(F32) + attended, gain_ref[0:1, :], shift_ref[0:1, :]
    )
    if own_refs:

        @pl.when(step == 0)
        def _():
            own_refs[0][...] = first
            own_refs[1][...] = inverse

    @pl.when(step == 0)
    def _():
        for load in loads[4:]:
            load.wait()

    first_low = first.astype(BF16)
    first_low_ref[...] = first_low
    inner, slope = gelu_both(dot(first_low, in_ref[...]) + bias_ref[...])
    inner = inner.astype(BF16)
    inner_ref[...] = inner
    slope_ref[...] = slope.astype(BF16)
    fed = dot(inner, out_ref[...]).astype(BF16)

    @pl.when(step == 0)
    def _():
        near_ref[...] = fed

    @pl.when(step == 1)
    def _():
        far_ref[...] = fed


def feed(half, tokens, contexts, mixes, ffn_in, bias, ffn_out, gains, shifts):
    rows, width = tokens.shape
    block = rows // 4
    columns = contexts[0].shape[1]
    hidden = ffn_in.shape[1]
    row_block = pl.BlockSpec((block, width), lambda i: (i, 0))
    hidden_block = pl.BlockSpec((block, hidden), lambda i: (i, 0))
    in_specs = [pl.BlockSpec((block, width), lambda i: (i + 2 * half, 0))]
    for k in range(4):
        in_specs.append(pl.BlockSpec((block, columns), lambda i, k=k: ((i + 2 * half) ^ k, 0)))
    in_specs += [fixed(array.shape, 0, 0) for array in (bias, gains, shifts)] + whole_hbm(6)
    out_specs = [row_block, hidden_block, hidden_block] + [fixed((block, width), 0, 0)] * 2
    out_shape = [
        jax.ShapeDtypeStruct((2 * block, width), BF16),
        jax.ShapeDtypeStruct((2 * block, hidden), BF16),
        jax.ShapeDtypeStruct((2 * block, hidden), BF16),
        jax.ShapeDtypeStruct((block, width), BF16),
        jax.ShapeDtypeStruct((block, width), BF16),
    ]
    if half == 0:
        out_specs += [fixed((block, width), 0, 0), fixed((block, 1), 0, 0)]
        out_shape += [
            jax.ShapeDtypeStruct((block, width), F32),
            jax.ShapeDtypeStruct((block, 1), F32),
        ]
    return pl.pallas_call(
        feed_kernel,
        grid=(2,),
        in_specs=in_specs,
        out_specs=out_specs,
        out_shape=out_shape,
        scratch_shapes=[
            VMEM((4, columns, width), BF16),
            VMEM(ffn_in.shape, BF16),
            VMEM(ffn_out.shape, BF16),
            pltpu.SemaphoreType.DMA((6,)),
        ],
        compiler_params=params(),
        cost_estimate=pl.CostEstimate(flops=3000000000, bytes_accessed=9000000, transcendentals=0),
        name="feed",
    )(tokens, *contexts, bias, gains, shifts, *mixes, ffn_in, ffn_out)


def feed_back_kernel(
    near_ref,
    far_ref,
    slope_ref,
    out_hbm,
    in_hbm,
    dinner_ref,
    near_part_ref,
    far_part_ref,
    sum_ref,
    out_ref,
    in_ref,
    sems,
):
    block = near_ref.shape[0]
    loads = (
        pltpu.make_async_copy(out_hbm, out_ref, sems.at[0]),
        pltpu.make_async_copy(in_hbm, in_ref, sems.at[1]),
    )
    for load in loads:
        load.start()
    for load in loads:
        load.wait()
    total = jnp.zeros((1, slope_ref.shape[1]), F32)
    for k, (dmid_ref, part_ref) in enumerate(
        ((near_ref, near_part_ref), (far_ref, far_part_ref))
    ):
        rows = slice(k * block, (k + 1) * block)
        dinner = (dot_nt(dmid_ref[...], out_ref[...]) * slope_ref[rows, :].astype(F32)).astype(BF16)
        dinner_ref[rows, :] = dinner
        total = total + jnp.sum(dinner.astype(F32), 0, keepdims=True)
        part_ref[...] = dot_nt(dinner, in_ref[...]).astype(BF16)
    sum_ref[0:1, :] = total
    sum_ref[1:8, :] = jnp.zeros((7, slope_ref.shape[1]), F32)


def feed_back(near, far, slope, ffn_out, ffn_in):
    block, width = near.shape
    hidden = slope.shape[1]
    part = jax.ShapeDtypeStruct((block, width), BF16)
    return pl.pallas_call(
        feed_back_kernel,
        grid=(1,),
        in_specs=[
            fixed(near.shape, 0, 0),
            fixed(far.shape, 0, 0),
            fixed((2 * block, hidden), 0, 0),
        ]
        + whole_hbm(2),
        out_specs=[
            fixed((2 * block, hidden), 0, 0),
            fixed(near.shape, 0, 0),
            fixed(far.shape, 0, 0),
            fixed((8, hidden), 0, 0),
        ],
        out_shape=[
            jax.ShapeDtypeStruct((2 * block, hidden), BF16),
            part,
            part,
            jax.ShapeDtypeStruct((8, hidden), F32),
        ],
        scratch_shapes=[
            VMEM(ffn_out.shape, BF16),
            VMEM(ffn_in.shape, BF16),
            pltpu.SemaphoreType.DMA((2,)),
        ],
        compiler_params=params(),
        cost_estimate=pl.CostEstimate(flops=1400000000, bytes_accessed=5000000, transcendentals=0),
        name="feed_back",
    )(near, far, slope, ffn_out, ffn_in)


def feed_grads_kernel(
    near_inner_hbm,
    far_inner_hbm,
    near_first_hbm,
    far_first_hbm,
    dmid0_hbm,
    dmid1_hbm,
    dmid2_hbm,
    dmid3_hbm,
    near_hbm,
    far_hbm,
    out_ref,
    in_ref,
    inner,
    dmid,
    first,
    dinner,
    sems,
):
    loads = [[], []]
    groups = (
        (0, inner, (near_inner_hbm, far_inner_hbm)),
        (0, dmid, (dmid0_hbm, dmid1_hbm, dmid2_hbm, dmid3_hbm)),
        (1, first, (near_first_hbm, far_first_hbm)),
        (1, dinner, (near_hbm, far_hbm)),
    )
    count = 0
    for turn, whole, parts in groups:
        start = 0
        for part in parts:
            rows = part.shape[0]
            loads[turn].append(
                pltpu.make_async_copy(part, whole.at[pl.ds(start, rows)], sems.at[count])
            )
            loads[turn][-1].start()
            start += rows
            count += 1
    for load in loads[0]:
        load.wait()
    out_ref[...] = dot_tn(inner[...], dmid[...]).astype(BF16)
    for load in loads[1]:
        load.wait()
    in_ref[...] = dot_tn(first[...], dinner[...]).astype(BF16)


def feed_grads(inners, firsts, dmids, near, far):
    rows, hidden = inners[0].shape[0] * 2, inners[0].shape[1]
    width = firsts[0].shape[1]
    arrays = (*inners, *firsts, *dmids, near, far)
    return pl.pallas_call(
        feed_grads_kernel,
        in_specs=whole_hbm(len(arrays)),
        out_specs=[pl.BlockSpec(memory_space=VMEM)] * 2,
        out_shape=[
            jax.ShapeDtypeStruct((hidden, width), BF16),
            jax.ShapeDtypeStruct((width, hidden), BF16),
        ],
        scratch_shapes=[
            VMEM((rows, hidden), BF16),
            VMEM((rows, width), BF16),
            VMEM((rows, width), BF16),
            VMEM((rows, hidden), BF16),
            pltpu.SemaphoreType.DMA((len(arrays),)),
        ],
        compiler_params=params(60),
        cost_estimate=pl.CostEstimate(flops=2400000000, bytes_accessed=9000000, transcendentals=0),
        name="feed_grads",
    )(*arrays)


def low_kernel(
    part_ref,
    beside_ref,
    across_ref,
    dmid_ref,
    first_ref,
    inverse_ref,
    gain_ref,
    shift_ref,
    small_ref,
    near_sum_ref,
    far_sum_ref,
    context0_hbm,
    context1_hbm,
    context2_hbm,
    context3_hbm,
    mix0_hbm,
    mix1_hbm,
    mix2_hbm,
    mix3_hbm,
    dlow_ref,
    dcontext0_ref,
    dcontext1_ref,
    dcontext23_ref,
    grad02_ref,
    grad13_ref,
    sums_ref,
    context_ref,
    mix_ref,
    sems,
):
    block = part_ref.shape[0]
    columns = dcontext0_ref.shape[1]
    loads = []
    for k, mix in enumerate((mix0_hbm, mix1_hbm, mix2_hbm, mix3_hbm)):
        loads.append(
            pltpu.make_async_copy(mix.at[pl.ds(0, columns)], mix_ref.at[k], sems.at[k])
        )
    for k, context in enumerate((context0_hbm, context1_hbm, context2_hbm, context3_hbm)):
        rows = pl.ds(k * block, block)
        loads.append(pltpu.make_async_copy(context.at[rows], context_ref.at[k], sems.at[4 + k]))
    for load in loads:
        load.start()
    dfirst = (
        part_ref[...].astype(F32)
        + beside_ref[...].astype(F32)
        + across_ref[...].astype(F32)
        + dmid_ref[...]
    )
    unit = (first_ref[...] - shift_ref[0:1, :]) / gain_ref[0:1, :]
    dlow, gain, shift = normalize_back(dfirst, unit, inverse_ref[...], gain_ref[0:1, :])
    dlow_ref[...] = dlow
    dlow_low = dlow.astype(BF16)
    for load in loads[:4]:
        load.wait()
    dcontext0_ref[...] = dot_nt(dlow_low, mix_ref[0]).astype(BF16)
    dcontext1_ref[...] = dot_nt(dlow_low, mix_ref[1]).astype(BF16)
    dcontext23_ref[0] = dot_nt(dlow_low, mix_ref[2]).astype(BF16)
    dcontext23_ref[1] = dot_nt(dlow_low, mix_ref[3]).astype(BF16)
    for load in loads[4:]:
        load.wait()
    grad02_ref[0:columns, :] = dot_tn(context_ref[0], dlow_low).astype(BF16)
    grad02_ref[columns:, :] = dot_tn(context_ref[2], dlow_low).astype(BF16)
    grad13_ref[0:columns, :] = dot_tn(context_ref[1], dlow_low).astype(BF16)
    grad13_ref[columns:, :] = dot_tn(context_ref[3], dlow_low).astype(BF16)
    sums_ref[0:6, :] = small_ref[0:6, :]
    sums_ref[6:7, :] = gain[None, :]
    sums_ref[7:8, :] = shift[None, :]
    sums_ref[8:16, :] = near_sum_ref[...] + far_sum_ref[...]


def low(
    part,
    near,
    far,
    dmid,
    first,
    inverse,
    gains,
    shifts,
    contexts,
    mixes,
    small,
    near_sum,
    far_sum,
):
    block, width = dmid.shape
    columns = contexts[0].shape[1]
    rows = fixed((block, width), 0, 0)
    in_specs = [rows] * 5
    in_specs += [fixed(array.shape, 0, 0) for array in (inverse, gains, shifts)]
    in_specs += [fixed(small.shape, 0, 0)] + [fixed(near_sum.shape, 0, 0)] * 2
    in_specs += whole_hbm(8)
    out_shape = [
        jax.ShapeDtypeStruct((block, width), F32),
        jax.ShapeDtypeStruct((block, columns), BF16),
        jax.ShapeDtypeStruct((block, columns), BF16),
        jax.ShapeDtypeStruct((2, block, columns), BF16),
        jax.ShapeDtypeStruct((2 * columns, width), BF16),
        jax.ShapeDtypeStruct((2 * columns, width), BF16),
        jax.ShapeDtypeStruct((16, width), F32),
    ]
    return pl.pallas_call(
        low_kernel,
        grid=(1,),
        in_specs=in_specs,
        out_specs=[fixed(out.shape, *([0] * len(out.shape))) for out in out_shape],
        out_shape=out_shape,
        scratch_shapes=[
            VMEM((4, block, columns), BF16),
            VMEM((4, columns, width), BF16),
            pltpu.SemaphoreType.DMA((8,)),
        ],
        compiler_params=params(60),
        cost_estimate=pl.CostEstimate(flops=600000000, bytes_accessed=6000000, transcendentals=0),
        name="low",
    )(
        part,
        near,
        far,
        dmid,
        first,
        inverse,
        gains,
        shifts,
        small,
        near_sum,
        far_sum,
        *contexts,
        *mixes,
    )


def merge_kernel(
    scalar_ref,
    first_ref,
    fed_ref,
    fed_beside_ref,
    fed_across_ref,
    bias_ref,
    gain_ref,
    shift_ref,
    cotangent_hbm,
    mix0_hbm,
    mix1_hbm,
    mix2_hbm,
    mix3_hbm,
    merging_hbm,
    output_ref,
    dmid_ref,
    dmid_low_ref,
    kept_ref,
    sent_ref,
    small_ref,
    down_ref,
    up_ref,
    mask_ref,
    merging_ref,
    cotangent_ref,
    sems,
):
    rows, width = first_ref.shape
    me = scalar_ref[0]
    length = scalar_ref[1]
    part = (mix0_hbm.shape[0] - MASK_ROWS) // 3
    columns = 4 * part
    copies = []
    for k, mix in enumerate((mix0_hbm, mix1_hbm, mix2_hbm, mix3_hbm)):
        place = pl.ds(k * part, part)
        copies.append(
            (
                pltpu.make_async_copy(mix.at[pl.ds(part, part)], down_ref.at[place], sems.at[k]),
                pltpu.make_async_copy(
                    mix.at[pl.ds(2 * part, part)], up_ref.at[place], sems.at[4 + k]
                ),
                pltpu.make_async_copy(
                    mix.at[pl.ds(3 * part, MASK_ROWS)], mask_ref.at[k], sems.at[8 + k]
                ),
            )
        )
    merging_copy = pltpu.make_async_copy(merging_hbm, merging_ref, sems.at[12])
    cotangent_copy = pltpu.make_async_copy(
        cotangent_hbm.at[pl.ds(pl.multiple_of(me * rows, rows), rows)], cotangent_ref, sems.at[13]
    )
    for group in copies:
        group[0].start()
    merging_copy.start()
    for group in copies:
        group[1].start()
        group[2].start()
    cotangent_copy.start()
    adapters = ADAPTERS
    scaling = width ** (-0.5)
    rank = columns // adapters
    held = adapters // 4
    expand = (
        lax.broadcasted_iota(jnp.int32, (adapters, columns), 1) // rank
        == lax.broadcasted_iota(jnp.int32, (adapters, columns), 0)
    ).astype(F32)
    expand = expand.astype(BF16)

    def collect(wide):
        high = wide.astype(BF16)
        rest = (wide - high.astype(F32)).astype(BF16)
        return dot_nt(high, expand) + dot_nt(rest, expand)

    fed = (
        fed_ref[...].astype(F32)
        + fed_beside_ref[...].astype(F32)
        + fed_across_ref[...].astype(F32)
        + bias_ref[...]
    )
    second, unit_second, inverse_second = normalize(
        first_ref[...] + fed, gain_ref[1:2, :], shift_ref[1:2, :]
    )
    second_low = second.astype(BF16)
    for group in copies:
        group[0].wait()
    squeezed, slope = gelu_both(dot_nt(second_low, down_ref[...]))
    squeezed = squeezed.astype(BF16).astype(F32)
    merging_copy.wait()
    fquery = dot(second_low, merging_ref[0]).astype(BF16)
    asked = dot_nt(fquery, merging_ref[1])
    for group in copies:
        group[1].wait()
        group[2].wait()
    cotangent_copy.wait()
    asked_up = dot_nt(asked.astype(BF16), up_ref[...])
    scores = scaling * (
        jnp.sum(asked * second, -1, keepdims=True) + collect(squeezed * asked_up)
    )
    lane = lax.broadcasted_iota(jnp.int32, (1, adapters), 1)
    usable = jnp.zeros((1, adapters), F32)
    for k in range(4):
        usable = jnp.where(lane // held == k, mask_ref[k, 0:1, 0:adapters].astype(F32), usable)
    usable = usable > 0.5
    scores = jnp.where(usable, scores, NEGATIVE)
    highest = jnp.max(scores, -1, keepdims=True)
    weights = jnp.where(usable, jnp.exp(scores - highest), 0.0)
    probs = weights / jnp.sum(weights, -1, keepdims=True)
    total = jnp.sum(probs, -1, keepdims=True)
    probs_wide = split_dot(probs, expand)
    mixed = total * second + dot((probs_wide * squeezed).astype(BF16), up_ref[...])
    mixed_low = mixed.astype(BF16)
    blended = dot(mixed_low, merging_ref[2])
    final, unit_third, inverse_third = normalize(
        second + blended, gain_ref[2:3, :], shift_ref[2:3, :]
    )
    output_ref[...] = final.astype(BF16)
    dthird, gain_third, shift_third = normalize_back(
        cotangent_ref[...].astype(F32), unit_third, inverse_third, gain_ref[2:3, :]
    )
    dthird_low = dthird.astype(BF16)
    pulled = dot_nt(dthird_low, merging_ref[2])
    pulled_up = dot_nt(pulled.astype(BF16), up_ref[...])
    dprobs = jnp.sum(pulled * second, -1, keepdims=True) + collect(squeezed * pulled_up)
    dscores = probs * (dprobs - jnp.sum(probs * dprobs, -1, keepdims=True)) * scaling
    dscores_total = jnp.sum(dscores, -1, keepdims=True)
    dscores_wide = split_dot(dscores, expand)
    weighed = dscores_total * second + dot((dscores_wide * squeezed).astype(BF16), up_ref[...])
    weighed_low = weighed.astype(BF16)
    dquery = dot(weighed_low, merging_ref[1]).astype(BF16)
    dbottle = ((dscores_wide * asked_up + probs_wide * pulled_up) * slope).astype(BF16)
    dsecond = (
        dthird
        + dscores_total * asked
        + total * pulled
        + dot(dbottle, down_ref[...])
        + dot_nt(dquery, merging_ref[0])
    )
    dmid, gain_second, shift_second = normalize_back(
        dsecond, unit_second, inverse_second, gain_ref[1:2, :]
    )
    dmid_ref[...] = dmid
    dmid_low_ref[...] = dmid.astype(BF16)
    position = me * rows + lax.broadcasted_iota(jnp.int32, (rows, 1), 0)
    mass = jnp.sum(jnp.where(position < length, probs, 0.0), 0, keepdims=True)
    source = lax.broadcasted_iota(jnp.int32, (adapters, width), 0)
    target = lax.broadcasted_iota(jnp.int32, (adapters, width), 1)
    move = ((source // held) ^ me) * held + source % held == target
    mass = lax.dot_general(
        jnp.broadcast_to(mass, (8, adapters)),
        move.astype(F32),
        (((1,), (0,)), ((), ())),
        precision=lax.Precision.HIGHEST,
        preferred_element_type=F32,
    )[0:1, :]
    counted = lax.broadcasted_iota(jnp.int32, (1, width), 1) == adapters
    small_ref[0:1, :] = gain_second[None, :]
    small_ref[1:2, :] = gain_third[None, :]
    small_ref[2:3, :] = shift_second[None, :]
    small_ref[3:4, :] = shift_third[None, :]
    small_ref[4:5, :] = jnp.sum(dmid, 0, keepdims=True)
    small_ref[5:6, :] = jnp.where(counted, 0.25 * length.astype(F32), mass)
    small_ref[6:8, :] = jnp.zeros((2, width), F32)
    core = me & 1
    quarter = width // 4
    for j, (left, right) in enumerate(
        ((second_low, dquery), (weighed_low, fquery), (mixed_low, dthird_low))
    ):
        grad = dot_tn(left, right).astype(BF16)
        for k in range(4):
            piece = 4 * j + k
            owner, place = piece // 3 % 2, piece // 6 * 3 + piece % 3
            value = grad[k * quarter : (k + 1) * quarter, :]

            @pl.when(core == owner)
            def _():
                kept_ref[place * quarter : (place + 1) * quarter, :] = value

            @pl.when(core != owner)
            def _():
                sent_ref[place * quarter : (place + 1) * quarter, :] = value


def merge(scalars, first, fed, near, far, bias, gains, shifts, cotangent, mixes, merging):
    rows, width = first.shape
    part = (mixes[0].shape[0] - MASK_ROWS) // 3
    grads = jax.ShapeDtypeStruct((3 * width // 2, width), BF16)
    out_shape = [
        jax.ShapeDtypeStruct((rows, width), BF16),
        jax.ShapeDtypeStruct((rows, width), F32),
        jax.ShapeDtypeStruct((rows, width), BF16),
        grads,
        grads,
        jax.ShapeDtypeStruct((8, width), F32),
    ]
    return pl.pallas_call(
        merge_kernel,
        grid=(1,),
        in_specs=[pl.BlockSpec(memory_space=pltpu.SMEM)]
        + [fixed(array.shape, 0, 0) for array in (first, fed, near, far, bias, gains, shifts)]
        + whole_hbm(6),
        out_specs=[fixed(array.shape, 0, 0) for array in out_shape],
        out_shape=out_shape,
        scratch_shapes=[
            VMEM((4 * part, width), BF16),
            VMEM((4 * part, width), BF16),
            VMEM((4, MASK_ROWS, width), BF16),
            VMEM(merging.shape, BF16),
            VMEM((rows, width), BF16),
            pltpu.SemaphoreType.DMA((14,)),
        ],
        compiler_params=params(),
        cost_estimate=pl.CostEstimate(flops=6000000000, bytes_accessed=14000000, transcendentals=0),
        name="merge",
    )(scalars, first, fed, near, far, bias, gains, shifts, cotangent, *mixes, merging)


def on_device(
    tokens,
    cotangent,
    attn_qkv,
    attn_out,
    ffn_in,
    ffn_bias_in,
    ffn_out,
    ffn_bias_out,
    norm_gains,
    norm_shifts,
    adapter_down,
    adapter_up,
    merging_proj,
    adapter_mask,
    lengths,
):
    me = lax.axis_index("ad")
    tok = lax.axis_size("tok")
    over_tok = tok_plan(tok)
    row_count, width = tokens.shape
    block = row_count // 4
    scalars = jnp.stack([me.astype(jnp.int32), lengths[0]])
    attn_qkv = attn_qkv.swapaxes(1, 2)

    mask = jnp.tile(adapter_mask.astype(BF16), (MASK_ROWS, width // adapter_mask.shape[1]))
    mix = jnp.concatenate([attn_out, adapter_down.T, adapter_up.reshape(-1, width), mask], 0)
    mix_far = across(mix)

    context, weights, inverses, query, key, value, tokens = attend(scalars, tokens, attn_qkv)
    contexts = gather_xor(context)
    mix_far = after(mix_far, context)
    mixes = [mix, beside(mix), mix_far, beside(mix_far)]
    shared_weights = (mixes, ffn_in, ffn_bias_in[None, :], ffn_out, norm_gains, norm_shifts)
    far_first, far_inner, far_slope, fed2, fed3 = feed(1, tokens, contexts, *shared_weights)
    fed_sum = add_low(fed2, beside(fed3))
    contexts[0] = after(context, fed_sum)
    near_first, near_inner, near_slope, fed0, fed1, first, inverse = feed(
        0, tokens, contexts, *shared_weights
    )
    fed1 = beside(fed1)
    fed_far, fed0 = lax.optimization_barrier((across(fed_sum), fed0))
    output_block, dmid, dmid_low, kept, sent, small = merge(
        scalars,
        first,
        fed0,
        fed1,
        fed_far,
        ffn_bias_out[None, :],
        norm_gains,
        norm_shifts,
        cotangent,
        mixes,
        merging_proj,
    )

    dmids = [dmid_low, beside(dmid_low), across(dmid_low)]
    received = beside(sent)
    near_dinner, part0, part1, near_sum = feed_back(
        dmids[0], dmids[1], near_slope, ffn_out, ffn_in
    )
    merging = add_low(after(kept, part0), received)
    bits = len(over_tok)
    merging = merging.reshape((2,) * (bits + 1) + (-1, width))
    places = [(over_tok[k], bits - k) for k in range(bits)]
    down_y = [(("ad", 4, 1), 0)]
    swapped = [(over_tok[1], bits - 1), (over_tok[0], bits - 1)]
    merging = [
        Chain(merging[..., : width // 2], places[:2]),
        Chain(merging[..., width // 2 :], swapped),
    ]
    dmids[2] = after(dmids[2], part0, *[chain.prepare() for chain in merging])
    dmids.append(beside(dmids[2]))
    far_dinner, part2, part3, far_sum = feed_back(dmids[2], dmids[3], far_slope, ffn_out, ffn_in)
    part_beside = beside(part1)
    part_sum = add_low(part2, beside(part3))
    part_far = across(part_sum)
    for chain in merging:
        chain.parts = (chain.parts[0], after(chain.parts[1], part_sum))
    grad_out, grad_in = feed_grads(
        (after(near_inner, part_sum), far_inner),
        (near_first, far_first),
        dmids,
        near_dinner,
        far_dinner,
    )
    grad_out = tok_chain(grad_out, over_tok)
    grad_in = tok_chain(grad_in, over_tok)
    part_far, part_beside, grad_out.array, grad_in.parts = advance(
        merging, part_far, part_beside, grad_out.array, grad_in.prepare()
    )
    part_far = after(part_far, grad_in.parts)

    dlow, dcontext0, dcontext1, dcontext23, grad02, grad13, sums = low(
        part0,
        part_beside,
        part_far,
        dmid,
        first,
        inverse,
        norm_gains,
        norm_shifts,
        contexts,
        mixes,
        small,
        near_sum,
        far_sum,
    )
    dcontext_far = across(dcontext23)
    pair = beside(jnp.stack([dcontext1, dcontext_far[1]]))
    dcontext = jnp.concatenate([dcontext0, pair[0], dcontext_far[0], pair[1]], 0)
    grad02 = add_low(grad02, beside(grad13))
    columns = context.shape[1]
    dcontext, grad02, grad_out.array = advance(
        merging + [grad_in], dcontext, grad02, grad_out.array
    )
    merging = Chain(
        jnp.concatenate([chain.array for chain in merging], -1), places[2:] + down_y
    )

    grad_attn_far = across(grad02[columns:])
    late, dtokens0, dtokens2, dtokens13 = attend_back(
        query,
        key,
        value,
        weights,
        context,
        inverses,
        dcontext,
        tokens,
        attn_qkv,
    )
    shared = sums[:8]
    late, grad_attn_far, received = advance(
        [merging, grad_in, grad_out], late, grad_attn_far, beside(shared)
    )
    shared = shared + received
    late = jnp.concatenate([late, add_low(grad02[:columns], grad_attn_far)], 0)
    late = tok_chain(late, over_tok)
    chains = [late, grad_out, grad_in]
    (received,) = advance([merging] + chains, beside(dtokens13))
    dtokens = dtokens0.astype(F32) + received[0].astype(F32) + dlow
    dtokens_far = across(add_low(dtokens2, received[1]))
    while merging.steps:
        advance([merging])
    merging = lax.all_gather(merging.array, ("ad", "tok"), axis=0)
    received, dtokens_far = advance(chains, across(shared), dtokens_far)
    sums = jnp.concatenate([shared + received, sums[8:]], 0)
    dtokens = (dtokens + dtokens_far.astype(F32)).astype(BF16)

    def sum_step(k):
        axis, size, bit = over_tok[k]
        return swap(sums, axis, size, 1 << bit)

    received, dtokens_far = advance(chains, sum_step(0), across(dtokens))
    sums = sums + received
    pair = beside(jnp.concatenate([dtokens, dtokens_far], 0))
    received, pair, output_far = advance(chains, sum_step(1), pair, across(output_block))
    sums = sums + received
    grad_tokens = place_xor([dtokens, pair[:block], dtokens_far, pair[block:]], me, F32)
    pair = beside(jnp.concatenate([output_block, output_far], 0))
    received, pair = advance(chains, sum_step(2), pair)
    sums = sums + received
    output = place_xor([output_block, pair[:block], output_far, pair[block:]], me, BF16)
    for k in range(3, bits):
        (received,) = advance(chains, sum_step(k))
        sums = sums + received
    while len(late.steps) > 1:
        advance(chains)
    merging = merging.reshape(3, width, width).astype(F32)
    output, merging = advance(chains, output, merging)
    late, grad_out, grad_in = [
        chain.array.reshape(-1, width) for chain in (late, grad_out, grad_in)
    ]

    held = ADAPTERS // 4
    usage = lax.dynamic_slice_in_dim(sums[5], me * held, held) / sums[5, ADAPTERS]
    return (
        output,
        grad_tokens,
        late[: 3 * columns].reshape(3, columns, width).swapaxes(1, 2).astype(F32),
        late[3 * columns :].astype(F32),
        grad_in.astype(F32),
        sums[8],
        grad_out.astype(F32),
        sums[4],
        jnp.stack([sums[6], sums[0], sums[1]]),
        jnp.stack([sums[7], sums[2], sums[3]]),
        merging,
        usage,
    )


def solution(mesh):
    placed = (
        P("tok", None),
        P("tok", None),
        P(None, None, "ad"),
        P("ad", None),
        P(None, "ad"),
        P("ad"),
        P("ad", None),
        P(),
        P(),
        P(),
        P(None, "ad"),
        P("ad", None, None),
        P(),
        P("tok", "ad"),
        P("tok"),
    )
    return jax.shard_map(
        on_device,
        mesh=mesh,
        in_specs=placed,
        out_specs=(
            P("tok", None),
            P("tok", None),
            P(None, None, "ad"),
            P("ad", None),
            P(None, "ad"),
            P("ad"),
            P("ad", None),
            P(),
            P(),
            P(),
            P(),
            P("ad"),
        ),
        check_vma=False,
    )
```

```python
import jax
import jax.numpy as jnp
from jax import lax
from jax.experimental import pallas as pl
from jax.experimental.pallas import tpu as pltpu
from jax.sharding import PartitionSpec as P

HEAD = 64
EPSILON = 1e-06
NEGATIVE = -1e30
ADAPTERS = 16
MASK_ROWS = 16
F32 = jnp.float32
BF16 = jnp.bfloat16


def normalize(values, gain, shift):
    centred = values - jnp.mean(values, -1, keepdims=True)
    inverse = lax.rsqrt(jnp.mean(centred * centred, -1, keepdims=True) + EPSILON)
    unit_rows = centred * inverse
    return (unit_rows * gain + shift, unit_rows, inverse)


def normalize_back(gradient, unit_rows, inverse, gain):
    scaled = gradient * gain
    centred = (
        scaled
        - jnp.mean(scaled, -1, keepdims=True)
        - unit_rows * jnp.mean(scaled * unit_rows, -1, keepdims=True)
    )
    return (centred * inverse, jnp.sum(gradient * unit_rows, 0), jnp.sum(gradient, 0))


def gelu_both(values):
    cdf = 0.5 * (1.0 + lax.erf(values * 0.7071067811865476))
    density = jnp.exp(-0.5 * values * values) * 0.3989422804014327
    return values * cdf, cdf + values * density


def dot(left, right, dims=((1,), (0,))):
    return lax.dot_general(left, right, (dims, ((), ())), preferred_element_type=F32)


def dot_nt(left, right):
    return dot(left, right, ((1,), (1,)))


def dot_tn(left, right):
    return dot(left, right, ((0,), (0,)))


def split_dot(left, right):
    high = left.astype(BF16)
    rest = (left - high.astype(F32)).astype(BF16)
    return dot(high, right) + dot(rest, right)


def after(array, *others):
    return lax.optimization_barrier((array, *others))[0]


def swap(array, axis, size, step):
    return lax.ppermute(array, axis, [(i, i ^ step) for i in range(size)])


def beside(array):
    return swap(array, "ad", 4, 1)


def across(array):
    return swap(array, "ad", 4, 2)


def gather_xor(block):
    far = across(block)
    return [block, beside(block), far, beside(far)]


def tok_plan(size):
    return [("tok", size, bit) for bit in range(size.bit_length() - 1)]


def side_of(step):
    axis, _, bit = step
    return (lax.axis_index(axis) >> bit) & 1


def halve_start(array, step):
    axis, size, bit = step
    side = side_of(step)
    rows = array.shape[0] // 2
    sent = lax.dynamic_slice_in_dim(array, (1 - side) * rows, rows)
    kept = lax.dynamic_slice_in_dim(array, side * rows, rows)
    return kept, swap(sent, axis, size, 1 << bit)


def add_low(kept, received):
    return (kept.astype(F32) + received.astype(F32)).astype(BF16)


def halve(array, plan):
    for step in plan:
        array = add_low(*halve_start(array, step))
    return array


def double(array, plan):
    for step in reversed(plan):
        axis, size, bit = step
        side = side_of(step) == 1
        other = swap(array, axis, size, 1 << bit)
        array = jnp.concatenate(
            [jnp.where(side, other, array), jnp.where(side, array, other)], 0
        )
    return array


class Chain:
    def __init__(self, array, halving, doubling=()):
        self.array = array
        self.steps = [(True, *step) for step in halving] + [(False, *step) for step in doubling]
        self.parts = None

    def prepare(self):
        halves, step, place = self.steps[0]
        self.parts = (self.array, self.array)
        if halves:
            side = side_of(step)
            self.parts = tuple(
                lax.dynamic_index_in_dim(self.array, part, place, keepdims=False)
                for part in (side, 1 - side)
            )
        return self.parts

    def start(self):
        _, (axis, size, bit), _ = self.steps[0]
        kept, sent = self.parts or self.prepare()
        self.parts = None
        return kept, swap(sent, axis, size, 1 << bit)

    def finish(self, own, received):
        halves, step, place = self.steps.pop(0)
        if halves:
            self.array = add_low(own, received)
        else:
            side = side_of(step) == 1
            self.array = jnp.stack(
                [jnp.where(side, received, own), jnp.where(side, own, received)], place
            )


def tok_chain(array, over_tok):
    bits = len(over_tok)
    steps = [(step, 0) for step in over_tok]
    return Chain(array.reshape((2,) * bits + (-1, array.shape[1])), steps, steps[::-1])


def advance(chains, *others):
    chains = [chain for chain in chains if chain.steps]
    flights = [chain.start() for chain in chains]
    flights, others = lax.optimization_barrier((flights, others))
    for chain, flight in zip(chains, flights):
        chain.finish(*flight)
    return others


def place_xor(blocks, me, dtype):
    rows = blocks[0].shape[0]
    whole = jnp.zeros((4 * rows,) + blocks[0].shape[1:], dtype)
    for k, block in enumerate(blocks):
        whole = lax.dynamic_update_slice_in_dim(whole, block.astype(dtype), (me ^ k) * rows, 0)
    return whole


def to_xor(blocks, me):
    return [lax.dynamic_index_in_dim(blocks, me ^ k, 0, keepdims=False) for k in range(4)]


VMEM = pltpu.VMEM


def whole_hbm(count):
    return [pl.BlockSpec(memory_space=pl.ANY)] * count


def fixed(shape, *index):
    return pl.BlockSpec(shape, lambda *_: index)


def params(limit=32):
    return pltpu.CompilerParams(vmem_limit_bytes=limit * 1024 * 1024)


def attend_rows(query, key_ref, value_ref, bias, context_ref, weight_ref, inverse_ref):
    lane = lax.broadcasted_iota(jnp.int32, inverse_ref.shape, 1)
    inverses = jnp.zeros(inverse_ref.shape, F32)
    for head in range(query.shape[1] // HEAD):
        lanes = slice(head * HEAD, (head + 1) * HEAD)
        logits = dot_nt(query[:, lanes], key_ref[:, lanes]) + bias
        expon = jnp.exp(logits - jnp.max(logits, -1, keepdims=True)).astype(BF16)
        weight_ref[head] = expon
        inverse = 1.0 / jnp.sum(expon.astype(F32), -1, keepdims=True)
        inverses = jnp.where(lane == head, inverse, inverses)
        context_ref[:, lanes] = (dot(expon, value_ref[:, lanes]) * inverse).astype(BF16)
    inverse_ref[...] = inverses


def key_bias(scalar_ref, rows):
    block = rows // 4
    column = lax.broadcasted_iota(jnp.int32, (1, rows), 1)
    position = ((column // block) ^ scalar_ref[0]) * block + column % block
    return jnp.where(position < scalar_ref[1], 0.0, NEGATIVE).astype(F32)


def attend_kernel(
    scalar_ref,
    tokens_hbm,
    qkv_ref,
    context_ref,
    weight_ref,
    inverse_ref,
    query_ref,
    key_ref,
    value_ref,
    placed_hbm,
    tokens_ref,
    sems,
):
    step = pl.program_id(0)
    rows = tokens_ref.shape[0]
    block = rows // 4
    loads = []
    for k in range(4):
        source = pl.multiple_of((scalar_ref[0] ^ k) * block, block)
        loads.append(
            pltpu.make_async_copy(
                tokens_hbm.at[pl.ds(source, block)],
                tokens_ref.at[pl.ds(k * block, block)],
                sems.at[k],
            )
        )
    placing = pltpu.make_async_copy(tokens_ref, placed_hbm, sems.at[4])

    @pl.when(step == 0)
    def _():
        for load in loads:
            load.start()
        for load in loads:
            load.wait()
        placing.start()
        placed = tokens_ref[...]
        query_ref[...] = (dot_nt(placed, qkv_ref[0]).astype(BF16) * HEAD ** (-0.5)).astype(BF16)
        key_ref[...] = dot_nt(placed, qkv_ref[1]).astype(BF16)
        value_ref[...] = dot_nt(placed, qkv_ref[2]).astype(BF16)

    bias = key_bias(scalar_ref, rows)
    query = query_ref[pl.ds(pl.multiple_of(step * block, block), block), :]
    attend_rows(query, key_ref, value_ref, bias, context_ref, weight_ref, inverse_ref)

    @pl.when(step == pl.num_programs(0) - 1)
    def _():
        placing.wait()


def attend(scalars, tokens, attn_qkv):
    rows, width = tokens.shape
    columns = attn_qkv.shape[1]
    heads = columns // HEAD
    block = rows // 4
    projected = jax.ShapeDtypeStruct((rows, columns), BF16)
    return pl.pallas_call(
        attend_kernel,
        grid=(4,),
        in_specs=[
            pl.BlockSpec(memory_space=pltpu.SMEM),
            pl.BlockSpec(memory_space=pl.ANY),
            fixed(attn_qkv.shape, 0, 0, 0),
        ],
        out_specs=[
            pl.BlockSpec((block, columns), lambda i: (i, 0)),
            pl.BlockSpec((heads, block, rows), lambda i: (0, i, 0)),
            pl.BlockSpec((block, 128), lambda i: (i, 0)),
        ]
        + [fixed((rows, columns), 0, 0)] * 3
        + [pl.BlockSpec(memory_space=pl.ANY)],
        out_shape=[
            jax.ShapeDtypeStruct((rows, columns), BF16),
            jax.ShapeDtypeStruct((heads, rows, rows), BF16),
            jax.ShapeDtypeStruct((rows, 128), F32),
        ]
        + [projected] * 3
        + [jax.ShapeDtypeStruct((rows, width), BF16)],
        scratch_shapes=[VMEM((rows, width), BF16), pltpu.SemaphoreType.DMA((5,))],
        compiler_params=params(),
        cost_estimate=pl.CostEstimate(flops=5000000000, bytes_accessed=14000000, transcendentals=0),
        name="attend",
    )(scalars, tokens, attn_qkv)


def attend_back_kernel(
    query_ref,
    key_ref,
    value_ref,
    context_ref,
    inverse_ref,
    dcontext_ref,
    weight_ref,
    tokens_hbm,
    qkv_hbm,
    late_ref,
    part0_ref,
    part2_ref,
    part13_ref,
    dquery,
    dkey,
    dvalue,
    tokens_ref,
    qkv_ref,
    sems,
):
    step = pl.program_id(0)
    block = query_ref.shape[0]
    columns = query_ref.shape[1]
    loads = (
        pltpu.make_async_copy(tokens_hbm, tokens_ref, sems.at[0]),
        pltpu.make_async_copy(qkv_hbm, qkv_ref, sems.at[1]),
    )

    @pl.when(step == 0)
    def _():
        for load in loads:
            load.start()
        dkey[...] = jnp.zeros_like(dkey)
        dvalue[...] = jnp.zeros_like(dvalue)

    scaling = HEAD ** (-0.5)
    rows = pl.ds(pl.multiple_of(step * block, block), block)
    for head in range(columns // HEAD):
        lanes = slice(head * HEAD, (head + 1) * HEAD)
        weights = weight_ref[head]
        scaled = dcontext_ref[:, lanes].astype(F32) * inverse_ref[:, head : head + 1]
        delta = jnp.sum(scaled * context_ref[:, lanes].astype(F32), -1, keepdims=True)
        dcontext = scaled.astype(BF16)
        dweights = dot_nt(dcontext, value_ref[:, lanes])
        dlogits = (weights.astype(F32) * (dweights - delta)).astype(BF16)
        dquery[rows, lanes] = (dot(dlogits, key_ref[:, lanes]) * scaling).astype(BF16)
        dkey[lanes, :] += dot_tn(query_ref[:, lanes], dlogits)
        dvalue[lanes, :] += dot_tn(dcontext, weights)

    @pl.when(step == pl.num_programs(0) - 1)
    def _():
        for load in loads:
            load.wait()
        dkey_low = dkey[...].astype(BF16)
        dvalue_low = dvalue[...].astype(BF16)
        tokens = tokens_ref[...]
        late_ref[0:columns, :] = dot_tn(dquery[...], tokens).astype(BF16)
        late_ref[columns : 2 * columns, :] = dot(dkey_low, tokens).astype(BF16)
        late_ref[2 * columns :, :] = dot(dvalue_low, tokens).astype(BF16)
        part_refs = (part0_ref, part13_ref.at[0], part2_ref, part13_ref.at[1])
        for k, part_ref in enumerate(part_refs):
            part = slice(k * block, (k + 1) * block)
            dtokens = (
                dot(dquery[part, :], qkv_ref[0])
                + dot_tn(dkey_low[:, part], qkv_ref[1])
                + dot_tn(dvalue_low[:, part], qkv_ref[2])
            )
            part_ref[...] = dtokens.astype(BF16)


def attend_back(query, key, value, weights, context, inverses, dcontext, tokens, attn_qkv):
    rows, columns = query.shape
    heads = columns // HEAD
    width = tokens.shape[1]
    block = rows // 4
    part = jax.ShapeDtypeStruct((block, width), BF16)
    return pl.pallas_call(
        attend_back_kernel,
        grid=(4,),
        in_specs=[
            pl.BlockSpec((block, columns), lambda i: (i, 0)),
            fixed((rows, columns), 0, 0),
            fixed((rows, columns), 0, 0),
            pl.BlockSpec((block, columns), lambda i: (i, 0)),
            pl.BlockSpec((block, 128), lambda i: (i, 0)),
            pl.BlockSpec((block, columns), lambda i: (i, 0)),
            pl.BlockSpec((heads, block, rows), lambda i: (0, i, 0)),
        ]
        + whole_hbm(2),
        out_specs=[fixed((3 * columns, width), 0, 0)]
        + [fixed((block, width), 0, 0)] * 2
        + [fixed((2, block, width), 0, 0, 0)],
        out_shape=[
            jax.ShapeDtypeStruct((3 * columns, width), BF16),
            part,
            part,
            jax.ShapeDtypeStruct((2, block, width), BF16),
        ],
        scratch_shapes=[
            VMEM((rows, columns), BF16),
            VMEM((columns, rows), F32),
            VMEM((columns, rows), F32),
            VMEM(tokens.shape, BF16),
            VMEM(attn_qkv.shape, BF16),
            pltpu.SemaphoreType.DMA((2,)),
        ],
        compiler_params=params(),
        cost_estimate=pl.CostEstimate(flops=6000000000, bytes_accessed=14000000, transcendentals=0),
        name="attend_back",
    )(query, key, value, context, inverses, dcontext, weights, tokens, attn_qkv)


def feed_kernel(
    tokens_ref,
    context0_ref,
    context1_ref,
    context2_ref,
    context3_ref,
    bias_ref,
    gain_ref,
    shift_ref,
    mix0_hbm,
    mix1_hbm,
    mix2_hbm,
    mix3_hbm,
    in_hbm,
    out_hbm,
    first_low_ref,
    inner_ref,
    slope_ref,
    near_ref,
    far_ref,
    *refs,
):
    own_refs, (mix_ref, in_ref, out_ref, sems) = refs[:-4], refs[-4:]
    step = pl.program_id(0)
    columns = context0_ref.shape[1]
    loads = []
    for k, mix in enumerate((mix0_hbm, mix1_hbm, mix2_hbm, mix3_hbm)):
        loads.append(
            pltpu.make_async_copy(mix.at[pl.ds(0, columns)], mix_ref.at[k], sems.at[k])
        )
    loads.append(pltpu.make_async_copy(in_hbm, in_ref, sems.at[4]))
    loads.append(pltpu.make_async_copy(out_hbm, out_ref, sems.at[5]))

    @pl.when(step == 0)
    def _():
        for load in loads:
            load.start()
        for load in loads[:4]:
            load.wait()

    attended = (
        dot(context0_ref[...], mix_ref[0])
        + dot(context1_ref[...], mix_ref[1])
        + dot(context2_ref[...], mix_ref[2])
        + dot(context3_ref[...], mix_ref[3])
    )
    first, _, inverse = normalize(
        tokens_ref[...].astype(F32) + attended, gain_ref[0:1, :], shift_ref[0:1, :]
    )
    if own_refs:

        @pl.when(step == 0)
        def _():
            own_refs[0][...] = first
            own_refs[1][...] = inverse

    @pl.when(step == 0)
    def _():
        for load in loads[4:]:
            load.wait()

    first_low = first.astype(BF16)
    first_low_ref[...] = first_low
    inner, slope = gelu_both(dot(first_low, in_ref[...]) + bias_ref[...])
    inner = inner.astype(BF16)
    inner_ref[...] = inner
    slope_ref[...] = slope.astype(BF16)
    fed = dot(inner, out_ref[...]).astype(BF16)

    @pl.when(step == 0)
    def _():
        near_ref[...] = fed

    @pl.when(step == 1)
    def _():
        far_ref[...] = fed


def feed(half, tokens, contexts, mixes, ffn_in, bias, ffn_out, gains, shifts):
    rows, width = tokens.shape
    block = rows // 4
    columns = contexts[0].shape[1]
    hidden = ffn_in.shape[1]
    row_block = pl.BlockSpec((block, width), lambda i: (i, 0))
    hidden_block = pl.BlockSpec((block, hidden), lambda i: (i, 0))
    in_specs = [pl.BlockSpec((block, width), lambda i: (i + 2 * half, 0))]
    for k in range(4):
        in_specs.append(pl.BlockSpec((block, columns), lambda i, k=k: ((i + 2 * half) ^ k, 0)))
    in_specs += [fixed(array.shape, 0, 0) for array in (bias, gains, shifts)] + whole_hbm(6)
    out_specs = [row_block, hidden_block, hidden_block] + [fixed((block, width), 0, 0)] * 2
    out_shape = [
        jax.ShapeDtypeStruct((2 * block, width), BF16),
        jax.ShapeDtypeStruct((2 * block, hidden), BF16),
        jax.ShapeDtypeStruct((2 * block, hidden), BF16),
        jax.ShapeDtypeStruct((block, width), BF16),
        jax.ShapeDtypeStruct((block, width), BF16),
    ]
    if half == 0:
        out_specs += [fixed((block, width), 0, 0), fixed((block, 1), 0, 0)]
        out_shape += [
            jax.ShapeDtypeStruct((block, width), F32),
            jax.ShapeDtypeStruct((block, 1), F32),
        ]
    return pl.pallas_call(
        feed_kernel,
        grid=(2,),
        in_specs=in_specs,
        out_specs=out_specs,
        out_shape=out_shape,
        scratch_shapes=[
            VMEM((4, columns, width), BF16),
            VMEM(ffn_in.shape, BF16),
            VMEM(ffn_out.shape, BF16),
            pltpu.SemaphoreType.DMA((6,)),
        ],
        compiler_params=params(),
        cost_estimate=pl.CostEstimate(flops=3000000000, bytes_accessed=9000000, transcendentals=0),
        name="feed",
    )(tokens, *contexts, bias, gains, shifts, *mixes, ffn_in, ffn_out)


def feed_back_kernel(
    near_ref,
    far_ref,
    slope_ref,
    out_hbm,
    in_hbm,
    dinner_ref,
    near_part_ref,
    far_part_ref,
    sum_ref,
    out_ref,
    in_ref,
    sems,
):
    block = near_ref.shape[0]
    loads = (
        pltpu.make_async_copy(out_hbm, out_ref, sems.at[0]),
        pltpu.make_async_copy(in_hbm, in_ref, sems.at[1]),
    )
    for load in loads:
        load.start()
    for load in loads:
        load.wait()
    total = jnp.zeros((1, slope_ref.shape[1]), F32)
    for k, (dmid_ref, part_ref) in enumerate(
        ((near_ref, near_part_ref), (far_ref, far_part_ref))
    ):
        rows = slice(k * block, (k + 1) * block)
        dinner = (dot_nt(dmid_ref[...], out_ref[...]) * slope_ref[rows, :].astype(F32)).astype(BF16)
        dinner_ref[rows, :] = dinner
        total = total + jnp.sum(dinner.astype(F32), 0, keepdims=True)
        part_ref[...] = dot_nt(dinner, in_ref[...]).astype(BF16)
    sum_ref[0:1, :] = total
    sum_ref[1:8, :] = jnp.zeros((7, slope_ref.shape[1]), F32)


def feed_back(near, far, slope, ffn_out, ffn_in):
    block, width = near.shape
    hidden = slope.shape[1]
    part = jax.ShapeDtypeStruct((block, width), BF16)
    return pl.pallas_call(
        feed_back_kernel,
        grid=(1,),
        in_specs=[
            fixed(near.shape, 0, 0),
            fixed(far.shape, 0, 0),
            fixed((2 * block, hidden), 0, 0),
        ]
        + whole_hbm(2),
        out_specs=[
            fixed((2 * block, hidden), 0, 0),
            fixed(near.shape, 0, 0),
            fixed(far.shape, 0, 0),
            fixed((8, hidden), 0, 0),
        ],
        out_shape=[
            jax.ShapeDtypeStruct((2 * block, hidden), BF16),
            part,
            part,
            jax.ShapeDtypeStruct((8, hidden), F32),
        ],
        scratch_shapes=[
            VMEM(ffn_out.shape, BF16),
            VMEM(ffn_in.shape, BF16),
            pltpu.SemaphoreType.DMA((2,)),
        ],
        compiler_params=params(),
        cost_estimate=pl.CostEstimate(flops=1400000000, bytes_accessed=5000000, transcendentals=0),
        name="feed_back",
    )(near, far, slope, ffn_out, ffn_in)


def feed_grads_kernel(
    near_inner_hbm,
    far_inner_hbm,
    near_first_hbm,
    far_first_hbm,
    dmid0_hbm,
    dmid1_hbm,
    dmid2_hbm,
    dmid3_hbm,
    near_hbm,
    far_hbm,
    out_ref,
    in_ref,
    inner,
    dmid,
    first,
    dinner,
    sems,
):
    loads = [[], []]
    groups = (
        (0, inner, (near_inner_hbm, far_inner_hbm)),
        (0, dmid, (dmid0_hbm, dmid1_hbm, dmid2_hbm, dmid3_hbm)),
        (1, first, (near_first_hbm, far_first_hbm)),
        (1, dinner, (near_hbm, far_hbm)),
    )
    count = 0
    for turn, whole, parts in groups:
        start = 0
        for part in parts:
            rows = part.shape[0]
            loads[turn].append(
                pltpu.make_async_copy(part, whole.at[pl.ds(start, rows)], sems.at[count])
            )
            loads[turn][-1].start()
            start += rows
            count += 1
    for load in loads[0]:
        load.wait()
    out_ref[...] = dot_tn(inner[...], dmid[...]).astype(BF16)
    for load in loads[1]:
        load.wait()
    in_ref[...] = dot_tn(first[...], dinner[...]).astype(BF16)


def feed_grads(inners, firsts, dmids, near, far):
    rows, hidden = inners[0].shape[0] * 2, inners[0].shape[1]
    width = firsts[0].shape[1]
    arrays = (*inners, *firsts, *dmids, near, far)
    return pl.pallas_call(
        feed_grads_kernel,
        in_specs=whole_hbm(len(arrays)),
        out_specs=[pl.BlockSpec(memory_space=VMEM)] * 2,
        out_shape=[
            jax.ShapeDtypeStruct((hidden, width), BF16),
            jax.ShapeDtypeStruct((width, hidden), BF16),
        ],
        scratch_shapes=[
            VMEM((rows, hidden), BF16),
            VMEM((rows, width), BF16),
            VMEM((rows, width), BF16),
            VMEM((rows, hidden), BF16),
            pltpu.SemaphoreType.DMA((len(arrays),)),
        ],
        compiler_params=params(60),
        cost_estimate=pl.CostEstimate(flops=2400000000, bytes_accessed=9000000, transcendentals=0),
        name="feed_grads",
    )(*arrays)


def low_kernel(
    part_ref,
    beside_ref,
    across_ref,
    dmid_ref,
    first_ref,
    inverse_ref,
    gain_ref,
    shift_ref,
    small_ref,
    near_sum_ref,
    far_sum_ref,
    mix0_hbm,
    mix1_hbm,
    mix2_hbm,
    mix3_hbm,
    dlow_ref,
    dcontext0_ref,
    dcontext1_ref,
    dcontext23_ref,
    dlow_low_ref,
    sums_ref,
    mix_ref,
    sems,
):
    columns = dcontext0_ref.shape[1]
    loads = []
    for k, mix in enumerate((mix0_hbm, mix1_hbm, mix2_hbm, mix3_hbm)):
        loads.append(
            pltpu.make_async_copy(mix.at[pl.ds(0, columns)], mix_ref.at[k], sems.at[k])
        )
    for load in loads:
        load.start()
    dfirst = (
        part_ref[...].astype(F32)
        + beside_ref[...].astype(F32)
        + across_ref[...].astype(F32)
        + dmid_ref[...]
    )
    unit = (first_ref[...] - shift_ref[0:1, :]) / gain_ref[0:1, :]
    dlow, gain, shift = normalize_back(dfirst, unit, inverse_ref[...], gain_ref[0:1, :])
    dlow_ref[...] = dlow
    dlow_low = dlow.astype(BF16)
    dlow_low_ref[...] = dlow_low
    for load in loads:
        load.wait()
    dcontext0_ref[...] = dot_nt(dlow_low, mix_ref[0]).astype(BF16)
    dcontext1_ref[...] = dot_nt(dlow_low, mix_ref[1]).astype(BF16)
    dcontext23_ref[0] = dot_nt(dlow_low, mix_ref[2]).astype(BF16)
    dcontext23_ref[1] = dot_nt(dlow_low, mix_ref[3]).astype(BF16)
    sums_ref[0:6, :] = small_ref[0:6, :]
    sums_ref[6:7, :] = gain[None, :]
    sums_ref[7:8, :] = shift[None, :]
    sums_ref[8:16, :] = near_sum_ref[...] + far_sum_ref[...]


def low(
    part,
    near,
    far,
    dmid,
    first,
    inverse,
    gains,
    shifts,
    mixes,
    small,
    near_sum,
    far_sum,
):
    block, width = dmid.shape
    columns = width // 4
    rows = fixed((block, width), 0, 0)
    in_specs = [rows] * 5
    in_specs += [fixed(array.shape, 0, 0) for array in (inverse, gains, shifts)]
    in_specs += [fixed(small.shape, 0, 0)] + [fixed(near_sum.shape, 0, 0)] * 2
    in_specs += whole_hbm(4)
    out_shape = [
        jax.ShapeDtypeStruct((block, width), F32),
        jax.ShapeDtypeStruct((block, columns), BF16),
        jax.ShapeDtypeStruct((block, columns), BF16),
        jax.ShapeDtypeStruct((2, block, columns), BF16),
        jax.ShapeDtypeStruct((block, width), BF16),
        jax.ShapeDtypeStruct((16, width), F32),
    ]
    return pl.pallas_call(
        low_kernel,
        grid=(1,),
        in_specs=in_specs,
        out_specs=[fixed(out.shape, *([0] * len(out.shape))) for out in out_shape],
        out_shape=out_shape,
        scratch_shapes=[
            VMEM((4, columns, width), BF16),
            pltpu.SemaphoreType.DMA((4,)),
        ],
        compiler_params=params(60),
        cost_estimate=pl.CostEstimate(flops=600000000, bytes_accessed=6000000, transcendentals=0),
        name="low",
    )(
        part,
        near,
        far,
        dmid,
        first,
        inverse,
        gains,
        shifts,
        small,
        near_sum,
        far_sum,
        *mixes,
    )


def low_grads_kernel(
    dlow_ref, context0_ref, context1_ref, context2_ref, context3_ref, grad02_ref, grad13_ref
):
    columns = context0_ref.shape[1]
    dlow = dlow_ref[...]
    grad02_ref[0:columns, :] = dot_tn(context0_ref[...], dlow).astype(BF16)
    grad02_ref[columns:, :] = dot_tn(context2_ref[...], dlow).astype(BF16)
    grad13_ref[0:columns, :] = dot_tn(context1_ref[...], dlow).astype(BF16)
    grad13_ref[columns:, :] = dot_tn(context3_ref[...], dlow).astype(BF16)


def low_grads(dlow, contexts):
    block, width = dlow.shape
    columns = contexts[0].shape[1]
    grads = jax.ShapeDtypeStruct((2 * columns, width), BF16)
    return pl.pallas_call(
        low_grads_kernel,
        grid=(1,),
        in_specs=[fixed((block, width), 0, 0)] + [fixed((block, columns), k, 0) for k in range(4)],
        out_specs=[fixed(grads.shape, 0, 0)] * 2,
        out_shape=[grads] * 2,
        compiler_params=params(60),
        cost_estimate=pl.CostEstimate(flops=300000000, bytes_accessed=2000000, transcendentals=0),
        name="low_grads",
    )(dlow, *contexts)


def merge_kernel(
    scalar_ref,
    first_ref,
    fed_ref,
    fed_beside_ref,
    fed_across_ref,
    bias_ref,
    gain_ref,
    shift_ref,
    cotangent_hbm,
    mix0_hbm,
    mix1_hbm,
    mix2_hbm,
    mix3_hbm,
    merging_hbm,
    output_ref,
    dmid_ref,
    dmid_low_ref,
    kept_ref,
    sent_ref,
    small_ref,
    down_ref,
    up_ref,
    mask_ref,
    merging_ref,
    cotangent_ref,
    sems,
):
    rows, width = first_ref.shape
    me = scalar_ref[0]
    length = scalar_ref[1]
    part = (mix0_hbm.shape[0] - MASK_ROWS) // 3
    columns = 4 * part
    copies = []
    for k, mix in enumerate((mix0_hbm, mix1_hbm, mix2_hbm, mix3_hbm)):
        place = pl.ds(k * part, part)
        copies.append(
            (
                pltpu.make_async_copy(mix.at[pl.ds(part, part)], down_ref.at[place], sems.at[k]),
                pltpu.make_async_copy(
                    mix.at[pl.ds(2 * part, part)], up_ref.at[place], sems.at[4 + k]
                ),
                pltpu.make_async_copy(
                    mix.at[pl.ds(3 * part, MASK_ROWS)], mask_ref.at[k], sems.at[8 + k]
                ),
            )
        )
    merging_copy = pltpu.make_async_copy(merging_hbm, merging_ref, sems.at[12])
    cotangent_copy = pltpu.make_async_copy(
        cotangent_hbm.at[pl.ds(pl.multiple_of(me * rows, rows), rows)], cotangent_ref, sems.at[13]
    )
    for group in copies:
        group[0].start()
    merging_copy.start()
    for group in copies:
        group[1].start()
        group[2].start()
    cotangent_copy.start()
    adapters = ADAPTERS
    scaling = width ** (-0.5)
    rank = columns // adapters
    held = adapters // 4
    expand = (
        lax.broadcasted_iota(jnp.int32, (adapters, columns), 1) // rank
        == lax.broadcasted_iota(jnp.int32, (adapters, columns), 0)
    ).astype(F32)
    expand = expand.astype(BF16)

    def collect(wide):
        high = wide.astype(BF16)
        rest = (wide - high.astype(F32)).astype(BF16)
        return dot_nt(high, expand) + dot_nt(rest, expand)

    fed = (
        fed_ref[...].astype(F32)
        + fed_beside_ref[...].astype(F32)
        + fed_across_ref[...].astype(F32)
        + bias_ref[...]
    )
    second, unit_second, inverse_second = normalize(
        first_ref[...] + fed, gain_ref[1:2, :], shift_ref[1:2, :]
    )
    second_low = second.astype(BF16)
    for group in copies:
        group[0].wait()
    squeezed, slope = gelu_both(dot_nt(second_low, down_ref[...]))
    squeezed = squeezed.astype(BF16).astype(F32)
    merging_copy.wait()
    fquery = dot(second_low, merging_ref[0]).astype(BF16)
    asked = dot_nt(fquery, merging_ref[1])
    for group in copies:
        group[1].wait()
        group[2].wait()
    cotangent_copy.wait()
    asked_up = dot_nt(asked.astype(BF16), up_ref[...])
    scores = scaling * (
        jnp.sum(asked * second, -1, keepdims=True) + collect(squeezed * asked_up)
    )
    lane = lax.broadcasted_iota(jnp.int32, (1, adapters), 1)
    usable = jnp.zeros((1, adapters), F32)
    for k in range(4):
        usable = jnp.where(lane // held == k, mask_ref[k, 0:1, 0:adapters].astype(F32), usable)
    usable = usable > 0.5
    scores = jnp.where(usable, scores, NEGATIVE)
    highest = jnp.max(scores, -1, keepdims=True)
    weights = jnp.where(usable, jnp.exp(scores - highest), 0.0)
    probs = weights / jnp.sum(weights, -1, keepdims=True)
    total = jnp.sum(probs, -1, keepdims=True)
    probs_wide = split_dot(probs, expand)
    mixed = total * second + dot((probs_wide * squeezed).astype(BF16), up_ref[...])
    mixed_low = mixed.astype(BF16)
    blended = dot(mixed_low, merging_ref[2])
    final, unit_third, inverse_third = normalize(
        second + blended, gain_ref[2:3, :], shift_ref[2:3, :]
    )
    output_ref[...] = final.astype(BF16)
    dthird, gain_third, shift_third = normalize_back(
        cotangent_ref[...].astype(F32), unit_third, inverse_third, gain_ref[2:3, :]
    )
    dthird_low = dthird.astype(BF16)
    pulled = dot_nt(dthird_low, merging_ref[2])
    pulled_up = dot_nt(pulled.astype(BF16), up_ref[...])
    dprobs = jnp.sum(pulled * second, -1, keepdims=True) + collect(squeezed * pulled_up)
    dscores = probs * (dprobs - jnp.sum(probs * dprobs, -1, keepdims=True)) * scaling
    dscores_total = jnp.sum(dscores, -1, keepdims=True)
    dscores_wide = split_dot(dscores, expand)
    weighed = dscores_total * second + dot((dscores_wide * squeezed).astype(BF16), up_ref[...])
    weighed_low = weighed.astype(BF16)
    dquery = dot(weighed_low, merging_ref[1]).astype(BF16)
    dbottle = ((dscores_wide * asked_up + probs_wide * pulled_up) * slope).astype(BF16)
    dsecond = (
        dthird
        + dscores_total * asked
        + total * pulled
        + dot(dbottle, down_ref[...])
        + dot_nt(dquery, merging_ref[0])
    )
    dmid, gain_second, shift_second = normalize_back(
        dsecond, unit_second, inverse_second, gain_ref[1:2, :]
    )
    dmid_ref[...] = dmid
    dmid_low_ref[...] = dmid.astype(BF16)
    position = me * rows + lax.broadcasted_iota(jnp.int32, (rows, 1), 0)
    mass = jnp.sum(jnp.where(position < length, probs, 0.0), 0, keepdims=True)
    source = lax.broadcasted_iota(jnp.int32, (adapters, width), 0)
    target = lax.broadcasted_iota(jnp.int32, (adapters, width), 1)
    move = ((source // held) ^ me) * held + source % held == target
    mass = lax.dot_general(
        jnp.broadcast_to(mass, (8, adapters)),
        move.astype(F32),
        (((1,), (0,)), ((), ())),
        precision=lax.Precision.HIGHEST,
        preferred_element_type=F32,
    )[0:1, :]
    counted = lax.broadcasted_iota(jnp.int32, (1, width), 1) == adapters
    small_ref[0:1, :] = gain_second[None, :]
    small_ref[1:2, :] = gain_third[None, :]
    small_ref[2:3, :] = shift_second[None, :]
    small_ref[3:4, :] = shift_third[None, :]
    small_ref[4:5, :] = jnp.sum(dmid, 0, keepdims=True)
    small_ref[5:6, :] = jnp.where(counted, 0.25 * length.astype(F32), mass)
    small_ref[6:8, :] = jnp.zeros((2, width), F32)
    core = me & 1
    quarter = width // 4
    for j, (left, right) in enumerate(
        ((second_low, dquery), (weighed_low, fquery), (mixed_low, dthird_low))
    ):
        grad = dot_tn(left, right).astype(BF16)
        for k in range(4):
            piece = 4 * j + k
            owner, place = piece // 3 % 2, piece // 6 * 3 + piece % 3
            value = grad[k * quarter : (k + 1) * quarter, :]

            @pl.when(core == owner)
            def _():
                kept_ref[place * quarter : (place + 1) * quarter, :] = value

            @pl.when(core != owner)
            def _():
                sent_ref[place * quarter : (place + 1) * quarter, :] = value


def merge(scalars, first, fed, near, far, bias, gains, shifts, cotangent, mixes, merging):
    rows, width = first.shape
    part = (mixes[0].shape[0] - MASK_ROWS) // 3
    grads = jax.ShapeDtypeStruct((3 * width // 2, width), BF16)
    out_shape = [
        jax.ShapeDtypeStruct((rows, width), BF16),
        jax.ShapeDtypeStruct((rows, width), F32),
        jax.ShapeDtypeStruct((rows, width), BF16),
        grads,
        grads,
        jax.ShapeDtypeStruct((8, width), F32),
    ]
    return pl.pallas_call(
        merge_kernel,
        grid=(1,),
        in_specs=[pl.BlockSpec(memory_space=pltpu.SMEM)]
        + [fixed(array.shape, 0, 0) for array in (first, fed, near, far, bias, gains, shifts)]
        + whole_hbm(6),
        out_specs=[fixed(array.shape, 0, 0) for array in out_shape],
        out_shape=out_shape,
        scratch_shapes=[
            VMEM((4 * part, width), BF16),
            VMEM((4 * part, width), BF16),
            VMEM((4, MASK_ROWS, width), BF16),
            VMEM(merging.shape, BF16),
            VMEM((rows, width), BF16),
            pltpu.SemaphoreType.DMA((14,)),
        ],
        compiler_params=params(),
        cost_estimate=pl.CostEstimate(flops=6000000000, bytes_accessed=14000000, transcendentals=0),
        name="merge",
    )(scalars, first, fed, near, far, bias, gains, shifts, cotangent, *mixes, merging)


def on_device(
    tokens,
    cotangent,
    attn_qkv,
    attn_out,
    ffn_in,
    ffn_bias_in,
    ffn_out,
    ffn_bias_out,
    norm_gains,
    norm_shifts,
    adapter_down,
    adapter_up,
    merging_proj,
    adapter_mask,
    lengths,
):
    me = lax.axis_index("ad")
    tok = lax.axis_size("tok")
    over_tok = tok_plan(tok)
    row_count, width = tokens.shape
    block = row_count // 4
    scalars = jnp.stack([me.astype(jnp.int32), lengths[0]])
    attn_qkv = attn_qkv.swapaxes(1, 2)

    mask = jnp.tile(adapter_mask.astype(BF16), (MASK_ROWS, width // adapter_mask.shape[1]))
    mix = jnp.concatenate([attn_out, adapter_down.T, adapter_up.reshape(-1, width), mask], 0)
    mix_far = across(mix)

    context, weights, inverses, query, key, value, tokens = attend(scalars, tokens, attn_qkv)
    contexts = gather_xor(context)
    mix_far = after(mix_far, context)
    mixes = [mix, beside(mix), mix_far, beside(mix_far)]
    shared_weights = (mixes, ffn_in, ffn_bias_in[None, :], ffn_out, norm_gains, norm_shifts)
    far_first, far_inner, far_slope, fed2, fed3 = feed(1, tokens, contexts, *shared_weights)
    fed_sum = add_low(fed2, beside(fed3))
    contexts[0] = after(context, fed_sum)
    near_first, near_inner, near_slope, fed0, fed1, first, inverse = feed(
        0, tokens, contexts, *shared_weights
    )
    fed1 = beside(fed1)
    fed_far, fed0 = lax.optimization_barrier((across(fed_sum), fed0))
    output_block, dmid, dmid_low, kept, sent, small = merge(
        scalars,
        first,
        fed0,
        fed1,
        fed_far,
        ffn_bias_out[None, :],
        norm_gains,
        norm_shifts,
        cotangent,
        mixes,
        merging_proj,
    )

    dmids = [dmid_low, beside(dmid_low), across(dmid_low)]
    received = beside(sent)
    near_dinner, part0, part1, near_sum = feed_back(
        dmids[0], dmids[1], near_slope, ffn_out, ffn_in
    )
    merging = add_low(after(kept, part0), received)
    bits = len(over_tok)
    merging = merging.reshape((2,) * (bits + 1) + (-1, width))
    places = [(over_tok[k], bits - k) for k in range(bits)]
    down_y = [(("ad", 4, 1), 0)]
    swapped = [(over_tok[1], bits - 1), (over_tok[0], bits - 1)]
    merging = [
        Chain(merging[..., : width // 2], places[:2]),
        Chain(merging[..., width // 2 :], swapped),
    ]
    dmids[2] = after(dmids[2], part0, *[chain.prepare() for chain in merging])
    dmids.append(beside(dmids[2]))
    far_dinner, part2, part3, far_sum = feed_back(dmids[2], dmids[3], far_slope, ffn_out, ffn_in)
    part_beside = beside(part1)
    part_sum = add_low(part2, beside(part3))
    part_far = across(part_sum)
    for chain in merging:
        chain.parts = (chain.parts[0], after(chain.parts[1], part_sum))
    grad_out, grad_in = feed_grads(
        (after(near_inner, part_sum), far_inner),
        (near_first, far_first),
        dmids,
        near_dinner,
        far_dinner,
    )
    grad_out = tok_chain(grad_out, over_tok)
    grad_in = tok_chain(grad_in, over_tok)
    part_far, part_beside, grad_out.array, grad_in.parts = advance(
        merging, part_far, part_beside, grad_out.array, grad_in.prepare()
    )
    part_far = after(part_far, grad_in.parts)

    dlow, dcontext0, dcontext1, dcontext23, dlow_low, sums = low(
        part0,
        part_beside,
        part_far,
        dmid,
        first,
        inverse,
        norm_gains,
        norm_shifts,
        mixes,
        small,
        near_sum,
        far_sum,
    )
    dcontext_far = across(dcontext23)
    grad02, grad13 = low_grads(dlow_low, contexts)
    dcontext_far = after(dcontext_far, grad13)
    pair = beside(jnp.stack([dcontext1, dcontext_far[1]]))
    dcontext = jnp.concatenate([dcontext0, pair[0], dcontext_far[0], pair[1]], 0)
    grad02 = add_low(grad02, beside(grad13))
    columns = context.shape[1]
    dcontext, grad02, grad_out.array = advance(
        merging + [grad_in], dcontext, grad02, grad_out.array
    )
    merging = Chain(
        jnp.concatenate([chain.array for chain in merging], -1), places[2:] + down_y
    )

    grad_attn_far = across(grad02[columns:])
    late, dtokens0, dtokens2, dtokens13 = attend_back(
        query,
        key,
        value,
        weights,
        context,
        inverses,
        dcontext,
        tokens,
        attn_qkv,
    )
    shared = sums[:8]
    late, grad_attn_far, received = advance(
        [merging, grad_in, grad_out], late, grad_attn_far, beside(shared)
    )
    shared = shared + received
    late = jnp.concatenate([late, add_low(grad02[:columns], grad_attn_far)], 0)
    late = tok_chain(late, over_tok)
    chains = [late, grad_out, grad_in]
    (received,) = advance([merging] + chains, beside(dtokens13))
    dtokens = dtokens0.astype(F32) + received[0].astype(F32) + dlow
    dtokens_far = across(add_low(dtokens2, received[1]))
    while merging.steps:
        advance([merging])
    merging = lax.all_gather(merging.array, ("ad", "tok"), axis=0)
    received, dtokens_far = advance(chains, across(shared), dtokens_far)
    sums = jnp.concatenate([shared + received, sums[8:]], 0)
    dtokens = (dtokens + dtokens_far.astype(F32)).astype(BF16)

    def sum_step(k):
        axis, size, bit = over_tok[k]
        return swap(sums, axis, size, 1 << bit)

    received, dtokens_far = advance(chains, sum_step(0), across(dtokens))
    sums = sums + received
    pair = beside(jnp.concatenate([dtokens, dtokens_far], 0))
    received, pair, output_far = advance(chains, sum_step(1), pair, across(output_block))
    sums = sums + received
    grad_tokens = place_xor([dtokens, pair[:block], dtokens_far, pair[block:]], me, F32)
    pair = beside(jnp.concatenate([output_block, output_far], 0))
    received, pair = advance(chains, sum_step(2), pair)
    sums = sums + received
    output = place_xor([output_block, pair[:block], output_far, pair[block:]], me, BF16)
    for k in range(3, bits):
        (received,) = advance(chains, sum_step(k))
        sums = sums + received
    while len(late.steps) > 1:
        advance(chains)
    merging = merging.reshape(3, width, width).astype(F32)
    output, merging = advance(chains, output, merging)
    late, grad_out, grad_in = [
        chain.array.reshape(-1, width) for chain in (late, grad_out, grad_in)
    ]

    held = ADAPTERS // 4
    usage = lax.dynamic_slice_in_dim(sums[5], me * held, held) / sums[5, ADAPTERS]
    return (
        output,
        grad_tokens,
        late[: 3 * columns].reshape(3, columns, width).swapaxes(1, 2).astype(F32),
        late[3 * columns :].astype(F32),
        grad_in.astype(F32),
        sums[8],
        grad_out.astype(F32),
        sums[4],
        jnp.stack([sums[6], sums[0], sums[1]]),
        jnp.stack([sums[7], sums[2], sums[3]]),
        merging,
        usage,
    )


def solution(mesh):
    placed = (
        P("tok", None),
        P("tok", None),
        P(None, None, "ad"),
        P("ad", None),
        P(None, "ad"),
        P("ad"),
        P("ad", None),
        P(),
        P(),
        P(),
        P(None, "ad"),
        P("ad", None, None),
        P(),
        P("tok", "ad"),
        P("tok"),
    )
    return jax.shard_map(
        on_device,
        mesh=mesh,
        in_specs=placed,
        out_specs=(
            P("tok", None),
            P("tok", None),
            P(None, None, "ad"),
            P("ad", None),
            P(None, "ad"),
            P("ad"),
            P("ad", None),
            P(),
            P(),
            P(),
            P(),
            P("ad"),
        ),
        check_vma=False,
    )
```
